32 devices in a mesh: face: 4 (over x, core), tile: 8 (over z, y).
Axes of the slice: x: 2, y: 2, z: 4, core: 2. Of those that a mesh axis runs over, the one named last changes fastest.
Arguments:
- atmos: bfloat16 [64, 192, 2048], P(None, 'tile', 'face'), may hold values from -6 to 6
- ocean: bfloat16 [64, 65536], P(None, ('face', 'tile')), may hold values from -6 to 6
- surface_heat_weight: float32 [64], replicated, may hold values from -4 to 4
- air_conv_first_weight: bfloat16 [3, 3, 64, 64], replicated, may hold values from -0.25 to 0.25
- air_conv_second_weight: bfloat16 [3, 3, 64, 64], replicated, may hold values from -0.25 to 0.25
- marine_conv_first_weight: bfloat16 [9, 64, 64], replicated, may hold values from -0.25 to 0.25
- marine_conv_second_weight: bfloat16 [9, 64, 64], replicated, may hold values from -0.25 to 0.25
- marine_coupling_slot: int32 [65536], P(('face', 'tile')), may hold values from 0 to 4095, as said below
- coupling_air_cells: int32 [32, 4096], P(('face', 'tile')), may hold values from 0 to 12287
- marine_neighbour_index: int32 [9, 65536], P(None, ('face', 'tile')), may hold values from 0 to 2559, as said below
Outputs:
- atmos_next: bfloat16 [64, 192, 2048], P(None, 'tile', 'face')
- ocean_next: bfloat16 [64, 65536], P(None, ('face', 'tile'))
The draws below stay inside these ranges and needn't reach their ends.
Inputs may be any that keep to these rules, and one draw needn't show every extreme that they name: `marine_coupling_slot`: within one ocean device's 2048 entries the values are distinct; value // 128 is the atmosphere device serving the cell, so no atmosphere device serves more than 128 cells of one ocean device, and on every ocean device some atmosphere device serves exactly 128. `marine_neighbour_index`: entry [k, g] lies within 256 of the cell's own position 256 + g % 2048; every device's entries reach both ends.
All inputs are finite; a program needn't handle non-finite values.
Results may differ from the reference program's by a relative error of at most 0.0064.
Values may be sent and summed in bfloat16 or wider, within the bound.
No kernel may reach another device: no remote copies, remote signals or barrier semaphores. Data moves between devices by JAX's collectives and lax.ppermute only.
A program may use at most 128 MiB of HBM per device.

```python
import jax
import jax.numpy as jnp
from jax import lax

LEVEL_CHANNELS = 64
AR = 24
ACOL = 512
OCN = 2048
HALO = 256
K = 9
CAP = 128
GRID_ROWS = 192
GRID_COLUMNS = 2048
OCELLS = 65536
N_TILE = 8
DEVICES = 32


def draw_marine_coupling_slot(key, part):
    key = jax.random.fold_in(key, 11)
    device_count = OCELLS // OCN
    slot_space = 2 * OCN

    def one_block(block_key):
        first_key, second_key, third_key = jax.random.split(block_key, 3)
        order_scores = jax.random.permutation(first_key, slot_space).astype(jnp.int32)
        favoured = jax.random.randint(second_key, (), 0, device_count)
        slots = jnp.arange(slot_space, dtype=jnp.int32)
        scores = order_scores + jnp.where(slots // CAP == favoured, 0, slot_space)
        scores = jnp.where(slots == 0, -2, scores)
        scores = jnp.where(slots == slot_space - 1, -1, scores)
        chosen = jnp.argsort(scores, stable=True)[:OCN].astype(jnp.int32)
        shuffle = jax.random.permutation(third_key, OCN)
        return chosen[shuffle].astype(jnp.int32)
    block_keys = jax.random.split(key, device_count)
    return jax.vmap(one_block)(block_keys).reshape(-1).astype(jnp.int32)


def draw_marine_neighbour_index(key, part):
    key = jax.random.fold_in(key, 23)
    offsets = jax.random.randint(key, (K, OCELLS), -HALO, HALO + 1).astype(jnp.int32)
    within = (jnp.arange(OCELLS, dtype=jnp.int32) % OCN)[None, :]
    taps = jnp.arange(K, dtype=jnp.int32)[:, None]
    offsets = jnp.where((within == 0) & (taps == 0), -HALO, offsets)
    offsets = jnp.where((within == OCN - 1) & (taps == K - 1), HALO, offsets)
    return (HALO + within + offsets).astype(jnp.int32)


def plant(drawn, own_key, smallest, largest):
    longest = drawn.shape.index(max(drawn.shape))
    spots = []
    for shift in (0, 1):
        where = [jax.random.randint(jax.random.fold_in(own_key, axis), (), 0, length) for axis, length in enumerate(drawn.shape)]
        where[longest] = (where[longest] + shift) % drawn.shape[longest]
        spots.append(tuple(where))
    return drawn.at[spots[0]].set(smallest).at[spots[1]].set(largest)


def levels(rng, shape, cuts, smallest, top_value):
    factor_of = 1.0
    for dim, shards_of in cuts:
        heights = jax.random.uniform(jax.random.fold_in(jax.random.fold_in(rng, 6), dim), (shards_of,), jnp.float32, smallest / len(cuts), top_value / len(cuts))
        factor_of = factor_of * jnp.repeat(jnp.exp(heights), shape[dim] // shards_of).reshape((-1,) + (1,) * (len(shape) - 1 - dim))
    return factor_of


def noise(stream_key, dims, spread, reach, cuts=(), kind=jnp.bfloat16):
    loudness = levels(stream_key, dims, cuts, -0.22, 0.18) if cuts else 1.0
    drawn = jax.random.normal(stream_key, dims, jnp.float32) * spread * loudness
    return jnp.minimum(jnp.maximum(drawn, -reach), reach).astype(kind)


def setup_inputs(seed: int = 0) -> dict:
    splits = jax.random.split(jax.random.key(seed), 11)
    atmos = noise(splits[0], (LEVEL_CHANNELS, GRID_ROWS, GRID_COLUMNS), 1.0, 6.0, ((1, 8), (2, 4)))
    ocean = noise(splits[1], (LEVEL_CHANNELS, OCELLS), 1.0, 6.0, ((1, 32),))
    surface_heat_weight = noise(splits[2], (LEVEL_CHANNELS,), 1.0, 4.0, (), jnp.float32)
    air_conv_first_weight = noise(splits[3], (3, 3, LEVEL_CHANNELS, LEVEL_CHANNELS), (9 * LEVEL_CHANNELS) ** -0.5, 0.25)
    air_conv_second_weight = noise(splits[4], (3, 3, LEVEL_CHANNELS, LEVEL_CHANNELS), (9 * LEVEL_CHANNELS) ** -0.5, 0.25)
    marine_conv_first_weight = noise(splits[5], (K, LEVEL_CHANNELS, LEVEL_CHANNELS), (K * LEVEL_CHANNELS) ** -0.5, 0.25)
    marine_conv_second_weight = noise(splits[6], (K, LEVEL_CHANNELS, LEVEL_CHANNELS), (K * LEVEL_CHANNELS) ** -0.5, 0.25)
    marine_coupling_slot = draw_marine_coupling_slot(jax.random.fold_in(splits[10], 71), 0)
    coupling_air_cells = plant(jax.random.randint(splits[8], (DEVICES, DEVICES * CAP), 0, AR * ACOL), jax.random.fold_in(splits[8], 1), 0, (AR * ACOL) - 1).astype(jnp.int32)
    marine_neighbour_index = draw_marine_neighbour_index(jax.random.fold_in(splits[10], 71), 0)
    return {"atmos": atmos, "ocean": ocean, "surface_heat_weight": surface_heat_weight, "air_conv_first_weight": air_conv_first_weight, "air_conv_second_weight": air_conv_second_weight, "marine_conv_first_weight": marine_conv_first_weight, "marine_conv_second_weight": marine_conv_second_weight, "marine_coupling_slot": marine_coupling_slot, "coupling_air_cells": coupling_air_cells, "marine_neighbour_index": marine_neighbour_index}


def atmosphere_conv(values, weight):
    padded = jnp.pad(values, ((0, 0), (1, 1), (0, 0)))
    padded = jnp.concatenate([padded[:, :, -1:], padded, padded[:, :, :1]], axis=2)
    channels, row_total, column_total = values.shape
    summed = jnp.zeros((channels, row_total * column_total), jnp.float32)
    for row_tap in range(3):
        for col_tap in range(3):
            window = padded[:, row_tap:row_tap + row_total, col_tap:col_tap + column_total].reshape(channels, -1)
            summed = summed + jnp.dot(weight[row_tap, col_tap], window, preferred_element_type=jnp.float32)
    return summed.reshape(channels, row_total, column_total)


def ocean_layer(values, weight, neighbours):
    padded = jnp.pad(values, ((0, 0), (HALO, HALO)))
    device_count = OCELLS // OCN

    def one_device(device):
        window = lax.dynamic_slice_in_dim(padded, device * OCN, OCN + 2 * HALO, 1)
        taps_here = lax.dynamic_slice_in_dim(neighbours, device * OCN, OCN, 1)
        summed = jnp.zeros((values.shape[0], OCN), jnp.float32)
        for tap in range(K):
            summed = summed + jnp.dot(weight[tap], jnp.take(window, taps_here[tap], axis=1), preferred_element_type=jnp.float32)
        return summed

    blocks = lax.map(one_device, jnp.arange(device_count, dtype=jnp.int32))
    return jnp.transpose(blocks, (1, 0, 2)).reshape(values.shape[0], OCELLS)


def reference(atmos, ocean, surface_heat_weight, air_conv_first_weight, air_conv_second_weight, marine_conv_first_weight, marine_conv_second_weight, marine_coupling_slot, coupling_air_cells, marine_neighbour_index):
    device = jnp.arange(OCELLS, dtype=jnp.int32) // OCN
    source = marine_coupling_slot // CAP
    position = marine_coupling_slot % CAP
    local_cell = coupling_air_cells[source, device * CAP + position]
    face_index = source // N_TILE
    tile_index = source % N_TILE
    row_index = tile_index * AR + local_cell // ACOL
    col_index = face_index * ACOL + local_cell % ACOL
    flat_cell = row_index * GRID_COLUMNS + col_index
    overall_sums = jnp.zeros((GRID_ROWS * GRID_COLUMNS,), jnp.float32).at[flat_cell].add(ocean[0].astype(jnp.float32))
    running_counts = jnp.zeros((GRID_ROWS * GRID_COLUMNS,), jnp.float32).at[flat_cell].add(jnp.ones((OCELLS,), jnp.float32))
    surface_heat_field = (overall_sums / jnp.maximum(running_counts, 1.0)).reshape(GRID_ROWS, GRID_COLUMNS)
    begin_offset = (atmos.astype(jnp.float32) + surface_heat_weight[:, None, None] * surface_heat_field[None]).astype(jnp.bfloat16)
    hidden = jax.nn.gelu(atmosphere_conv(begin_offset, air_conv_first_weight)).astype(jnp.bfloat16)
    atmos_next = (begin_offset.astype(jnp.float32) + atmosphere_conv(hidden, air_conv_second_weight)).astype(jnp.bfloat16)
    forcing = jnp.take(atmos_next.reshape(atmos.shape[0], -1), flat_cell, axis=1)
    ocean_start = (ocean.astype(jnp.float32) + forcing.astype(jnp.float32)).astype(jnp.bfloat16)
    ocean_hidden = jax.nn.gelu(ocean_layer(ocean_start, marine_conv_first_weight, marine_neighbour_index)).astype(jnp.bfloat16)
    ocean_next = (ocean_start.astype(jnp.float32) + ocean_layer(ocean_hidden, marine_conv_second_weight, marine_neighbour_index)).astype(jnp.bfloat16)
    return atmos_next, ocean_next
```

```python
import jax
import jax.numpy as jnp
import numpy as np
from jax import lax
from jax.experimental import pallas as pl
from jax.experimental.pallas import tpu as pltpu
from jax.sharding import PartitionSpec as P

HALO = 256
LANES = 128
BF = jnp.bfloat16
F32 = jnp.float32
NEIGHBOURS = ((0, 0), (-1, 0), (1, 0), (0, -1), (0, 1), (-1, -1), (1, -1), (-1, 1), (1, 1))
VMEM_LIMIT = 20 * 1024 * 1024
VMEM_WHOLE = 60 * 1024 * 1024

VMEM = pl.BlockSpec(memory_space=pltpu.VMEM)
ANY = pl.BlockSpec(memory_space=pl.ANY)
HBM = pl.BlockSpec(memory_space=pltpu.HBM)


def call(body, outs, ins, scratch=(), parts=None, untouched=(), out_specs=None, limit=VMEM_LIMIT):
    parts = parts or {}
    held = [i for i in range(len(ins)) if i not in untouched]
    shapes = [
        tuple(len(range(*cut.indices(n))) for cut, n in zip(parts[i], ins[i].shape))
        if i in parts
        else ins[i].shape
        for i in held
    ]
    count = len(jax.tree.leaves(outs))

    def kernel(*refs):
        sources, refs = refs[: len(ins)], refs[len(ins) :]
        results, refs = refs[:count], refs[count:]
        copies, refs, done = refs[: len(held)], refs[len(held) : -1], refs[-1]
        moves = {}
        for k, i in enumerate(held):
            source = sources[i].at[parts[i]] if i in parts else sources[i]
            moves[i] = pltpu.make_async_copy(source, copies[k], done.at[k])
            moves[i].start()
        waiting = set(held)

        def wait(*which):
            for i in which:
                waiting.remove(i)
                moves[i].wait()

        body(wait, *copies, *results, *refs)
        assert not waiting

    return pl.pallas_call(
        kernel,
        out_shape=outs,
        in_specs=[ANY] * len(ins),
        out_specs=out_specs or jax.tree.map(lambda _: VMEM, outs),
        scratch_shapes=[pltpu.VMEM(shape, ins[i].dtype) for shape, i in zip(shapes, held)]
        + list(scratch)
        + [pltpu.SemaphoreType.DMA((len(held),))],
        compiler_params=pltpu.CompilerParams(vmem_limit_bytes=limit),
    )(*ins)


def one_hot(index_row, size):
    places = lax.broadcasted_iota(jnp.int32, (size, index_row.shape[1]), 0)
    return jnp.where(places == index_row, 1.0, 0.0).astype(BF)


def nt_dot(a, b):
    return lax.dot_general(a, b, (((1,), (1,)), ((), ())), preferred_element_type=F32)


def gelu(x):
    inner = x * (0.7978845608028654 + 0.035677408136300125 * (x * x))
    return (0.5 * x) * (1.0 + jnp.tanh(inner))


def slot_values(heat_ref, slot_ref, rows):
    heat = heat_ref[...].astype(F32)[0:1]
    slot = slot_ref[...]
    places = lax.broadcasted_iota(jnp.int32, (rows, slot.shape[1]), 0)
    match = places == (slot >> 7)
    left = jnp.concatenate([jnp.where(match, heat, 0.0), jnp.where(match, 1.0, 0.0)], axis=0)
    return nt_dot(left.astype(BF), one_hot(slot & 127, LANES))


def or_inf(value, live):
    return jnp.where(live > 0.5, value, jnp.inf).astype(BF)


def slot_table_body(wait, heat_ref, slot_ref, out_ref):
    wait(0, 1)
    rows = out_ref.shape[0]
    table = slot_values(heat_ref, slot_ref, rows)
    out_ref[...] = or_inf(table[:rows], table[rows:])


def spread_table_body(wait, heat_ref, slot_ref, spread_ref, out_ref):
    wait(0, 1)
    count, rows = spread_ref.shape
    table = slot_values(heat_ref, slot_ref, rows)
    pair = jnp.concatenate([table[:rows], table[rows:]], axis=1).astype(BF)
    wait(2)
    spread = jnp.dot(spread_ref[...], pair, preferred_element_type=F32)
    out_ref[...] = or_inf(spread[:, :LANES], spread[:, LANES:]).reshape(out_ref.shape)


def neighbourhoods(faces, tiles):
    around = np.full((faces * tiles, 16), -1)
    for f in range(faces):
        for t in range(tiles):
            for n, (dr, dc) in enumerate(NEIGHBOURS):
                if 0 <= t + dr < tiles:
                    around[f * tiles + t, n] = (f + dc) % faces * tiles + t + dr
    return around


def heat_table(ocean, slots, capacity, faces, tiles):
    devices = faces * tiles
    around = neighbourhoods(faces, tiles)
    ins = [ocean, slots.reshape(1, -1)]
    if capacity == LANES:
        spread = (around.reshape(-1, 1) == np.arange(devices)).astype(np.float32)
        return call(
            spread_table_body,
            jax.ShapeDtypeStruct((devices, 16, LANES), BF),
            ins + [jnp.asarray(spread, BF)],
            parts={0: (slice(0, 16), slice(None))},
            limit=VMEM_WHOLE,
        )
    rows = devices * capacity // LANES
    out = jax.ShapeDtypeStruct((rows, LANES), BF)
    table = call(slot_table_body, out, ins, parts={0: (slice(0, 16), slice(None))})
    table = table.reshape(devices, capacity)
    return jnp.where((around >= 0)[:, :, None], table[np.maximum(around, 0)], jnp.inf).astype(BF)


def heat_slots(table, both):
    capacity = table.shape[2]
    got = lax.all_to_all(table, both, split_axis=0, concat_axis=0, tiled=True)
    if capacity != LANES:
        got = jnp.transpose(got, (1, 0, 2)).reshape(16, -1, LANES)
        got = jnp.transpose(got, (1, 0, 2))
    return got


def live_entry(value, cell, cols, rows, dr):
    live = value < jnp.inf
    value = jnp.where(live, value, 0.0)
    row, col = cell >> (cols.bit_length() - 1), cell & (cols - 1)
    if dr == -1:
        live = live & (row >= rows - 2)
    if dr == 1:
        live = live & (row < 2)
    return value, live, row + (rows * dr + 2), col


def for_chunks(count, many, body):
    def step(i, carry):
        for part in range(many):
            body(i * many + part)
        return carry

    lax.fori_loop(0, count // many, step, 0)


def lanes_at(e, width=LANES):
    return pl.ds(pl.multiple_of(e * width, width), width)


def scatter_body(
    wait, vals_ref, cell_ref, above_ref, below_ref, out_ref, targets, left, right, prod, prod_ends
):
    rows, cols = out_ref.shape[0] - 8, out_ref.shape[1]
    blocks = cols // LANES
    span = rows * blocks
    wait(2, 3)
    targets[0] = decoded(above_ref[0:64, cols:])
    targets[1] = decoded(below_ref[0:64, cols:])
    wait(0, 1)

    def chunk(e):
        lanes = lanes_at(e)
        values = vals_ref[e].astype(F32)
        for n, (dr, _) in enumerate(NEIGHBOURS[:3]):
            cell = targets[n - 1, pl.ds(e, 1), :] if n else cell_ref[:, lanes]
            value, live, row, col = live_entry(values[n : n + 1], cell, cols, rows, dr)
            block = col >> 7
            if n == 0:
                high, size, start = block * rows + row - 2, span, 0
            else:
                high, size = 2 * block + row - (0 if dr < 0 else rows + 2), 8
                start = 2 * span + 16 * (n - 1)
            match = lax.broadcasted_iota(jnp.int32, (size, LANES), 0) == jnp.where(live, high, -1)
            left[start : start + 2 * size, lanes] = jnp.concatenate(
                [jnp.where(match, value, 0.0), jnp.where(match, 1.0, 0.0)], axis=0
            ).astype(BF)
            right[n * LANES : (n + 1) * LANES, lanes] = one_hot(col & 127, LANES)

    for_chunks(vals_ref.shape[0], 2, chunk)
    prod[...] = nt_dot(left[0 : 2 * span], right[0:LANES])
    prod_ends[...] = nt_dot(left[2 * span :], right[LANES:])

    def mean(ref, first, count, rows_on, lanes):
        return ref[first : first + count, lanes] / jnp.maximum(
            ref[first + rows_on : first + rows_on + count, lanes], 1.0
        )

    first, second = slice(0, LANES), slice(LANES, 2 * LANES)
    for b in range(blocks):
        to = slice(b * LANES, (b + 1) * LANES)
        out_ref[2 : rows + 2, to] = mean(prod, b * rows, rows, span, first)
        out_ref[0:2, to] = mean(prod_ends, 2 * b, 2, 8, first)
        out_ref[rows + 2 : rows + 4, to] = mean(prod_ends, 16 + 2 * b, 2, 8, second)


def scatter_heat(vals, cells, above, below, rows):
    slots = cells.size
    cols = above.shape[1] - LANES
    span = rows * (cols // LANES)
    return call(
        scatter_body,
        jax.ShapeDtypeStruct((rows + 8, cols), F32),
        [vals, cells, above, below],
        scratch=[
            pltpu.VMEM((2, slots // LANES, LANES), jnp.int32),
            pltpu.VMEM((2 * span + 32, slots), BF),
            pltpu.VMEM((3 * LANES, slots), BF),
            pltpu.VMEM((2 * span, LANES), F32),
            pltpu.VMEM((32, 2 * LANES), F32),
        ],
    )


def scatter_beside(vals_ref, west_ref, east_ref, targets, left, right, rows, cols):
    for ref, places in ((west_ref, (0, 2, 3)), (east_ref, (1, 4, 5))):
        first = ref.shape[0] - 3 * 64
        for part, place in enumerate(places):
            targets[place] = decoded(ref[first + 64 * part : first + 64 * (part + 1)])

    def chunk(e):
        lanes = lanes_at(e)
        values = vals_ref[e].astype(F32)
        place = lax.broadcasted_iota(jnp.int32, (64, LANES), 0)
        halves = [jnp.zeros((64, LANES), F32)] * 2
        heats = []
        for k, (dr, dc) in enumerate(NEIGHBOURS[3:]):
            value, live, row, col = live_entry(
                values[k + 3 : k + 4], targets[k, pl.ds(e, 1), :], cols, rows, dr
            )
            side = 0 if dc < 0 else 1
            col = col if side else col - (cols - 2)
            live = live & ((col < 2) if side else (col >= 0))
            code = jnp.where(live, 2 * row + col, -1)
            halves[side] = jnp.where(place == code, 1.0, halves[side])
            heats += [value, jnp.where(live, 1.0, 0.0)]
        heats.append(jnp.zeros((16 - len(heats), LANES), F32))
        left[:, lanes] = jnp.concatenate(heats, axis=0).astype(BF)
        right[:, lanes] = jnp.concatenate(halves, axis=0).astype(BF)

    for_chunks(vals_ref.shape[0], 2, chunk)
    prod = nt_dot(left[...], right[...])
    lane = lax.broadcasted_iota(jnp.int32, (1, LANES), 1)
    place = lane & 63
    around = jnp.zeros((1, LANES), F32)
    for k, (dr, dc) in enumerate(NEIGHBOURS[3:]):
        first, last = {-1: (0, 4), 0: (4, 2 * rows + 4), 1: (2 * rows + 4, 2 * rows + 8)}[dr]
        here = (place >= first) & (place < last) & ((lane >= 64) == (dc > 0))
        mean = prod[2 * k : 2 * k + 1] / jnp.maximum(prod[2 * k + 1 : 2 * k + 2], 1.0)
        around = jnp.where(here, mean, around)
    return around


def end_columns(field):
    high, cols = field.shape
    row = lax.broadcasted_iota(jnp.int32, (high, LANES), 0)
    lane = lax.broadcasted_iota(jnp.int32, (high, LANES), 1)
    here = row < high - 4
    own = jnp.where(here & (lane == 2 * row), field[:, 0:1], 0.0) + jnp.where(
        here & (lane == 2 * row + 65), field[:, cols - 1 : cols], 0.0
    )
    return jnp.sum(own, axis=0, keepdims=True)


def coded(cells):
    return jnp.concatenate([cells >> 7, cells & 127], axis=0).astype(BF)


def decoded(code):
    half = code.shape[0] // 2
    return (code[:half].astype(F32) * 128.0 + code[half:].astype(F32)).astype(jnp.int32)


def side_body(
    wait, first_ref, last_ref, above_ref, below_ref, cell_ref, west_ref, east_ref
):
    rows, channels, _ = first_ref.shape
    cols = above_ref.shape[1] - LANES
    wait(0, 1, 2, 3, 4)

    def column(i, lanes, air_ref):
        if i < 2:
            return above_ref[i * channels : (i + 1) * channels, lanes]
        if i < rows + 2:
            return air_ref[i - 2]
        i = i - rows - 2
        return below_ref[i * channels : (i + 1) * channels, lanes]

    lane = lax.broadcasted_iota(jnp.int32, (channels, LANES), 1)
    for ref, air_ref, lanes, shift, half in (
        (west_ref, first_ref, slice(0, LANES), 0, 0),
        (east_ref, last_ref, slice(cols - LANES, cols), 66, 32),
    ):
        total = jnp.zeros((channels, LANES), F32)
        for i in range(rows + 4):
            moved = pltpu.roll(column(i, lanes, air_ref).astype(F32), (2 * i + shift) % LANES, 1)
            total = jnp.where(lane >> 1 == i + half, moved, total)
        ref[0:channels] = total.astype(BF)
        first = channels
        for part in (coded(cell_ref[...]), above_ref[0:64, cols:], below_ref[0:64, cols:]):
            ref[first : first + 64] = part
            first += 64


def sides(air, above, below, cells):
    channels, cols = air.shape[1:]
    every = slice(None)
    return call(
        side_body,
        (jax.ShapeDtypeStruct((channels + 3 * 64, LANES), BF),) * 2,
        [air, air, above, below, cells],
        parts={0: (every, every, slice(0, LANES)), 1: (every, every, slice(cols - LANES, cols))},
    )


def shifted(center, from_left, from_right, at_left, at_right, left_lane, right_lane):
    width = center.shape[1]
    left = pltpu.roll(from_left, 1, 1)
    right = pltpu.roll(from_right, width - 1, 1)
    lane = lax.broadcasted_iota(jnp.int32, at_left.shape, 1)
    first = jnp.where(lane == 0, pltpu.roll(at_left, LANES - left_lane, 1), left[:, :LANES])
    last = jnp.where(
        lane == LANES - 1, pltpu.roll(at_right, LANES - 1 - right_lane, 1), right[:, -LANES:]
    )
    left = jnp.concatenate([first, left[:, LANES:]], axis=1)
    right = jnp.concatenate([right[:, :-LANES], last], axis=1)
    return center + (left + right)


def stack_weight(weight_ref, out):
    taps, _, channels, _ = weight_ref.shape
    none = jnp.zeros((channels, channels), F32)
    for u in range(taps):
        rows = [weight_ref[p, u].astype(F32) for p in range(taps)]
        for k, line in enumerate((rows + [none], [none] + rows)):
            first = (k * taps + u) * channels
            out[first : first + channels] = jnp.concatenate(line, axis=1).astype(BF)


def atmosphere_body(
    wait, air_ref, above_ref, below_ref, west_ref, east_ref, own_west_ref, own_east_ref, field,
    vals_ref, cell_ref, heat_weight_ref, weight1_ref, weight2_ref,
    next_out, send_ref,
    next_ref, out_done, start, hidden, edge1, edge2, first_ref, second_ref, targets, left, right,
):
    rows, channels, cols = next_ref.shape
    taps = 3 * channels
    tile, tiles = lax.axis_index("tile"), lax.axis_size("tile")
    edge_ref = [jnp.where(tile > 0, 1.0, 0.0), jnp.where(tile < tiles - 1, 1.0, 0.0)]
    wait(3, 4, 8)
    around = scatter_beside(vals_ref, west_ref, east_ref, targets, left, right, rows, cols)
    wait(11, 12)
    stack_weight(weight1_ref, first_ref)
    stack_weight(weight2_ref, second_ref)
    wait(0, 1, 2, 5, 6, 7, 9, 10)
    lane = lax.broadcasted_iota(jnp.int32, (channels, LANES), 1)
    row = lax.broadcasted_iota(jnp.int32, (channels, channels), 0)
    same = row == lax.broadcasted_iota(jnp.int32, (channels, channels), 1)
    weights = jnp.sum(jnp.where(same, heat_weight_ref[...], 0.0), axis=1, keepdims=True)
    heat_weight = jnp.broadcast_to(weights, (channels, cols))

    beside = jnp.where(
        lane < 64, east_ref[0:channels].astype(F32), west_ref[0:channels].astype(F32)
    )
    beside = pltpu.roll(beside, 64, 1)
    own = own_west_ref[0:channels].astype(F32) + own_east_ref[0:channels].astype(F32)
    narrow = heat_weight[:, 0:LANES]
    beside = beside + narrow * around
    own = own + narrow * end_columns(field[...])

    def three_rows(x):
        return jnp.concatenate(
            [x, pltpu.roll(x, LANES - 2, 1), pltpu.roll(x, LANES - 4, 1)], axis=0
        ).astype(BF)

    plain = jnp.dot(
        first_ref[0:taps, 0:taps],
        jnp.concatenate([three_rows(beside), three_rows(own)], axis=1),
        preferred_element_type=F32,
    )

    def tap(u, of_own):
        return plain[u * channels : (u + 1) * channels, of_own * LANES : (of_own + 1) * LANES]

    def back(x):
        return pltpu.roll(x, LANES - 1, 1)

    edge1[0] = tap(0, 0)
    edge1[1] = tap(2, 0)
    at_left = tap(0, 0) + back(tap(1, 0)) + tap(2, 1)
    at_right = back(tap(0, 1)) + tap(1, 0) + back(tap(2, 0))
    place = lane & 63
    inside = jnp.where(
        place == 0, edge_ref[0], jnp.where(place == 2 * (rows + 1), edge_ref[1], 1.0)
    )
    hidden_beside = gelu(jnp.where(lane < 64, at_left, at_right)) * inside
    plain = jnp.dot(
        second_ref[0:taps, 0:taps], three_rows(hidden_beside), preferred_element_type=F32
    )
    edge2[0] = plain[0:channels]
    edge2[1] = plain[2 * channels : taps]

    for i in range(2):
        for ref, r in ((above_ref, i), (below_ref, rows + 2 + i)):
            x = ref[i * channels : (i + 1) * channels, 0:cols].astype(F32)
            start[r] = (x + heat_weight * field[r : r + 1, :]).astype(BF)

    def first_stage(j):
        for k in range(2):
            r = 2 * j + k
            x = air_ref[r].astype(F32) + heat_weight * field[pl.ds(r + 2, 1), :]
            start[r + 2] = x.astype(BF)

    def mixed(weight_ref, source, j):
        window = source[pl.ds(2 * j, 4)].reshape(4 * channels, cols)
        return jnp.dot(weight_ref[...], window, preferred_element_type=F32)

    def parts(product, k):
        return [
            product[(3 * k + u) * channels : (3 * k + u + 1) * channels] for u in (1, 0, 2)
        ]

    def second_stage(j):
        product = mixed(first_ref, start, j)
        for k in range(2):
            h = 2 * j + k
            inside = jnp.where(h == 0, edge_ref[0], jnp.where(h == rows + 1, edge_ref[1], 1.0))
            total = shifted(*parts(product, k), edge1[0], edge1[1], 2 * h + 1, 64 + 2 * h)
            hidden[h] = (gelu(total) * inside).astype(BF)

    def third_stage(j):
        product = mixed(second_ref, hidden, j)
        for k in range(2):
            r = 2 * j + k
            total = shifted(*parts(product, k), edge2[0], edge2[1], 2 * r, 64 + 2 * r)
            next_ref[r] = (start[r + 2].astype(F32) + total).astype(BF)

    def steps(first, last, *stages):
        def step(j, carry):
            for stage, late in stages:
                stage(j - late)
            return carry

        lax.fori_loop(first, last, step, 0)

    half = rows // 2
    one, two, three = (first_stage, 0), (second_stage, 1), (third_stage, 3)
    steps(0, 1, one)
    steps(1, 3, two, one)
    steps(3, half, three, two, one)
    steps(half, half + 2, three, two)
    steps(half + 2, half + 3, three)


    copy = pltpu.make_async_copy(next_ref, next_out, out_done.at[0])
    copy.start()
    gather_cells(next_ref, cell_ref, send_ref)
    copy.wait()


def gather_cells(next_ref, cell_ref, send_ref):
    rows, channels, cols = next_ref.shape
    shift = cols.bit_length() - 1
    width = 256
    group = 6

    def pick(tile):
        cell = cell_ref[:, lanes_at(tile, width)]
        low = one_hot(cell & (cols - 1), cols)
        high = (cell >> shift).astype(F32).astype(BF)
        total = jnp.zeros((channels, width), BF)
        for g in range(0, rows, group):
            block = next_ref[g : g + group].reshape(group * channels, cols)
            got = jnp.dot(block, low, preferred_element_type=F32).astype(BF)
            for r in range(group):
                here = high == jnp.asarray(g + r, BF)
                total = jnp.where(here, got[r * channels : (r + 1) * channels], total)
        for part in range(width // LANES):
            send_ref[tile * (width // LANES) + part] = total[:, part * LANES : (part + 1) * LANES]

    for_chunks(cell_ref.shape[1] // width, 4, pick)


def atmosphere(
    air, above, below, west, east, to_west, to_east, field, vals, cells, heat_weight, first, second
):
    rows, channels, cols = air.shape
    slots = cells.size
    stacked = pltpu.VMEM((6 * channels, 4 * channels), BF)
    return call(
        atmosphere_body,
        (
            jax.ShapeDtypeStruct((rows, channels, cols), BF),
            jax.ShapeDtypeStruct((slots // LANES, channels, LANES), BF),
        ),
        [
            air, above, below, west, east, to_west, to_east, field, vals, cells,
            heat_weight.reshape(1, -1), first, second,
        ],
        out_specs=(HBM, VMEM),
        limit=VMEM_WHOLE,
        scratch=[
            pltpu.VMEM((rows, channels, cols), BF),
            pltpu.SemaphoreType.DMA((1,)),
            pltpu.VMEM((rows + 4, channels, cols), BF),
            pltpu.VMEM((rows + 2, channels, cols), BF),
            pltpu.VMEM((2, channels, LANES), F32),
            pltpu.VMEM((2, channels, LANES), F32),
            stacked,
            stacked,
            pltpu.VMEM((6, slots // LANES, LANES), jnp.int32),
            pltpu.VMEM((16, slots), BF),
            pltpu.VMEM((LANES, slots), BF),
        ],
    )


def forcing_body(
    wait, arrived_ref, slot_ref, ocean_ref, index_ref, out_ref, head_ref, tail_ref, table
):
    groups, channels, depth = table.shape
    wait(0, 1, 2, 3)
    parts = depth // LANES
    for g in range(groups):
        for p in range(parts):
            table[g, :, p * LANES : (p + 1) * LANES] = arrived_ref[g * parts + p]
    shift = depth.bit_length() - 1
    width = 256

    def block(b, carry):
        lanes = pl.ds(pl.multiple_of(b * width, width), width)
        slot = slot_ref[:, lanes]
        low = one_hot(slot & (depth - 1), depth)
        high = slot >> shift
        got = jnp.dot(
            table[...].reshape(groups * channels, depth), low, preferred_element_type=F32
        )
        total = got[0:channels]
        for g in range(1, groups):
            total = jnp.where(high == g, got[g * channels : (g + 1) * channels], total)
        out_ref[:, lanes] = (ocean_ref[:, lanes].astype(F32) + total).astype(BF)
        return carry

    channels, cells = ocean_ref.shape
    lax.fori_loop(0, cells // width, block, 0)
    reach = 2 * HALO
    for ref, first, start in ((head_ref, 0, 0), (tail_ref, cells - reach, cells - HALO)):
        ref[0:channels] = out_ref[:, first : first + reach]
        index = index_ref[:, start : start + HALO]
        far = index - start - lax.broadcasted_iota(jnp.int32, index.shape, 1)
        rest = jnp.zeros((ref.shape[0] - channels - index.shape[0], reach), F32)
        code = jnp.concatenate([far & (HALO - 1), far >> 8], axis=1).astype(F32)
        ref[channels:] = jnp.concatenate([code, rest], axis=0).astype(BF)


def add_forcing(arrived, slots, ocean, index, *ready):
    channels = ocean.shape[0]
    depth = 512
    end = jax.ShapeDtypeStruct((channels + 16, 2 * HALO), BF)
    return call(
        forcing_body,
        (jax.ShapeDtypeStruct(ocean.shape, BF), end, end),
        [arrived, slots.reshape(1, -1), ocean, index, *ready],
        untouched=range(4, 4 + len(ready)),
        scratch=[pltpu.VMEM((arrived.shape[0] * LANES // depth, channels, depth), BF)],
    )


def neighbour_block(source, b, local, weight):
    channels, width = source.shape[1:]
    window = source[pl.ds(b, 3)].reshape(3 * channels, width)
    picked = []
    for k in range(local.shape[0]):
        where = local[k : k + 1, :]
        got = jnp.dot(window, one_hot(where & (width - 1), width), preferred_element_type=F32)
        high = where >> 8
        picked.append(
            jnp.where(
                high == 0,
                got[0:channels],
                jnp.where(high == 1, got[channels : 2 * channels], got[2 * channels :]),
            ).astype(BF)
        )
    return jnp.dot(weight, jnp.concatenate(picked, axis=0), preferred_element_type=F32)


def own_positions(index_ref, b):
    return index_ref[:, b * HALO : (b + 1) * HALO] - b * HALO


def hide_block(hidden, at, values, b, local, weight_ref, inside=None):
    mixed = gelu(neighbour_block(values, b, local, weight_ref[...]))
    hidden[at] = (mixed if inside is None else mixed * inside).astype(BF)


def inner_body(
    wait, own_ref, index_ref, first_ref, second_ref, hidden_ref, out_ref, values, local
):
    wait(0, 1, 2, 3)
    taps = index_ref.shape[0]
    blocks = values.shape[0]
    for b in range(blocks):
        values[b] = own_ref[:, b * HALO : (b + 1) * HALO]
    for b in range(blocks - 2):
        local[b, 0:taps] = own_positions(index_ref, b + 1)

    def hide(b, carry):
        hide_block(hidden_ref, b, values, b, local[b, 0:taps], first_ref)
        return carry

    lax.fori_loop(0, blocks - 2, hide, 0)

    def finish(b, carry):
        mixed = neighbour_block(hidden_ref, b, local[b + 1, 0:taps], second_ref[...])
        lanes = pl.ds(pl.multiple_of(b * HALO, HALO), HALO)
        out_ref[:, lanes] = (values[b + 2].astype(F32) + mixed).astype(BF)
        return carry

    lax.fori_loop(0, blocks - 4, finish, 0)


def ocean_inner(own, index, first, second):
    channels, cells = own.shape
    blocks = cells // HALO
    return call(
        inner_body,
        (
            jax.ShapeDtypeStruct((blocks - 2, channels, HALO), BF),
            jax.ShapeDtypeStruct((channels, cells - 4 * HALO), BF),
        ),
        [own, index, first, second],
        scratch=[
            pltpu.VMEM((blocks, channels, HALO), BF),
            pltpu.VMEM((blocks - 2, 16, HALO), jnp.int32),
        ],
    )


def outer_body(
    wait, own_ref, inner_ref, done_ref, before_ref, after_ref, index_ref, first_ref, second_ref,
    out_ref, values, hidden, local,
):
    width = HALO
    both = ("face", "tile")
    number, devices = lax.axis_index(both), lax.axis_size(both)
    edge_ref = [jnp.where(number > 0, 1.0, 0.0), jnp.where(number < devices - 1, 1.0, 0.0)]
    wait(*range(8))
    channels, blocks = own_ref.shape[0], own_ref.shape[1] // width
    taps = index_ref.shape[0]
    for b in range(2):
        lanes = slice(b * width, (b + 1) * width)
        values[b] = before_ref[0:channels, lanes]
        values[2 + b] = own_ref[:, lanes]
        values[4 + b] = own_ref[:, (blocks - 2 + b) * width : (blocks - 1 + b) * width]
        values[6 + b] = after_ref[0:channels, lanes]
        hidden[2 + b] = inner_ref[b]
        hidden[4 + b] = inner_ref[blocks - 4 + b]
    out_ref[:, 2 * width : (blocks - 2) * width] = done_ref[...]
    for i, b in enumerate((0, 1, blocks - 2, blocks - 1)):
        local[1 + i, 0:taps] = own_positions(index_ref, b)
    place = lax.broadcasted_iota(jnp.int32, (taps, width), 1)
    for i, ref in ((0, before_ref), (5, after_ref)):
        code = ref[channels:].astype(F32).astype(jnp.int32)[0:taps]
        local[i, 0:taps] = place + code[:, :width] + (code[:, width:] << 8)
    for at, first, i, inside in (
        (0, 0, 0, edge_ref[0]), (1, 1, 1, None), (6, 4, 4, None), (7, 5, 5, edge_ref[1])
    ):
        hide_block(hidden, at, values, first, local[i, 0:taps], first_ref, inside)
    for b, first, i in ((0, 0, 1), (1, 1, 2), (blocks - 2, 4, 3), (blocks - 1, 5, 4)):
        mixed = neighbour_block(hidden, first, local[i, 0:taps], second_ref[...])
        lanes = slice(b * width, (b + 1) * width)
        out_ref[:, lanes] = (own_ref[:, lanes].astype(F32) + mixed).astype(BF)


def flat_weight(weight):
    taps, out, inner = weight.shape
    return jnp.transpose(weight, (1, 0, 2)).reshape(out, taps * inner)


def ocean_outer(own, inner, done, before, after, index, first, second):
    channels = own.shape[0]
    return call(
        outer_body,
        jax.ShapeDtypeStruct(own.shape, BF),
        [own, inner, done, before, after, index, first, second],
        scratch=[
            pltpu.VMEM((8, channels, HALO), BF),
            pltpu.VMEM((8, channels, HALO), BF),
            pltpu.VMEM((6, 16, HALO), jnp.int32),
        ],
    )


def from_neighbours(low, high, axis, closed=False):
    count = lax.axis_size(axis)
    ends = count if closed else count - 1
    before = lax.ppermute(high, axis, [(i, (i + 1) % count) for i in range(ends)])
    after = lax.ppermute(low, axis, [((i + 1) % count, i) for i in range(ends)])
    return before, after


def shards(
    atmos,
    ocean,
    surface_heat_weight,
    air_conv_first_weight,
    air_conv_second_weight,
    marine_conv_first_weight,
    marine_conv_second_weight,
    marine_coupling_slot,
    coupling_air_cells,
    marine_neighbour_index,
):
    both = ("face", "tile")
    devices = lax.axis_size(both)
    faces, tiles = lax.axis_size("face"), lax.axis_size("tile")
    slot_space = coupling_air_cells.shape[1]
    capacity = slot_space // devices
    channels, rows, cols = atmos.shape

    own_cells = coupling_air_cells.reshape(-1, LANES)
    code = coded(own_cells)
    code = jnp.concatenate([code, jnp.zeros((2 * channels - code.shape[0], LANES), BF)], axis=0)

    def two_rows(first):
        two = jnp.transpose(atmos[:, first : first + 2], (1, 0, 2)).reshape(2 * channels, cols)
        return jnp.concatenate([two, code], axis=1)

    low, high, heats = lax.optimization_barrier((two_rows(0), two_rows(rows - 2), ocean))
    above, below = from_neighbours(low, high, "tile")

    table = heat_table(heats, marine_coupling_slot, capacity, faces, tiles)
    table, above = lax.optimization_barrier((table, above))
    heat = heat_slots(table, both)

    air = jnp.transpose(atmos, (1, 0, 2))
    to_west, to_east = sides(air, above, below, own_cells)
    west, east = from_neighbours(to_west, to_east, "face", closed=True)

    field = scatter_heat(heat, coupling_air_cells, above, below, rows)
    air_next, outgoing = atmosphere(
        air, above, below, west, east, to_west, to_east, field, heat, coupling_air_cells,
        surface_heat_weight, air_conv_first_weight, air_conv_second_weight,
    )
    air_out = jnp.transpose(air_next, (1, 0, 2))

    def by_device(blocks):
        many = LANES // capacity
        split = blocks.reshape(-1, channels, many, capacity)
        return jnp.transpose(split, (0, 2, 1, 3)).reshape(devices, channels, capacity)

    def by_lanes(blocks):
        many = LANES // capacity
        split = blocks.reshape(-1, many, channels, capacity)
        return jnp.transpose(split, (0, 2, 1, 3)).reshape(-1, channels, LANES)

    if capacity != LANES:
        outgoing = by_device(outgoing)
    arrived = lax.all_to_all(outgoing, both, split_axis=0, concat_axis=0, tiled=True)
    if capacity != LANES:
        arrived = by_lanes(arrived)

    first_mix = flat_weight(marine_conv_first_weight)
    second_mix = flat_weight(marine_conv_second_weight)
    ocean_start, head, tail = add_forcing(
        arrived, marine_coupling_slot, ocean, marine_neighbour_index, air_out, first_mix, second_mix
    )
    before, after = from_neighbours(head, tail, both)
    inner, done = ocean_inner(ocean_start, marine_neighbour_index, first_mix, second_mix)
    ocean_next = ocean_outer(
        ocean_start,
        inner,
        done,
        before,
        after,
        marine_neighbour_index,
        first_mix,
        second_mix,
    )
    return (air_out, ocean_next)


def solution(mesh):
    placed = (
        P(None, "tile", "face"),
        P(None, ("face", "tile")),
        P(),
        P(),
        P(),
        P(),
        P(),
        P(("face", "tile")),
        P(("face", "tile"), None),
        P(None, ("face", "tile")),
    )
    return jax.shard_map(
        shards,
        mesh=mesh,
        in_specs=placed,
        out_specs=(P(None, "tile", "face"), P(None, ("face", "tile"))),
        check_vma=False,
    )
```

```python
import jax
import jax.numpy as jnp
import numpy as np
from jax import lax
from jax.experimental import pallas as pl
from jax.experimental.pallas import tpu as pltpu
from jax.sharding import PartitionSpec as P

HALO = 256
LANES = 128
BF = jnp.bfloat16
F32 = jnp.float32
NEIGHBOURS = ((0, 0), (-1, 0), (1, 0), (0, -1), (0, 1), (-1, -1), (1, -1), (-1, 1), (1, 1))
VMEM_LIMIT = 20 * 1024 * 1024
VMEM_WHOLE = 60 * 1024 * 1024
VMEM_MOST = 62_200_000

VMEM = pl.BlockSpec(memory_space=pltpu.VMEM)
ANY = pl.BlockSpec(memory_space=pl.ANY)
HBM = pl.BlockSpec(memory_space=pltpu.HBM)


def call(body, outs, ins, scratch=(), parts=None, untouched=(), out_specs=None, limit=None):
    if limit is None:
        touched = [i for i in range(len(ins)) if i not in untouched]

        def plain(*refs):
            body(lambda *_: None, *(refs[i] for i in touched), *refs[len(ins) :])

        return pl.pallas_call(
            plain,
            out_shape=outs,
            in_specs=[VMEM if i in touched else ANY for i in range(len(ins))],
            out_specs=jax.tree.map(lambda _: VMEM, outs),
            scratch_shapes=list(scratch),
            compiler_params=pltpu.CompilerParams(vmem_limit_bytes=VMEM_LIMIT),
        )(*ins)
    parts = parts or {}
    held = [i for i in range(len(ins)) if i not in untouched]
    shapes = [
        tuple(len(range(*cut.indices(n))) for cut, n in zip(parts[i], ins[i].shape))
        if i in parts
        else ins[i].shape
        for i in held
    ]
    count = len(jax.tree.leaves(outs))

    def kernel(*refs):
        sources, refs = refs[: len(ins)], refs[len(ins) :]
        results, refs = refs[:count], refs[count:]
        copies, refs, done = refs[: len(held)], refs[len(held) : -1], refs[-1]
        moves = {}
        for k, i in enumerate(held):
            source = sources[i].at[parts[i]] if i in parts else sources[i]
            moves[i] = pltpu.make_async_copy(source, copies[k], done.at[k])
            moves[i].start()
        waiting = set(held)

        def wait(*which):
            for i in which:
                waiting.remove(i)
                moves[i].wait()

        body(wait, *copies, *results, *refs)
        assert not waiting

    return pl.pallas_call(
        kernel,
        out_shape=outs,
        in_specs=[ANY] * len(ins),
        out_specs=out_specs or jax.tree.map(lambda _: VMEM, outs),
        scratch_shapes=[pltpu.VMEM(shape, ins[i].dtype) for shape, i in zip(shapes, held)]
        + list(scratch)
        + [pltpu.SemaphoreType.DMA((len(held),))],
        compiler_params=pltpu.CompilerParams(vmem_limit_bytes=limit),
    )(*ins)


def one_hot(index_row, size):
    places = lax.broadcasted_iota(jnp.int32, (size, index_row.shape[1]), 0)
    return jnp.where(places == index_row, 1.0, 0.0).astype(BF)


def nt_dot(a, b):
    return lax.dot_general(a, b, (((1,), (1,)), ((), ())), preferred_element_type=F32)


def gelu(x):
    inner = x * (0.7978845608028654 + 0.035677408136300125 * (x * x))
    return (0.5 * x) * (1.0 + jnp.tanh(inner))


def slot_values(heat_ref, slot_ref, rows):
    heat = heat_ref[0:16, :].astype(F32)[0:1]
    slot = slot_ref[...]
    places = lax.broadcasted_iota(jnp.int32, (rows, slot.shape[1]), 0)
    match = places == (slot >> 7)
    left = jnp.concatenate([jnp.where(match, heat, 0.0), jnp.where(match, 1.0, 0.0)], axis=0)
    return nt_dot(left.astype(BF), one_hot(slot & 127, LANES))


def or_inf(value, live):
    return jnp.where(live > 0.5, value, jnp.inf).astype(BF)


def slot_table_body(wait, heat_ref, slot_ref, out_ref):
    wait(0, 1)
    rows = out_ref.shape[0]
    table = slot_values(heat_ref, slot_ref, rows)
    out_ref[...] = or_inf(table[:rows], table[rows:])


def spread_table_body(wait, heat_ref, slot_ref, spread_ref, out_ref):
    wait(0, 1)
    count, rows = spread_ref.shape
    table = slot_values(heat_ref, slot_ref, rows)
    pair = jnp.concatenate([table[:rows], table[rows:]], axis=1).astype(BF)
    wait(2)
    spread = jnp.dot(spread_ref[...], pair, preferred_element_type=F32)
    out_ref[...] = or_inf(spread[:, :LANES], spread[:, LANES:]).reshape(out_ref.shape)


def neighbourhoods(faces, tiles):
    around = np.full((faces * tiles, 16), -1)
    for f in range(faces):
        for t in range(tiles):
            for n, (dr, dc) in enumerate(NEIGHBOURS):
                if 0 <= t + dr < tiles:
                    around[f * tiles + t, n] = (f + dc) % faces * tiles + t + dr
    return around


def heat_table(ocean, slots, capacity, faces, tiles):
    devices = faces * tiles
    around = neighbourhoods(faces, tiles)
    ins = [ocean, slots.reshape(1, -1)]
    if capacity == LANES:
        spread = (around.reshape(-1, 1) == np.arange(devices)).astype(np.float32)
        return call(
            spread_table_body,
            jax.ShapeDtypeStruct((devices, 16, LANES), BF),
            ins + [jnp.asarray(spread, BF)],
            parts={0: (slice(0, 16), slice(None))},
            limit=VMEM_WHOLE,
        )
    rows = devices * capacity // LANES
    table = call(slot_table_body, jax.ShapeDtypeStruct((rows, LANES), BF), ins)
    table = table.reshape(devices, capacity)
    return jnp.where((around >= 0)[:, :, None], table[np.maximum(around, 0)], jnp.inf).astype(BF)


def heat_slots(table, both):
    capacity = table.shape[2]
    got = lax.all_to_all(table, both, split_axis=0, concat_axis=0, tiled=True)
    if capacity != LANES:
        got = jnp.transpose(got, (1, 0, 2)).reshape(16, -1, LANES)
        got = jnp.transpose(got, (1, 0, 2))
    return got


def live_entry(value, cell, cols, rows, dr):
    live = value < jnp.inf
    value = jnp.where(live, value, 0.0)
    row, col = cell >> (cols.bit_length() - 1), cell & (cols - 1)
    if dr == -1:
        live = live & (row >= rows - 2)
    if dr == 1:
        live = live & (row < 2)
    return value, live, row + (rows * dr + 2), col


def for_chunks(count, many, body):
    def step(i, carry):
        for part in range(many):
            body(i * many + part)
        return carry

    lax.fori_loop(0, count // many, step, 0)


def lanes_at(e, width=LANES):
    return pl.ds(pl.multiple_of(e * width, width), width)


def one_hot_heat(value, live, high, size):
    match = lax.broadcasted_iota(jnp.int32, (size, LANES), 0) == jnp.where(live, high, -1)
    both = [jnp.where(match, value, 0.0), jnp.where(match, 1.0, 0.0)]
    return jnp.concatenate(both, axis=0).astype(BF)


def mean_heat(ref, first, count, rows_on, lanes):
    return ref[first : first + count, lanes] / jnp.maximum(
        ref[first + rows_on : first + rows_on + count, lanes], 1.0
    )


def scatter_own_body(wait, vals_ref, cell_ref, out_ref, left, right, prod):
    rows, cols = out_ref.shape
    blocks = cols // LANES
    span = rows * blocks

    def chunk(e):
        lanes = lanes_at(e)
        value, live, row, col = live_entry(
            vals_ref[e].astype(F32)[0:1], cell_ref[:, lanes], cols, rows, 0
        )
        left[:, lanes] = one_hot_heat(value, live, (col >> 7) * rows + row - 2, span)
        right[:, lanes] = one_hot(col & 127, LANES)

    for_chunks(vals_ref.shape[0], 4, chunk)
    prod[...] = nt_dot(left[...], right[...])
    for b in range(blocks):
        out_ref[:, b * LANES : (b + 1) * LANES] = mean_heat(prod, b * rows, rows, span, slice(None))


def scatter_own(vals, cells, rows, cols):
    span = rows * (cols // LANES)
    return call(
        scatter_own_body,
        jax.ShapeDtypeStruct((rows, cols), F32),
        [vals, cells],
        scratch=[
            pltpu.VMEM((2 * span, cells.size), BF),
            pltpu.VMEM((LANES, cells.size), BF),
            pltpu.VMEM((2 * span, LANES), F32),
        ],
    )


def scatter_ends_body(
    wait, own_ref, vals_ref, above_ref, below_ref, out_ref, targets, left, right, prod
):
    rows, cols = own_ref.shape
    targets[0] = decoded(above_ref[0:64, cols:])
    targets[1] = decoded(below_ref[0:64, cols:])
    out_ref[2 : rows + 2, :] = own_ref[...]

    def chunk(e):
        lanes = lanes_at(e)
        values = vals_ref[e].astype(F32)
        for n, (dr, _) in enumerate(NEIGHBOURS[1:3]):
            value, live, row, col = live_entry(
                values[n + 1 : n + 2], targets[n, pl.ds(e, 1), :], cols, rows, dr
            )
            high = 2 * (col >> 7) + row - (0 if dr < 0 else rows + 2)
            left[16 * n : 16 * (n + 1), lanes] = one_hot_heat(value, live, high, 8)
            right[n * LANES : (n + 1) * LANES, lanes] = one_hot(col & 127, LANES)

    for_chunks(vals_ref.shape[0], 4, chunk)
    prod[...] = nt_dot(left[...], right[...])
    for b in range(cols // LANES):
        to = slice(b * LANES, (b + 1) * LANES)
        out_ref[0:2, to] = mean_heat(prod, 2 * b, 2, 8, slice(0, LANES))
        out_ref[rows + 2 : rows + 4, to] = mean_heat(prod, 16 + 2 * b, 2, 8, slice(LANES, None))


def scatter_ends(own, vals, above, below):
    rows, cols = own.shape
    slots = vals.shape[0] * LANES
    return call(
        scatter_ends_body,
        jax.ShapeDtypeStruct((rows + 8, cols), F32),
        [own, vals, above, below],
        scratch=[
            pltpu.VMEM((2, slots // LANES, LANES), jnp.int32),
            pltpu.VMEM((32, slots), BF),
            pltpu.VMEM((2 * LANES, slots), BF),
            pltpu.VMEM((32, 2 * LANES), F32),
        ],
    )


def scatter_beside(vals_ref, west_ref, east_ref, targets, left, right, rows, cols):
    for ref, places in ((west_ref, (0, 2, 3)), (east_ref, (1, 4, 5))):
        first = ref.shape[0] - 3 * 64
        for part, place in enumerate(places):
            targets[place] = decoded(ref[first + 64 * part : first + 64 * (part + 1)])

    def chunk(e):
        lanes = lanes_at(e)
        values = vals_ref[e].astype(F32)
        place = lax.broadcasted_iota(jnp.int32, (64, LANES), 0)
        halves = [jnp.zeros((64, LANES), F32)] * 2
        heats = []
        for k, (dr, dc) in enumerate(NEIGHBOURS[3:]):
            value, live, row, col = live_entry(
                values[k + 3 : k + 4], targets[k, pl.ds(e, 1), :], cols, rows, dr
            )
            side = 0 if dc < 0 else 1
            col = col if side else col - (cols - 2)
            live = live & ((col < 2) if side else (col >= 0))
            code = jnp.where(live, 2 * row + col, -1)
            halves[side] = jnp.where(place == code, 1.0, halves[side])
            heats += [value, jnp.where(live, 1.0, 0.0)]
        heats.append(jnp.zeros((16 - len(heats), LANES), F32))
        left[:, lanes] = jnp.concatenate(heats, axis=0).astype(BF)
        right[:, lanes] = jnp.concatenate(halves, axis=0).astype(BF)

    for_chunks(vals_ref.shape[0], 2, chunk)
    prod = nt_dot(left[...], right[...])
    lane = lax.broadcasted_iota(jnp.int32, (1, LANES), 1)
    place = lane & 63
    around = jnp.zeros((1, LANES), F32)
    for k, (dr, dc) in enumerate(NEIGHBOURS[3:]):
        first, last = {-1: (0, 4), 0: (4, 2 * rows + 4), 1: (2 * rows + 4, 2 * rows + 8)}[dr]
        here = (place >= first) & (place < last) & ((lane >= 64) == (dc > 0))
        mean = prod[2 * k : 2 * k + 1] / jnp.maximum(prod[2 * k + 1 : 2 * k + 2], 1.0)
        around = jnp.where(here, mean, around)
    return around


def end_columns(field):
    high, cols = field.shape
    row = lax.broadcasted_iota(jnp.int32, (high, LANES), 0)
    lane = lax.broadcasted_iota(jnp.int32, (high, LANES), 1)
    here = row < high - 4
    own = jnp.where(here & (lane == 2 * row), field[:, 0:1], 0.0) + jnp.where(
        here & (lane == 2 * row + 65), field[:, cols - 1 : cols], 0.0
    )
    return jnp.sum(own, axis=0, keepdims=True)


def coded(cells):
    return jnp.concatenate([cells >> 7, cells & 127], axis=0).astype(BF)


def decoded(code):
    half = code.shape[0] // 2
    return (code[:half].astype(F32) * 128.0 + code[half:].astype(F32)).astype(jnp.int32)


def side_body(wait, air_ref, above_ref, below_ref, cell_ref, west_ref, east_ref):
    rows, channels, cols = air_ref.shape

    def column(i, lanes):
        if i < 2:
            return above_ref[i * channels : (i + 1) * channels, lanes]
        if i < rows + 2:
            return air_ref[i - 2, :, lanes]
        i = i - rows - 2
        return below_ref[i * channels : (i + 1) * channels, lanes]

    lane = lax.broadcasted_iota(jnp.int32, (channels, LANES), 1)
    for ref, lanes, shift, half in (
        (west_ref, slice(0, LANES), 0, 0),
        (east_ref, slice(cols - LANES, cols), 66, 32),
    ):
        total = jnp.zeros((channels, LANES), F32)
        for i in range(rows + 4):
            moved = pltpu.roll(column(i, lanes).astype(F32), (2 * i + shift) % LANES, 1)
            total = jnp.where(lane >> 1 == i + half, moved, total)
        ref[0:channels] = total.astype(BF)
        first = channels
        for part in (coded(cell_ref[...]), above_ref[0:64, cols:], below_ref[0:64, cols:]):
            ref[first : first + 64] = part
            first += 64


def sides(air, above, below, cells, ready):
    out = jax.ShapeDtypeStruct((air.shape[1] + 3 * 64, LANES), BF)
    return call(side_body, (out, out), [air, above, below, cells, ready], untouched=(4,))


def shifted(center, from_left, from_right, at_left, at_right, left_lane, right_lane):
    width = center.shape[1]
    left = pltpu.roll(from_left, 1, 1)
    right = pltpu.roll(from_right, width - 1, 1)
    lane = lax.broadcasted_iota(jnp.int32, at_left.shape, 1)
    first = jnp.where(lane == 0, pltpu.roll(at_left, LANES - left_lane, 1), left[:, :LANES])
    last = jnp.where(
        lane == LANES - 1, pltpu.roll(at_right, LANES - 1 - right_lane, 1), right[:, -LANES:]
    )
    left = jnp.concatenate([first, left[:, LANES:]], axis=1)
    right = jnp.concatenate([right[:, :-LANES], last], axis=1)
    return center + (left + right)


def stack_weight(weight_ref, out):
    taps, _, channels, _ = weight_ref.shape
    none = jnp.zeros((channels, channels), F32)
    for u in range(taps):
        rows = [weight_ref[p, u].astype(F32) for p in range(taps)]
        for k, line in enumerate((rows + [none], [none] + rows)):
            first = (k * taps + u) * channels
            out[first : first + channels] = jnp.concatenate(line, axis=1).astype(BF)


def atmosphere_body(
    wait, air_ref, above_ref, below_ref, west_ref, east_ref, own_west_ref, own_east_ref, field,
    vals_ref, cell_ref, heat_weight_ref, weight1_ref, weight2_ref,
    next_out, send_ref,
    next_ref, out_done, start, hidden, edge1, edge2, first_ref, second_ref, targets, left, right,
):
    rows, channels, cols = next_ref.shape
    taps = 3 * channels
    tile, tiles = lax.axis_index("tile"), lax.axis_size("tile")
    edge_ref = [jnp.where(tile > 0, 1.0, 0.0), jnp.where(tile < tiles - 1, 1.0, 0.0)]
    wait(3, 4, 8)
    around = scatter_beside(vals_ref, west_ref, east_ref, targets, left, right, rows, cols)
    wait(11, 12)
    stack_weight(weight1_ref, first_ref)
    stack_weight(weight2_ref, second_ref)
    wait(0, 1, 2, 5, 6, 7, 9, 10)
    lane = lax.broadcasted_iota(jnp.int32, (channels, LANES), 1)
    row = lax.broadcasted_iota(jnp.int32, (channels, channels), 0)
    same = row == lax.broadcasted_iota(jnp.int32, (channels, channels), 1)
    weights = jnp.sum(jnp.where(same, heat_weight_ref[...], 0.0), axis=1, keepdims=True)
    heat_weight = jnp.broadcast_to(weights, (channels, cols))

    beside = jnp.where(
        lane < 64, east_ref[0:channels].astype(F32), west_ref[0:channels].astype(F32)
    )
    beside = pltpu.roll(beside, 64, 1)
    own = own_west_ref[0:channels].astype(F32) + own_east_ref[0:channels].astype(F32)
    narrow = heat_weight[:, 0:LANES]
    beside = beside + narrow * around
    own = own + narrow * end_columns(field[...])

    def three_rows(x):
        return jnp.concatenate(
            [x, pltpu.roll(x, LANES - 2, 1), pltpu.roll(x, LANES - 4, 1)], axis=0
        ).astype(BF)

    plain = jnp.dot(
        first_ref[0:taps, 0:taps],
        jnp.concatenate([three_rows(beside), three_rows(own)], axis=1),
        preferred_element_type=F32,
    )

    def tap(u, of_own):
        return plain[u * channels : (u + 1) * channels, of_own * LANES : (of_own + 1) * LANES]

    def back(x):
        return pltpu.roll(x, LANES - 1, 1)

    edge1[0] = tap(0, 0)
    edge1[1] = tap(2, 0)
    at_left = tap(0, 0) + back(tap(1, 0)) + tap(2, 1)
    at_right = back(tap(0, 1)) + tap(1, 0) + back(tap(2, 0))
    place = lane & 63
    inside = jnp.where(
        place == 0, edge_ref[0], jnp.where(place == 2 * (rows + 1), edge_ref[1], 1.0)
    )
    hidden_beside = gelu(jnp.where(lane < 64, at_left, at_right)) * inside
    plain = jnp.dot(
        second_ref[0:taps, 0:taps], three_rows(hidden_beside), preferred_element_type=F32
    )
    edge2[0] = plain[0:channels]
    edge2[1] = plain[2 * channels : taps]

    for i in range(2):
        for ref, r in ((above_ref, i), (below_ref, rows + 2 + i)):
            x = ref[i * channels : (i + 1) * channels, 0:cols].astype(F32)
            start[r] = (x + heat_weight * field[r : r + 1, :]).astype(BF)

    def first_stage(j):
        for k in range(2):
            r = 2 * j + k
            x = air_ref[r].astype(F32) + heat_weight * field[pl.ds(r + 2, 1), :]
            start[r + 2] = x.astype(BF)

    def mixed(weight_ref, source, j):
        window = source[pl.ds(2 * j, 4)].reshape(4 * channels, cols)
        return jnp.dot(weight_ref[...], window, preferred_element_type=F32)

    def parts(product, k):
        return [
            product[(3 * k + u) * channels : (3 * k + u + 1) * channels] for u in (1, 0, 2)
        ]

    def second_stage(j):
        product = mixed(first_ref, start, j)
        for k in range(2):
            h = 2 * j + k
            inside = jnp.where(h == 0, edge_ref[0], jnp.where(h == rows + 1, edge_ref[1], 1.0))
            total = shifted(*parts(product, k), edge1[0], edge1[1], 2 * h + 1, 64 + 2 * h)
            hidden[h] = (gelu(total) * inside).astype(BF)

    def third_stage(j):
        product = mixed(second_ref, hidden, j)
        for k in range(2):
            r = 2 * j + k
            total = shifted(*parts(product, k), edge2[0], edge2[1], 2 * r, 64 + 2 * r)
            next_ref[r] = (start[r + 2].astype(F32) + total).astype(BF)

    def steps(first, last, *stages):
        def step(j):
            for stage, late in stages:
                stage(first + j - late)

        count = last - first
        for_chunks(count, 3 if count % 3 == 0 else 1, step)

    half = rows // 2
    one, two, three = (first_stage, 0), (second_stage, 1), (third_stage, 3)
    steps(0, 1, one)
    steps(1, 3, two, one)
    steps(3, half, three, two, one)
    steps(half, half + 2, three, two)
    steps(half + 2, half + 3, three)


    copy = pltpu.make_async_copy(next_ref, next_out, out_done.at[0])
    copy.start()
    gather_cells(next_ref, cell_ref, send_ref)
    copy.wait()


def gather_cells(next_ref, cell_ref, send_ref):
    rows, channels, cols = next_ref.shape
    shift = cols.bit_length() - 1
    width = 256
    group = 12

    def pick(tile):
        cell = cell_ref[:, lanes_at(tile, width)]
        low = one_hot(cell & (cols - 1), cols)
        high = (cell >> shift).astype(F32).astype(BF)
        total = jnp.zeros((channels, width), BF)
        for g in range(0, rows, group):
            block = next_ref[g : g + group].reshape(group * channels, cols)
            got = jnp.dot(block, low, preferred_element_type=F32).astype(BF)
            for r in range(group):
                here = high == jnp.asarray(g + r, BF)
                total = jnp.where(here, got[r * channels : (r + 1) * channels], total)
        for part in range(width // LANES):
            send_ref[tile * (width // LANES) + part] = total[:, part * LANES : (part + 1) * LANES]

    for_chunks(cell_ref.shape[1] // width, 4, pick)


def atmosphere(
    air, above, below, west, east, to_west, to_east, field, vals, cells, heat_weight, first, second
):
    rows, channels, cols = air.shape
    slots = cells.size
    stacked = pltpu.VMEM((6 * channels, 4 * channels), BF)
    return call(
        atmosphere_body,
        (
            jax.ShapeDtypeStruct((rows, channels, cols), BF),
            jax.ShapeDtypeStruct((slots // LANES, channels, LANES), BF),
        ),
        [
            air, above, below, west, east, to_west, to_east, field, vals, cells,
            heat_weight.reshape(1, -1), first, second,
        ],
        out_specs=(HBM, VMEM),
        limit=VMEM_MOST,
        scratch=[
            pltpu.VMEM((rows, channels, cols), BF),
            pltpu.SemaphoreType.DMA((1,)),
            pltpu.VMEM((rows + 4, channels, cols), BF),
            pltpu.VMEM((rows + 2, channels, cols), BF),
            pltpu.VMEM((2, channels, LANES), F32),
            pltpu.VMEM((2, channels, LANES), F32),
            stacked,
            stacked,
            pltpu.VMEM((6, slots // LANES, LANES), jnp.int32),
            pltpu.VMEM((16, slots), BF),
            pltpu.VMEM((LANES, slots), BF),
        ],
    )


def forcing_body(
    wait, arrived_ref, slot_ref, ocean_ref, index_ref, out_ref, head_ref, tail_ref, table
):
    groups, channels, depth = table.shape
    wait(0, 1, 2, 3)
    parts = depth // LANES
    for g in range(groups):
        for p in range(parts):
            table[g, :, p * LANES : (p + 1) * LANES] = arrived_ref[g * parts + p]
    shift = depth.bit_length() - 1
    width = 256

    def block(b, carry):
        lanes = pl.ds(pl.multiple_of(b * width, width), width)
        slot = slot_ref[:, lanes]
        low = one_hot(slot & (depth - 1), depth)
        high = slot >> shift
        got = jnp.dot(
            table[...].reshape(groups * channels, depth), low, preferred_element_type=F32
        )
        total = got[0:channels]
        for g in range(1, groups):
            total = jnp.where(high == g, got[g * channels : (g + 1) * channels], total)
        out_ref[:, lanes] = (ocean_ref[:, lanes].astype(F32) + total).astype(BF)
        return carry

    channels, cells = ocean_ref.shape
    lax.fori_loop(0, cells // width, block, 0)
    reach = 2 * HALO
    for ref, first, start in ((head_ref, 0, 0), (tail_ref, cells - reach, cells - HALO)):
        ref[0:channels] = out_ref[:, first : first + reach]
        index = index_ref[:, start : start + HALO]
        far = index - start - lax.broadcasted_iota(jnp.int32, index.shape, 1)
        rest = jnp.zeros((ref.shape[0] - channels - index.shape[0], reach), F32)
        code = jnp.concatenate([far & (HALO - 1), far >> 8], axis=1).astype(F32)
        ref[channels:] = jnp.concatenate([code, rest], axis=0).astype(BF)


def add_forcing(arrived, slots, ocean, index, *ready):
    channels = ocean.shape[0]
    depth = 512
    end = jax.ShapeDtypeStruct((channels + 16, 2 * HALO), BF)
    return call(
        forcing_body,
        (jax.ShapeDtypeStruct(ocean.shape, BF), end, end),
        [arrived, slots.reshape(1, -1), ocean, index, *ready],
        untouched=range(4, 4 + len(ready)),
        scratch=[pltpu.VMEM((arrived.shape[0] * LANES // depth, channels, depth), BF)],
    )


def neighbour_block(source, b, local, weight):
    channels, width = source.shape[1:]
    window = source[pl.ds(b, 3)].reshape(3 * channels, width)
    picked = []
    for k in range(local.shape[0]):
        where = local[k : k + 1, :]
        got = jnp.dot(window, one_hot(where & (width - 1), width), preferred_element_type=F32)
        high = where >> 8
        picked.append(
            jnp.where(
                high == 0,
                got[0:channels],
                jnp.where(high == 1, got[channels : 2 * channels], got[2 * channels :]),
            ).astype(BF)
        )
    return jnp.dot(weight, jnp.concatenate(picked, axis=0), preferred_element_type=F32)


def own_positions(index_ref, b):
    return index_ref[:, b * HALO : (b + 1) * HALO] - b * HALO


def hide_block(hidden, at, values, b, local, weight_ref, inside=None):
    mixed = gelu(neighbour_block(values, b, local, weight_ref[...]))
    hidden[at] = (mixed if inside is None else mixed * inside).astype(BF)


def inner_body(
    wait, own_ref, index_ref, first_ref, second_ref, hidden_ref, out_ref, values, local
):
    wait(0, 1, 2, 3)
    taps = index_ref.shape[0]
    blocks = values.shape[0]
    for b in range(blocks):
        values[b] = own_ref[:, b * HALO : (b + 1) * HALO]
    for b in range(blocks - 2):
        local[b, 0:taps] = own_positions(index_ref, b + 1)

    def hide(b, carry):
        hide_block(hidden_ref, b, values, b, local[b, 0:taps], first_ref)
        return carry

    lax.fori_loop(0, blocks - 2, hide, 0)

    def finish(b, carry):
        mixed = neighbour_block(hidden_ref, b, local[b + 1, 0:taps], second_ref[...])
        lanes = pl.ds(pl.multiple_of(b * HALO, HALO), HALO)
        out_ref[:, lanes] = (values[b + 2].astype(F32) + mixed).astype(BF)
        return carry

    lax.fori_loop(0, blocks - 4, finish, 0)


def ocean_inner(own, index, first, second):
    channels, cells = own.shape
    blocks = cells // HALO
    return call(
        inner_body,
        (
            jax.ShapeDtypeStruct((blocks - 2, channels, HALO), BF),
            jax.ShapeDtypeStruct((channels, cells - 4 * HALO), BF),
        ),
        [own, index, first, second],
        scratch=[
            pltpu.VMEM((blocks, channels, HALO), BF),
            pltpu.VMEM((blocks - 2, 16, HALO), jnp.int32),
        ],
    )


def outer_body(
    wait, own_ref, inner_ref, done_ref, before_ref, after_ref, index_ref, first_ref, second_ref,
    out_ref, values, hidden, local,
):
    width = HALO
    both = ("face", "tile")
    number, devices = lax.axis_index(both), lax.axis_size(both)
    edge_ref = [jnp.where(number > 0, 1.0, 0.0), jnp.where(number < devices - 1, 1.0, 0.0)]
    wait(*range(8))
    channels, blocks = own_ref.shape[0], own_ref.shape[1] // width
    taps = index_ref.shape[0]
    for b in range(2):
        lanes = slice(b * width, (b + 1) * width)
        values[b] = before_ref[0:channels, lanes]
        values[2 + b] = own_ref[:, lanes]
        values[4 + b] = own_ref[:, (blocks - 2 + b) * width : (blocks - 1 + b) * width]
        values[6 + b] = after_ref[0:channels, lanes]
        hidden[2 + b] = inner_ref[b]
        hidden[4 + b] = inner_ref[blocks - 4 + b]
    out_ref[:, 2 * width : (blocks - 2) * width] = done_ref[...]
    for i, b in enumerate((0, 1, blocks - 2, blocks - 1)):
        local[1 + i, 0:taps] = own_positions(index_ref, b)
    place = lax.broadcasted_iota(jnp.int32, (taps, width), 1)
    for i, ref in ((0, before_ref), (5, after_ref)):
        code = ref[channels:].astype(F32).astype(jnp.int32)[0:taps]
        local[i, 0:taps] = place + code[:, :width] + (code[:, width:] << 8)
    for at, first, i, inside in (
        (0, 0, 0, edge_ref[0]), (1, 1, 1, None), (6, 4, 4, None), (7, 5, 5, edge_ref[1])
    ):
        hide_block(hidden, at, values, first, local[i, 0:taps], first_ref, inside)
    for b, first, i in ((0, 0, 1), (1, 1, 2), (blocks - 2, 4, 3), (blocks - 1, 5, 4)):
        mixed = neighbour_block(hidden, first, local[i, 0:taps], second_ref[...])
        lanes = slice(b * width, (b + 1) * width)
        out_ref[:, lanes] = (own_ref[:, lanes].astype(F32) + mixed).astype(BF)


def flat_weight(weight):
    taps, out, inner = weight.shape
    return jnp.transpose(weight, (1, 0, 2)).reshape(out, taps * inner)


def ocean_outer(own, inner, done, before, after, index, first, second):
    channels = own.shape[0]
    return call(
        outer_body,
        jax.ShapeDtypeStruct(own.shape, BF),
        [own, inner, done, before, after, index, first, second],
        scratch=[
            pltpu.VMEM((8, channels, HALO), BF),
            pltpu.VMEM((8, channels, HALO), BF),
            pltpu.VMEM((6, 16, HALO), jnp.int32),
        ],
    )


def from_neighbours(low, high, axis, closed=False):
    count = lax.axis_size(axis)
    ends = count if closed else count - 1
    before = lax.ppermute(high, axis, [(i, (i + 1) % count) for i in range(ends)])
    after = lax.ppermute(low, axis, [((i + 1) % count, i) for i in range(ends)])
    return before, after


def shards(
    atmos,
    ocean,
    surface_heat_weight,
    air_conv_first_weight,
    air_conv_second_weight,
    marine_conv_first_weight,
    marine_conv_second_weight,
    marine_coupling_slot,
    coupling_air_cells,
    marine_neighbour_index,
):
    both = ("face", "tile")
    devices = lax.axis_size(both)
    faces, tiles = lax.axis_size("face"), lax.axis_size("tile")
    slot_space = coupling_air_cells.shape[1]
    capacity = slot_space // devices
    channels, rows, cols = atmos.shape

    table = heat_table(ocean, marine_coupling_slot, capacity, faces, tiles)
    table, atmos, own_cells = lax.optimization_barrier(
        (table, atmos, coupling_air_cells.reshape(-1, LANES))
    )
    heat = heat_slots(table, both)

    code = coded(own_cells)
    code = jnp.concatenate([code, jnp.zeros((2 * channels - code.shape[0], LANES), BF)], axis=0)

    def two_rows(first):
        two = jnp.transpose(atmos[:, first : first + 2], (1, 0, 2)).reshape(2 * channels, cols)
        return jnp.concatenate([two, code], axis=1)

    above, below = from_neighbours(two_rows(0), two_rows(rows - 2), "tile")

    air = jnp.transpose(atmos, (1, 0, 2))
    field = scatter_own(heat, coupling_air_cells, rows, cols)
    to_west, to_east = sides(air, above, below, own_cells, field)
    west, east = from_neighbours(to_west, to_east, "face", closed=True)

    field = scatter_ends(field, heat, above, below)
    air_next, outgoing = atmosphere(
        air, above, below, west, east, to_west, to_east, field, heat, coupling_air_cells,
        surface_heat_weight, air_conv_first_weight, air_conv_second_weight,
    )
    air_out = jnp.transpose(air_next, (1, 0, 2))

    def by_device(blocks):
        many = LANES // capacity
        split = blocks.reshape(-1, channels, many, capacity)
        return jnp.transpose(split, (0, 2, 1, 3)).reshape(devices, channels, capacity)

    def by_lanes(blocks):
        many = LANES // capacity
        split = blocks.reshape(-1, many, channels, capacity)
        return jnp.transpose(split, (0, 2, 1, 3)).reshape(-1, channels, LANES)

    if capacity != LANES:
        outgoing = by_device(outgoing)
    arrived = lax.all_to_all(outgoing, both, split_axis=0, concat_axis=0, tiled=True)
    if capacity != LANES:
        arrived = by_lanes(arrived)

    first_mix = flat_weight(marine_conv_first_weight)
    second_mix = flat_weight(marine_conv_second_weight)
    ocean_start, head, tail = add_forcing(
        arrived, marine_coupling_slot, ocean, marine_neighbour_index, air_out, first_mix, second_mix
    )
    before, after = from_neighbours(head, tail, both)
    inner, done = ocean_inner(ocean_start, marine_neighbour_index, first_mix, second_mix)
    ocean_next = ocean_outer(
        ocean_start,
        inner,
        done,
        before,
        after,
        marine_neighbour_index,
        first_mix,
        second_mix,
    )
    return (air_out, ocean_next)


def solution(mesh):
    placed = (
        P(None, "tile", "face"),
        P(None, ("face", "tile")),
        P(),
        P(),
        P(),
        P(),
        P(),
        P(("face", "tile")),
        P(("face", "tile"), None),
        P(None, ("face", "tile")),
    )
    return jax.shard_map(
        shards,
        mesh=mesh,
        in_specs=placed,
        out_specs=(P(None, "tile", "face"), P(None, ("face", "tile"))),
        check_vma=False,
    )
```

```python
import jax
import jax.numpy as jnp
import numpy as np
from jax import lax
from jax.experimental import pallas as pl
from jax.experimental.pallas import tpu as pltpu
from jax.sharding import PartitionSpec as P

HALO = 256
LANES = 128
BF = jnp.bfloat16
F32 = jnp.float32
NEIGHBOURS = ((0, 0), (-1, 0), (1, 0), (0, -1), (0, 1), (-1, -1), (1, -1), (-1, 1), (1, 1))
VMEM_LIMIT = 20 * 1024 * 1024
VMEM_WHOLE = 60 * 1024 * 1024
VMEM_MOST = 62_200_000

VMEM = pl.BlockSpec(memory_space=pltpu.VMEM)
ANY = pl.BlockSpec(memory_space=pl.ANY)
HBM = pl.BlockSpec(memory_space=pltpu.HBM)


def call(body, outs, ins, scratch=(), parts=None, untouched=(), scalars=(), out_specs=None, limit=None):
    if limit is None:
        touched = [i for i in range(len(ins)) if i not in untouched]

        def plain(*refs):
            body(lambda *_: None, *(refs[i] for i in touched), *refs[len(ins) :])

        return pl.pallas_call(
            plain,
            out_shape=outs,
            in_specs=[VMEM if i in touched else ANY for i in range(len(ins))],
            out_specs=jax.tree.map(lambda _: VMEM, outs),
            scratch_shapes=list(scratch),
            compiler_params=pltpu.CompilerParams(vmem_limit_bytes=VMEM_LIMIT),
        )(*ins)
    parts = parts or {}
    held = [i for i in range(len(ins)) if i not in untouched]
    shapes = [
        tuple(len(range(*cut.indices(n))) for cut, n in zip(parts[i], ins[i].shape))
        if i in parts
        else ins[i].shape
        for i in held
    ]
    count = len(jax.tree.leaves(outs))

    def kernel(*refs):
        sources, refs = refs[: len(ins)], refs[len(ins) :]
        results, refs = refs[:count], refs[count:]
        copies, refs, done = refs[: len(held)], refs[len(held) : -1], refs[-1]
        moves = {}
        for k, i in enumerate(held):
            source = sources[i].at[parts[i]] if i in parts else sources[i]
            moves[i] = pltpu.make_async_copy(source, copies[k], done.at[k])
            moves[i].start()
        waiting = set(held)

        def wait(*which):
            for i in which:
                waiting.remove(i)
                moves[i].wait()

        body(wait, *copies, *results, *refs)
        assert not waiting

    return pl.pallas_call(
        kernel,
        out_shape=outs,
        in_specs=[ANY] * len(ins),
        out_specs=out_specs or jax.tree.map(lambda _: VMEM, outs),
        scratch_shapes=[
            (pltpu.SMEM if i in scalars else pltpu.VMEM)(shape, ins[i].dtype)
            for shape, i in zip(shapes, held)
        ]
        + list(scratch)
        + [pltpu.SemaphoreType.DMA((len(held),))],
        compiler_params=pltpu.CompilerParams(vmem_limit_bytes=limit),
    )(*ins)


def one_hot(index_row, size):
    places = lax.broadcasted_iota(jnp.int32, (size, index_row.shape[1]), 0)
    return jnp.where(places == index_row, 1.0, 0.0).astype(BF)


def nt_dot(a, b):
    return lax.dot_general(a, b, (((1,), (1,)), ((), ())), preferred_element_type=F32)


def gelu(x):
    inner = x * (0.7978845608028654 + 0.035677408136300125 * (x * x))
    return (0.5 * x) * (1.0 + jnp.tanh(inner))


def slot_values(heat_ref, slot_ref, rows):
    heat = heat_ref[0:16, :].astype(F32)[0:1]
    slot = slot_ref[...]
    places = lax.broadcasted_iota(jnp.int32, (rows, slot.shape[1]), 0)
    match = places == (slot >> 7)
    left = jnp.concatenate([jnp.where(match, heat, 0.0), jnp.where(match, 1.0, 0.0)], axis=0)
    return nt_dot(left.astype(BF), one_hot(slot & 127, LANES))


def or_inf(value, live):
    return jnp.where(live > 0.5, value, jnp.inf).astype(BF)


def fold(rows):
    return jnp.concatenate([rows[e : e + 8] for e in range(0, rows.shape[0], 8)], axis=1)


def unfold(block):
    cols = block.shape[1]
    return jnp.concatenate([block[:, at : at + LANES] for at in range(0, cols, LANES)], axis=0)


def unfolded(code):
    code = code.astype(F32)
    return jnp.concatenate([unfold(code[:8]), unfold(code[8:])], axis=0)


def payload_body(cell_ref, rows, payloads):
    count = cell_ref.shape[1] // LANES
    cells = jnp.concatenate(
        [cell_ref[:, e * LANES : (e + 1) * LANES] for e in range(count)], axis=0
    )
    code = coded(fold(cells))
    for row_ref, out_ref in zip(rows, payloads):
        size = row_ref.shape[0]
        out_ref[0:size] = row_ref[...]
        out_ref[size:] = code


def slot_table_body(
    wait, heat_ref, slot_ref, cell_ref, low_ref, high_ref, out_ref, low_out, high_out
):
    rows = out_ref.shape[0]
    table = slot_values(heat_ref, slot_ref, rows)
    out_ref[...] = or_inf(table[:rows], table[rows:])
    payload_body(cell_ref, (low_ref, high_ref), (low_out, high_out))


def spread_table_body(
    wait, heat_ref, slot_ref, cell_ref, low_ref, high_ref, spread_ref, out_ref, low_out, high_out
):
    wait(0, 1)
    count, rows = spread_ref.shape
    table = slot_values(heat_ref, slot_ref, rows)
    pair = jnp.concatenate([table[:rows], table[rows:]], axis=1).astype(BF)
    wait(2, 3, 4, 5)
    spread = jnp.dot(spread_ref[...], pair, preferred_element_type=F32)
    out_ref[...] = or_inf(spread[:, :LANES], spread[:, LANES:]).reshape(out_ref.shape)
    payload_body(cell_ref, (low_ref, high_ref), (low_out, high_out))


def neighbourhoods(faces, tiles):
    around = np.full((faces * tiles, 16), -1)
    for f in range(faces):
        for t in range(tiles):
            for n, (dr, dc) in enumerate(NEIGHBOURS):
                if 0 <= t + dr < tiles:
                    around[f * tiles + t, n] = (f + dc) % faces * tiles + t + dr
    return around


def heat_table(ocean, slots, cells, low, high, capacity, faces, tiles):
    devices = faces * tiles
    around = neighbourhoods(faces, tiles)
    ins = [ocean, slots.reshape(1, -1), cells, low, high]
    payload = jax.ShapeDtypeStruct((low.shape[0] + 16, low.shape[1]), BF)
    if capacity == LANES:
        spread = (around.reshape(-1, 1) == np.arange(devices)).astype(np.float32)
        return call(
            spread_table_body,
            (jax.ShapeDtypeStruct((devices, 16, LANES), BF), payload, payload),
            ins + [jnp.asarray(spread, BF)],
            parts={0: (slice(0, 16), slice(None))},
            limit=VMEM_WHOLE,
        )
    rows = devices * capacity // LANES
    table, low, high = call(
        slot_table_body, (jax.ShapeDtypeStruct((rows, LANES), BF), payload, payload), ins
    )
    table = table.reshape(devices, capacity)
    table = jnp.where((around >= 0)[:, :, None], table[np.maximum(around, 0)], jnp.inf)
    return table.astype(BF), low, high


def heat_slots(table, both):
    capacity = table.shape[2]
    got = lax.all_to_all(table, both, split_axis=0, concat_axis=0, tiled=True)
    if capacity != LANES:
        got = jnp.transpose(got, (1, 0, 2)).reshape(16, -1, LANES)
        got = jnp.transpose(got, (1, 0, 2))
    return got


def row_and_column(cell, cols):
    return cell >> (cols.bit_length() - 1), cell & (cols - 1)


def for_chunks(count, many, body):
    def step(i, carry):
        for part in range(many):
            body(i * many + part)
        return carry

    lax.fori_loop(0, count // many, step, 0)


def lanes_at(e, width=LANES):
    return pl.ds(pl.multiple_of(e * width, width), width)


def one_hot_heat(value, live, high, size):
    match = lax.broadcasted_iota(jnp.int32, (size, LANES), 0) == jnp.where(live, high, -1)
    both = [jnp.where(match, value, 0.0), jnp.where(match, 1.0, 0.0)]
    return jnp.concatenate(both, axis=0).astype(BF)


def mean_heat(ref, first, count, rows_on, lanes):
    return ref[first : first + count, lanes] / jnp.maximum(
        ref[first + rows_on : first + rows_on + count, lanes], 1.0
    )


def scatter_own_body(
    wait, vals_ref, cell_ref, weight1_ref, weight2_ref,
    out_ref, first_ref, second_ref, before_ref, list_ref, left, right, prod, lives, packed, places,
):
    rows, cols = out_ref.shape
    blocks = cols // LANES
    span = rows * blocks
    chunks = vals_ref.shape[0]

    def chunk(e):
        lanes = lanes_at(e)
        value = vals_ref[e].astype(F32)[0:1]
        live = value < jnp.inf
        row, col = row_and_column(cell_ref[:, lanes], cols)
        high = (col >> 7) * rows + row
        left[:, lanes] = one_hot_heat(jnp.where(live, value, 0.0), live, high, span)
        right[:, lanes] = one_hot(col & 127, LANES)
        lives[pl.ds(e, 1), :] = jnp.where(live, 1.0, 0.0)

    for_chunks(chunks, 4, chunk)

    def triangle(size, above):
        row = lax.broadcasted_iota(jnp.int32, (size, size), 0)
        column = lax.broadcasted_iota(jnp.int32, (size, size), 1)
        return jnp.where(row < column if above else row > column, 1.0, 0.0).astype(BF)

    live = lives[...].astype(BF)
    in_row = jnp.dot(live, triangle(LANES, True), preferred_element_type=F32)
    rows_above = jnp.dot(triangle(chunks, False), live, preferred_element_type=F32)
    rows_above = jnp.sum(rows_above, axis=1, keepdims=True)
    before_ref[...] = (in_row + rows_above).astype(jnp.int32)
    tiles, width = list_ref.shape

    def pack(e):
        lanes = lanes_at(e)
        place = jnp.where(lives[pl.ds(e, 1), :] > 0.5, before_ref[pl.ds(e, 1), :], -1)
        cell = cell_ref[:, lanes]
        match = lax.broadcasted_iota(jnp.int32, (tiles, LANES), 0) == place >> 8
        parts = [jnp.where(match, part.astype(F32), 0.0) for part in (cell >> 7, cell & 127)]
        packed[:, lanes] = jnp.concatenate(parts, axis=0).astype(BF)
        places[:, lanes] = one_hot(place & (width - 1), width)

    for_chunks(chunks, 4, pack)
    cells = nt_dot(packed[...], places[...])
    list_ref[...] = (cells[:tiles] * 128.0 + cells[tiles:]).astype(jnp.int32)
    stack_weight(weight1_ref, first_ref)
    stack_weight(weight2_ref, second_ref)
    prod[...] = nt_dot(left[...], right[...])
    for b in range(blocks):
        out_ref[:, b * LANES : (b + 1) * LANES] = mean_heat(prod, b * rows, rows, span, slice(None))


def scatter_own(vals, cells, first, second, rows, cols):
    span = rows * (cols // LANES)
    channels = first.shape[2]
    slots = cells.size
    chunks, tiles = slots // LANES, slots // 256
    stacked = jax.ShapeDtypeStruct((6 * channels, 4 * channels), BF)
    return call(
        scatter_own_body,
        (
            jax.ShapeDtypeStruct((rows, cols), F32),
            stacked,
            stacked,
            jax.ShapeDtypeStruct((chunks, LANES), jnp.int32),
            jax.ShapeDtypeStruct((tiles, 256), jnp.int32),
        ),
        [vals, cells, first, second],
        scratch=[
            pltpu.VMEM((2 * span, slots), BF),
            pltpu.VMEM((LANES, slots), BF),
            pltpu.VMEM((2 * span, LANES), F32),
            pltpu.VMEM((chunks, LANES), F32),
            pltpu.VMEM((2 * tiles, slots), BF),
            pltpu.VMEM((256, slots), BF),
        ],
    )


def scatter_ends_body(
    wait, own_ref, vals_ref, above_ref, below_ref, out_ref, targets, left, right, prod
):
    rows, cols = own_ref.shape
    out_ref[2 : rows + 2, :] = own_ref[...]
    for n, (ref, dr) in enumerate(((above_ref, -1), (below_ref, 1))):
        code = unfolded(ref[ref.shape[0] - 16 :])
        row, col = row_and_column(decoded(code), cols)
        row = row - (rows - 2) if dr < 0 else row
        near = (row >= 0) & (row < 2)
        targets[2 * n] = jnp.where(near, 2 * (col >> 7) + row, -1)
        targets[2 * n + 1] = col & 127

    def chunk(e):
        lanes = lanes_at(e)
        values = vals_ref[e].astype(F32)
        for n in range(2):
            value = values[n + 1 : n + 2]
            live = value < jnp.inf
            high, low = (targets[2 * n + part, pl.ds(e, 1), :] for part in range(2))
            left[16 * n : 16 * (n + 1), lanes] = one_hot_heat(
                jnp.where(live, value, 0.0), live, high, 8
            )
            right[n * LANES : (n + 1) * LANES, lanes] = one_hot(low, LANES)

    for_chunks(vals_ref.shape[0], 4, chunk)
    prod[...] = nt_dot(left[...], right[...])
    for b in range(cols // LANES):
        to = slice(b * LANES, (b + 1) * LANES)
        out_ref[0:2, to] = mean_heat(prod, 2 * b, 2, 8, slice(0, LANES))
        out_ref[rows + 2 : rows + 4, to] = mean_heat(prod, 16 + 2 * b, 2, 8, slice(LANES, None))


def scatter_ends(own, vals, above, below):
    rows, cols = own.shape
    slots = vals.shape[0] * LANES
    return call(
        scatter_ends_body,
        jax.ShapeDtypeStruct((rows + 8, cols), F32),
        [own, vals, above, below],
        scratch=[
            pltpu.VMEM((4, slots // LANES, LANES), jnp.int32),
            pltpu.VMEM((32, slots), BF),
            pltpu.VMEM((2 * LANES, slots), BF),
            pltpu.VMEM((32, 2 * LANES), F32),
        ],
    )


def scatter_beside(vals_ref, west_ref, east_ref, targets, left, right, rows, cols):
    for ref, places in ((west_ref, (0, 2, 3)), (east_ref, (1, 4, 5))):
        first = ref.shape[0] - 3 * 64
        for part, place in enumerate(places):
            dr, dc = NEIGHBOURS[3 + place]
            cell = decoded(ref[first + 64 * part : first + 64 * (part + 1)])
            row, col = row_and_column(cell, cols)
            row = row + (rows * dr + 2)
            col = col if dc > 0 else col - (cols - 2)
            near = (row >= 0) & (row < rows + 4) & (col >= 0) & (col < 2)
            targets[place] = jnp.where(near, 2 * row + col, -1)

    def chunk(e):
        lanes = lanes_at(e)
        values = vals_ref[e].astype(F32)
        live = values < jnp.inf
        heats = [jnp.where(live, values, 0.0), jnp.where(live, 1.0, 0.0)]
        left[:, lanes] = jnp.concatenate(heats, axis=0).astype(BF)
        place = lax.broadcasted_iota(jnp.int32, (64, LANES), 0)
        halves = [jnp.zeros((64, LANES), F32)] * 2
        for k, (_, dc) in enumerate(NEIGHBOURS[3:]):
            side = 0 if dc < 0 else 1
            halves[side] = jnp.where(place == targets[k, pl.ds(e, 1), :], 1.0, halves[side])
        right[:, lanes] = jnp.concatenate(halves, axis=0).astype(BF)

    for_chunks(vals_ref.shape[0], 4, chunk)
    prod = nt_dot(left[...], right[...])
    lane = lax.broadcasted_iota(jnp.int32, (1, LANES), 1)
    place = lane & 63
    around = jnp.zeros((1, LANES), F32)
    for k, (dr, dc) in enumerate(NEIGHBOURS[3:]):
        first, last = {-1: (0, 4), 0: (4, 2 * rows + 4), 1: (2 * rows + 4, 2 * rows + 8)}[dr]
        here = (place >= first) & (place < last) & ((lane >= 64) == (dc > 0))
        mean = prod[k + 3 : k + 4] / jnp.maximum(prod[k + 19 : k + 20], 1.0)
        around = jnp.where(here, mean, around)
    return around


def end_columns(field):
    high, cols = field.shape
    row = lax.broadcasted_iota(jnp.int32, (high, LANES), 0)
    lane = lax.broadcasted_iota(jnp.int32, (high, LANES), 1)
    here = row < high - 4
    own = jnp.where(here & (lane == 2 * row), field[:, 0:1], 0.0) + jnp.where(
        here & (lane == 2 * row + 65), field[:, cols - 1 : cols], 0.0
    )
    return jnp.sum(own, axis=0, keepdims=True)


def coded(cells):
    return jnp.concatenate([cells >> 7, cells & 127], axis=0).astype(BF)


def decoded(code):
    half = code.shape[0] // 2
    return (code[:half].astype(F32) * 128.0 + code[half:].astype(F32)).astype(jnp.int32)


def side_body(wait, air_ref, above_ref, below_ref, own_ref, west_ref, east_ref):
    rows, channels, cols = air_ref.shape

    def column(i, lanes):
        if i < 2:
            return above_ref[i * channels : (i + 1) * channels, lanes]
        if i < rows + 2:
            return air_ref[i - 2, :, lanes]
        i = i - rows - 2
        return below_ref[i * channels : (i + 1) * channels, lanes]

    lane = lax.broadcasted_iota(jnp.int32, (channels, LANES), 1)
    for ref, lanes, shift, half in (
        (west_ref, slice(0, LANES), 0, 0),
        (east_ref, slice(cols - LANES, cols), 66, 32),
    ):
        total = jnp.zeros((channels, LANES), F32)
        for i in range(rows + 4):
            moved = pltpu.roll(column(i, lanes).astype(F32), (2 * i + shift) % LANES, 1)
            total = jnp.where(lane >> 1 == i + half, moved, total)
        ref[0:channels] = total.astype(BF)
        first = channels
        for payload in (own_ref, above_ref, below_ref):
            ref[first : first + 64] = unfolded(payload[2 * channels :]).astype(BF)
            first += 64


def sides(air, above, below, own, ready):
    out = jax.ShapeDtypeStruct((air.shape[1] + 3 * 64, LANES), BF)
    return call(side_body, (out, out), [air, above, below, own, ready], untouched=(4,))


def shifted(center, from_left, from_right, at_left, at_right, left_lane, right_lane):
    width = center.shape[1]
    left = pltpu.roll(from_left, 1, 1)
    right = pltpu.roll(from_right, width - 1, 1)
    lane = lax.broadcasted_iota(jnp.int32, at_left.shape, 1)
    first = jnp.where(lane == 0, pltpu.roll(at_left, LANES - left_lane, 1), left[:, :LANES])
    last = jnp.where(
        lane == LANES - 1, pltpu.roll(at_right, LANES - 1 - right_lane, 1), right[:, -LANES:]
    )
    left = jnp.concatenate([first, left[:, LANES:]], axis=1)
    right = jnp.concatenate([right[:, :-LANES], last], axis=1)
    return center + (left + right)


def stack_weight(weight_ref, out):
    taps, _, channels, _ = weight_ref.shape
    none = jnp.zeros((channels, channels), F32)
    for u in range(taps):
        rows = [weight_ref[p, u].astype(F32) for p in range(taps)]
        for k, line in enumerate((rows + [none], [none] + rows)):
            first = (k * taps + u) * channels
            out[first : first + channels] = jnp.concatenate(line, axis=1).astype(BF)


def atmosphere_body(
    wait, air_ref, above_ref, below_ref, west_ref, east_ref, own_west_ref, own_east_ref, field,
    vals_ref, before_ref, number_ref, list_ref, heat_weight_ref, first_ref, second_ref,
    next_out, send_ref,
    next_ref, out_done, start, hidden, edge1, edge2, targets, left, right, compact,
):
    rows, channels, cols = next_ref.shape
    taps = 3 * channels
    tile, tiles = lax.axis_index("tile"), lax.axis_size("tile")
    edge_ref = [jnp.where(tile > 0, 1.0, 0.0), jnp.where(tile < tiles - 1, 1.0, 0.0)]
    wait(3, 4, 8)
    around = scatter_beside(vals_ref, west_ref, east_ref, targets, left, right, rows, cols)
    wait(0, 1, 2, 5, 6, 7, 9, 10, 11, 12, 13, 14)
    lane = lax.broadcasted_iota(jnp.int32, (channels, LANES), 1)
    row = lax.broadcasted_iota(jnp.int32, (channels, channels), 0)
    same = row == lax.broadcasted_iota(jnp.int32, (channels, channels), 1)
    weights = jnp.sum(jnp.where(same, heat_weight_ref[...], 0.0), axis=1, keepdims=True)
    heat_weight = jnp.broadcast_to(weights, (channels, cols))

    beside = jnp.where(
        lane < 64, east_ref[0:channels].astype(F32), west_ref[0:channels].astype(F32)
    )
    beside = pltpu.roll(beside, 64, 1)
    own = own_west_ref[0:channels].astype(F32) + own_east_ref[0:channels].astype(F32)
    narrow = heat_weight[:, 0:LANES]
    beside = beside + narrow * around
    own = own + narrow * end_columns(field[...])

    def three_rows(x):
        return jnp.concatenate(
            [x, pltpu.roll(x, LANES - 2, 1), pltpu.roll(x, LANES - 4, 1)], axis=0
        ).astype(BF)

    plain = jnp.dot(
        first_ref[0:taps, 0:taps],
        jnp.concatenate([three_rows(beside), three_rows(own)], axis=1),
        preferred_element_type=F32,
    )

    def tap(u, of_own):
        return plain[u * channels : (u + 1) * channels, of_own * LANES : (of_own + 1) * LANES]

    def back(x):
        return pltpu.roll(x, LANES - 1, 1)

    edge1[0] = tap(0, 0)
    edge1[1] = tap(2, 0)
    at_left = tap(0, 0) + back(tap(1, 0)) + tap(2, 1)
    at_right = back(tap(0, 1)) + tap(1, 0) + back(tap(2, 0))
    place = lane & 63
    inside = jnp.where(
        place == 0, edge_ref[0], jnp.where(place == 2 * (rows + 1), edge_ref[1], 1.0)
    )
    hidden_beside = gelu(jnp.where(lane < 64, at_left, at_right)) * inside
    plain = jnp.dot(
        second_ref[0:taps, 0:taps], three_rows(hidden_beside), preferred_element_type=F32
    )
    edge2[0] = plain[0:channels]
    edge2[1] = plain[2 * channels : taps]

    for i in range(2):
        for ref, r in ((above_ref, i), (below_ref, rows + 2 + i)):
            x = ref[i * channels : (i + 1) * channels, 0:cols].astype(F32)
            start[r] = (x + heat_weight * field[r : r + 1, :]).astype(BF)

    def first_stage(j):
        for k in range(2):
            r = 2 * j + k
            x = air_ref[r].astype(F32) + heat_weight * field[pl.ds(r + 2, 1), :]
            start[r + 2] = x.astype(BF)

    def mixed(weight_ref, source, j):
        window = source[pl.ds(2 * j, 4)].reshape(4 * channels, cols)
        return jnp.dot(weight_ref[...], window, preferred_element_type=F32)

    def parts(product, k):
        return [
            product[(3 * k + u) * channels : (3 * k + u + 1) * channels] for u in (1, 0, 2)
        ]

    def second_stage(j):
        product = mixed(first_ref, start, j)
        for k in range(2):
            h = 2 * j + k
            inside = jnp.where(h == 0, edge_ref[0], jnp.where(h == rows + 1, edge_ref[1], 1.0))
            total = shifted(*parts(product, k), edge1[0], edge1[1], 2 * h + 1, 64 + 2 * h)
            hidden[h] = (gelu(total) * inside).astype(BF)

    def third_stage(j):
        product = mixed(second_ref, hidden, j)
        for k in range(2):
            r = 2 * j + k
            total = shifted(*parts(product, k), edge2[0], edge2[1], 2 * r, 64 + 2 * r)
            next_ref[r] = (start[r + 2].astype(F32) + total).astype(BF)

    def steps(first, last, *stages):
        def step(j):
            for stage, late in stages:
                stage(first + j - late)

        for_chunks(last - first, 1, step)

    half = rows // 2
    one, two, three = (first_stage, 0), (second_stage, 1), (third_stage, 3)
    steps(0, 1, one)
    steps(1, 3, two, one)
    steps(3, half, three, two, one)
    steps(half, half + 2, three, two)
    steps(half + 2, half + 3, three)


    copy = pltpu.make_async_copy(next_ref, next_out, out_done.at[0])
    copy.start()
    gather_live(next_ref, list_ref, number_ref, compact)
    spread_live(compact, before_ref, number_ref, send_ref)
    copy.wait()


def gather_live(next_ref, list_ref, number_ref, compact):
    rows, channels, cols = next_ref.shape
    shift = cols.bit_length() - 1
    tiles, width = list_ref.shape
    group, many = 6, 2
    compact[...] = jnp.zeros(compact.shape, BF)

    def pick(tile):
        cell = list_ref[pl.ds(tile, 1), :]
        low = one_hot(cell & (cols - 1), cols)
        high = (cell >> shift).astype(F32).astype(BF)
        total = jnp.zeros((channels, width), BF)
        for g in range(0, rows, group):
            block = next_ref[g : g + group].reshape(group * channels, cols)
            got = jnp.dot(block, low, preferred_element_type=F32).astype(BF)
            for r in range(group):
                here = high == jnp.asarray(g + r, BF)
                total = jnp.where(here, got[r * channels : (r + 1) * channels], total)
        compact[tile] = total

    def step(i, carry):
        for part in range(many):
            pick(i * many + part)
        return carry

    last = number_ref[number_ref.shape[0] - 1, number_ref.shape[1] - 1] + 1
    tiles_live = (last + (width - 1)) >> 8
    lax.fori_loop(0, tiles_live >> 1, step, 0)

    @pl.when((tiles_live & 1) == 1)
    def _():
        pick(tiles_live - 1)


def spread_live(compact, before_ref, number_ref, send_ref):
    _, channels, width = compact.shape

    def spread(i):
        place = jnp.concatenate(
            [before_ref[pl.ds(2 * i, 1), :], before_ref[pl.ds(2 * i + 1, 1), :]], axis=1
        )
        first = number_ref[2 * i, 0] >> 8
        window = compact[pl.ds(first, 2)].reshape(2 * channels, width)
        got = jnp.dot(window, one_hot(place & (width - 1), width), preferred_element_type=F32)
        total = jnp.where(place >> 8 == first, got[:channels], got[channels:]).astype(BF)
        for part in range(width // LANES):
            send_ref[2 * i + part] = total[:, part * LANES : (part + 1) * LANES]

    for_chunks(send_ref.shape[0] * LANES // width, 4, spread)


def atmosphere(
    air, above, below, west, east, to_west, to_east, field, vals, before, cells, heat_weight,
    first, second,
):
    rows, channels, cols = air.shape
    slots = before.size
    tiles = cells.shape[0]
    return call(
        atmosphere_body,
        (
            jax.ShapeDtypeStruct((rows, channels, cols), BF),
            jax.ShapeDtypeStruct((slots // LANES, channels, LANES), BF),
        ),
        [
            air, above, below, west, east, to_west, to_east, field, vals, before, before, cells,
            heat_weight.reshape(1, -1), first, second,
        ],
        scalars=(10,),
        out_specs=(HBM, VMEM),
        limit=VMEM_MOST,
        scratch=[
            pltpu.VMEM((rows, channels, cols), BF),
            pltpu.SemaphoreType.DMA((1,)),
            pltpu.VMEM((rows + 4, channels, cols), BF),
            pltpu.VMEM((rows + 2, channels, cols), BF),
            pltpu.VMEM((2, channels, LANES), F32),
            pltpu.VMEM((2, channels, LANES), F32),
            pltpu.VMEM((6, slots // LANES, LANES), jnp.int32),
            pltpu.VMEM((32, slots), BF),
            pltpu.VMEM((LANES, slots), BF),
            pltpu.VMEM((tiles + 1, channels, 256), BF),
        ],
    )


def forcing_body(
    wait, arrived_ref, slot_ref, ocean_ref, index_ref, out_ref, head_ref, tail_ref, table
):
    groups, channels, depth = table.shape
    wait(0, 1, 2, 3)
    parts = depth // LANES
    for g in range(groups):
        for p in range(parts):
            table[g, :, p * LANES : (p + 1) * LANES] = arrived_ref[g * parts + p]
    shift = depth.bit_length() - 1
    width = 256

    def block(b, carry):
        lanes = pl.ds(pl.multiple_of(b * width, width), width)
        slot = slot_ref[:, lanes]
        low = one_hot(slot & (depth - 1), depth)
        high = slot >> shift
        got = jnp.dot(
            table[...].reshape(groups * channels, depth), low, preferred_element_type=F32
        )
        total = got[0:channels]
        for g in range(1, groups):
            total = jnp.where(high == g, got[g * channels : (g + 1) * channels], total)
        out_ref[:, lanes] = (ocean_ref[:, lanes].astype(F32) + total).astype(BF)
        return carry

    channels, cells = ocean_ref.shape
    lax.fori_loop(0, cells // width, block, 0)
    reach = 2 * HALO
    for ref, first, start in ((head_ref, 0, 0), (tail_ref, cells - reach, cells - HALO)):
        ref[0:channels] = out_ref[:, first : first + reach]
        index = index_ref[:, start : start + HALO]
        far = index - start - lax.broadcasted_iota(jnp.int32, index.shape, 1)
        rest = jnp.zeros((ref.shape[0] - channels - index.shape[0], reach), F32)
        code = jnp.concatenate([far & (HALO - 1), far >> 8], axis=1).astype(F32)
        ref[channels:] = jnp.concatenate([code, rest], axis=0).astype(BF)


def add_forcing(arrived, slots, ocean, index, *ready):
    channels = ocean.shape[0]
    depth = 512
    end = jax.ShapeDtypeStruct((channels + 16, 2 * HALO), BF)
    return call(
        forcing_body,
        (jax.ShapeDtypeStruct(ocean.shape, BF), end, end),
        [arrived, slots.reshape(1, -1), ocean, index, *ready],
        untouched=range(4, 4 + len(ready)),
        scratch=[pltpu.VMEM((arrived.shape[0] * LANES // depth, channels, depth), BF)],
    )


def neighbour_block(source, b, local, weight):
    channels, width = source.shape[1:]
    window = source[pl.ds(b, 3)].reshape(3 * channels, width)
    picked = []
    for k in range(local.shape[0]):
        where = local[k : k + 1, :]
        got = jnp.dot(window, one_hot(where & (width - 1), width), preferred_element_type=F32)
        high = where >> 8
        picked.append(
            jnp.where(
                high == 0,
                got[0:channels],
                jnp.where(high == 1, got[channels : 2 * channels], got[2 * channels :]),
            ).astype(BF)
        )
    return jnp.dot(weight, jnp.concatenate(picked, axis=0), preferred_element_type=F32)


def own_positions(index_ref, b):
    return index_ref[:, b * HALO : (b + 1) * HALO] - b * HALO


def hide_block(hidden, at, values, b, local, weight_ref, inside=None):
    mixed = gelu(neighbour_block(values, b, local, weight_ref[...]))
    hidden[at] = (mixed if inside is None else mixed * inside).astype(BF)


def inner_body(
    wait, own_ref, index_ref, first_ref, second_ref, hidden_ref, out_ref, values, local
):
    wait(0, 1, 2, 3)
    taps = index_ref.shape[0]
    blocks = values.shape[0]
    for b in range(blocks):
        values[b] = own_ref[:, b * HALO : (b + 1) * HALO]
    for b in range(blocks - 2):
        local[b, 0:taps] = own_positions(index_ref, b + 1)

    def hide(b, carry):
        hide_block(hidden_ref, b, values, b, local[b, 0:taps], first_ref)
        return carry

    lax.fori_loop(0, blocks - 2, hide, 0)

    def finish(b, carry):
        mixed = neighbour_block(hidden_ref, b, local[b + 1, 0:taps], second_ref[...])
        lanes = pl.ds(pl.multiple_of(b * HALO, HALO), HALO)
        out_ref[:, lanes] = (values[b + 2].astype(F32) + mixed).astype(BF)
        return carry

    lax.fori_loop(0, blocks - 4, finish, 0)


def ocean_inner(own, index, first, second):
    channels, cells = own.shape
    blocks = cells // HALO
    return call(
        inner_body,
        (
            jax.ShapeDtypeStruct((blocks - 2, channels, HALO), BF),
            jax.ShapeDtypeStruct((channels, cells - 4 * HALO), BF),
        ),
        [own, index, first, second],
        scratch=[
            pltpu.VMEM((blocks, channels, HALO), BF),
            pltpu.VMEM((blocks - 2, 16, HALO), jnp.int32),
        ],
    )


def outer_body(
    wait, own_ref, inner_ref, done_ref, before_ref, after_ref, index_ref, first_ref, second_ref,
    out_ref, values, hidden, local,
):
    width = HALO
    both = ("face", "tile")
    number, devices = lax.axis_index(both), lax.axis_size(both)
    edge_ref = [jnp.where(number > 0, 1.0, 0.0), jnp.where(number < devices - 1, 1.0, 0.0)]
    wait(*range(8))
    channels, blocks = own_ref.shape[0], own_ref.shape[1] // width
    taps = index_ref.shape[0]
    for b in range(2):
        lanes = slice(b * width, (b + 1) * width)
        values[b] = before_ref[0:channels, lanes]
        values[2 + b] = own_ref[:, lanes]
        values[4 + b] = own_ref[:, (blocks - 2 + b) * width : (blocks - 1 + b) * width]
        values[6 + b] = after_ref[0:channels, lanes]
        hidden[2 + b] = inner_ref[b]
        hidden[4 + b] = inner_ref[blocks - 4 + b]
    out_ref[:, 2 * width : (blocks - 2) * width] = done_ref[...]
    for i, b in enumerate((0, 1, blocks - 2, blocks - 1)):
        local[1 + i, 0:taps] = own_positions(index_ref, b)
    place = lax.broadcasted_iota(jnp.int32, (taps, width), 1)
    for i, ref in ((0, before_ref), (5, after_ref)):
        code = ref[channels:].astype(F32).astype(jnp.int32)[0:taps]
        local[i, 0:taps] = place + code[:, :width] + (code[:, width:] << 8)
    for at, first, i, inside in (
        (0, 0, 0, edge_ref[0]), (1, 1, 1, None), (6, 4, 4, None), (7, 5, 5, edge_ref[1])
    ):
        hide_block(hidden, at, values, first, local[i, 0:taps], first_ref, inside)
    for b, first, i in ((0, 0, 1), (1, 1, 2), (blocks - 2, 4, 3), (blocks - 1, 5, 4)):
        mixed = neighbour_block(hidden, first, local[i, 0:taps], second_ref[...])
        lanes = slice(b * width, (b + 1) * width)
        out_ref[:, lanes] = (own_ref[:, lanes].astype(F32) + mixed).astype(BF)


def flat_weight(weight):
    taps, out, inner = weight.shape
    return jnp.transpose(weight, (1, 0, 2)).reshape(out, taps * inner)


def ocean_outer(own, inner, done, before, after, index, first, second):
    channels = own.shape[0]
    return call(
        outer_body,
        jax.ShapeDtypeStruct(own.shape, BF),
        [own, inner, done, before, after, index, first, second],
        scratch=[
            pltpu.VMEM((8, channels, HALO), BF),
            pltpu.VMEM((8, channels, HALO), BF),
            pltpu.VMEM((6, 16, HALO), jnp.int32),
        ],
    )


def from_neighbours(low, high, axis, closed=False):
    count = lax.axis_size(axis)
    ends = count if closed else count - 1
    before = lax.ppermute(high, axis, [(i, (i + 1) % count) for i in range(ends)])
    after = lax.ppermute(low, axis, [((i + 1) % count, i) for i in range(ends)])
    return before, after


def shards(
    atmos,
    ocean,
    surface_heat_weight,
    air_conv_first_weight,
    air_conv_second_weight,
    marine_conv_first_weight,
    marine_conv_second_weight,
    marine_coupling_slot,
    coupling_air_cells,
    marine_neighbour_index,
):
    both = ("face", "tile")
    devices = lax.axis_size(both)
    faces, tiles = lax.axis_size("face"), lax.axis_size("tile")
    slot_space = coupling_air_cells.shape[1]
    capacity = slot_space // devices
    channels, rows, cols = atmos.shape

    def two_rows(first):
        return jnp.transpose(atmos[:, first : first + 2], (1, 0, 2)).reshape(2 * channels, cols)

    table, low, high = heat_table(
        ocean, marine_coupling_slot, coupling_air_cells, two_rows(0), two_rows(rows - 2),
        capacity, faces, tiles,
    )
    above, below = from_neighbours(low, high, "tile")
    heat = heat_slots(table, both)

    air = jnp.transpose(atmos, (1, 0, 2))
    field, first, second, before, live_cells = scatter_own(
        heat, coupling_air_cells, air_conv_first_weight, air_conv_second_weight, rows, cols
    )
    to_west, to_east = sides(air, above, below, low, field)
    west, east = from_neighbours(to_west, to_east, "face", closed=True)

    field = scatter_ends(field, heat, above, below)
    air_next, outgoing = atmosphere(
        air, above, below, west, east, to_west, to_east, field, heat, before, live_cells,
        surface_heat_weight, first, second,
    )
    air_out = jnp.transpose(air_next, (1, 0, 2))

    def by_device(blocks):
        many = LANES // capacity
        split = blocks.reshape(-1, channels, many, capacity)
        return jnp.transpose(split, (0, 2, 1, 3)).reshape(devices, channels, capacity)

    def by_lanes(blocks):
        many = LANES // capacity
        split = blocks.reshape(-1, many, channels, capacity)
        return jnp.transpose(split, (0, 2, 1, 3)).reshape(-1, channels, LANES)

    if capacity != LANES:
        outgoing = by_device(outgoing)
    arrived = lax.all_to_all(outgoing, both, split_axis=0, concat_axis=0, tiled=True)
    if capacity != LANES:
        arrived = by_lanes(arrived)

    first_mix = flat_weight(marine_conv_first_weight)
    second_mix = flat_weight(marine_conv_second_weight)
    ocean_start, head, tail = add_forcing(
        arrived, marine_coupling_slot, ocean, marine_neighbour_index, air_out, first_mix, second_mix
    )
    ocean_before, ocean_after = from_neighbours(head, tail, both)
    inner, done = ocean_inner(ocean_start, marine_neighbour_index, first_mix, second_mix)
    ocean_next = ocean_outer(
        ocean_start,
        inner,
        done,
        ocean_before,
        ocean_after,
        marine_neighbour_index,
        first_mix,
        second_mix,
    )
    return (air_out, ocean_next)


def solution(mesh):
    placed = (
        P(None, "tile", "face"),
        P(None, ("face", "tile")),
        P(),
        P(),
        P(),
        P(),
        P(),
        P(("face", "tile")),
        P(("face", "tile"), None),
        P(None, ("face", "tile")),
    )
    return jax.shard_map(
        shards,
        mesh=mesh,
        in_specs=placed,
        out_specs=(P(None, "tile", "face"), P(None, ("face", "tile"))),
        check_vma=False,
    )
```

```python
import jax
import jax.numpy as jnp
import numpy as np
from jax import lax
from jax.experimental import pallas as pl
from jax.experimental.pallas import tpu as pltpu
from jax.sharding import PartitionSpec as P

HALO = 256
LANES = 128
BF = jnp.bfloat16
F32 = jnp.float32
NEIGHBOURS = ((0, 0), (-1, 0), (1, 0), (0, -1), (0, 1), (-1, -1), (1, -1), (-1, 1), (1, 1))
VMEM_LIMIT = 20 * 1024 * 1024
VMEM_WHOLE = 60 * 1024 * 1024
VMEM_MOST = 62_200_000

VMEM = pl.BlockSpec(memory_space=pltpu.VMEM)
ANY = pl.BlockSpec(memory_space=pl.ANY)
HBM = pl.BlockSpec(memory_space=pltpu.HBM)


def call(body, outs, ins, scratch=(), parts=None, untouched=(), scalars=(), out_specs=None, limit=None):
    if limit is None:
        touched = [i for i in range(len(ins)) if i not in untouched]

        def plain(*refs):
            body(lambda *_: None, *(refs[i] for i in touched), *refs[len(ins) :])

        return pl.pallas_call(
            plain,
            out_shape=outs,
            in_specs=[VMEM if i in touched else ANY for i in range(len(ins))],
            out_specs=jax.tree.map(lambda _: VMEM, outs),
            scratch_shapes=list(scratch),
            compiler_params=pltpu.CompilerParams(vmem_limit_bytes=VMEM_LIMIT),
        )(*ins)
    parts = parts or {}
    held = [i for i in range(len(ins)) if i not in untouched]
    shapes = [
        tuple(len(range(*cut.indices(n))) for cut, n in zip(parts[i], ins[i].shape))
        if i in parts
        else ins[i].shape
        for i in held
    ]
    count = len(jax.tree.leaves(outs))

    def kernel(*refs):
        sources, refs = refs[: len(ins)], refs[len(ins) :]
        results, refs = refs[:count], refs[count:]
        copies, refs, done = refs[: len(held)], refs[len(held) : -1], refs[-1]
        moves = {}
        for k, i in enumerate(held):
            source = sources[i].at[parts[i]] if i in parts else sources[i]
            moves[i] = pltpu.make_async_copy(source, copies[k], done.at[k])
            moves[i].start()
        waiting = set(held)

        def wait(*which):
            for i in which:
                waiting.remove(i)
                moves[i].wait()

        body(wait, *copies, *results, *refs)
        assert not waiting

    return pl.pallas_call(
        kernel,
        out_shape=outs,
        in_specs=[ANY] * len(ins),
        out_specs=out_specs or jax.tree.map(lambda _: VMEM, outs),
        scratch_shapes=[
            (pltpu.SMEM if i in scalars else pltpu.VMEM)(shape, ins[i].dtype)
            for shape, i in zip(shapes, held)
        ]
        + list(scratch)
        + [pltpu.SemaphoreType.DMA((len(held),))],
        compiler_params=pltpu.CompilerParams(vmem_limit_bytes=limit),
    )(*ins)


def one_hot(index_row, size):
    places = lax.broadcasted_iota(jnp.int32, (size, index_row.shape[1]), 0)
    return jnp.where(places == index_row, 1.0, 0.0).astype(BF)


def nt_dot(a, b):
    return lax.dot_general(a, b, (((1,), (1,)), ((), ())), preferred_element_type=F32)


def gelu(x):
    inner = x * (0.7978845608028654 + 0.035677408136300125 * (x * x))
    return (0.5 * x) * (1.0 + jnp.tanh(inner))


def slot_values(heat_ref, slot_ref, rows):
    heat = heat_ref[0:16, :].astype(F32)[0:1]
    slot = slot_ref[...]
    places = lax.broadcasted_iota(jnp.int32, (rows, slot.shape[1]), 0)
    match = places == (slot >> 7)
    left = jnp.concatenate([jnp.where(match, heat, 0.0), jnp.where(match, 1.0, 0.0)], axis=0)
    return nt_dot(left.astype(BF), one_hot(slot & 127, LANES))


def or_inf(value, live):
    return jnp.where(live > 0.5, value, jnp.inf).astype(BF)


def fold(rows):
    return jnp.concatenate([rows[e : e + 8] for e in range(0, rows.shape[0], 8)], axis=1)


def unfold(block):
    cols = block.shape[1]
    return jnp.concatenate([block[:, at : at + LANES] for at in range(0, cols, LANES)], axis=0)


def unfolded(code):
    code = code.astype(F32)
    return jnp.concatenate([unfold(code[:8]), unfold(code[8:])], axis=0)


def payload_body(cell_ref, rows, payloads):
    count = cell_ref.shape[1] // LANES
    cells = jnp.concatenate(
        [cell_ref[:, e * LANES : (e + 1) * LANES] for e in range(count)], axis=0
    )
    code = coded(fold(cells))
    for row_ref, out_ref in zip(rows, payloads):
        size = row_ref.shape[1]
        out_ref[0:size] = row_ref[0]
        out_ref[size : 2 * size] = row_ref[1]
        out_ref[2 * size :] = code


def slot_table_body(
    wait, heat_ref, slot_ref, cell_ref, low_ref, high_ref, out_ref, low_out, high_out
):
    rows = out_ref.shape[0]
    table = slot_values(heat_ref, slot_ref, rows)
    out_ref[...] = or_inf(table[:rows], table[rows:])
    payload_body(cell_ref, (low_ref, high_ref), (low_out, high_out))


def spread_table_body(
    wait, heat_ref, slot_ref, cell_ref, low_ref, high_ref, spread_ref, out_ref, low_out, high_out
):
    wait(0, 1)
    count, rows = spread_ref.shape
    table = slot_values(heat_ref, slot_ref, rows)
    pair = jnp.concatenate([table[:rows], table[rows:]], axis=1).astype(BF)
    wait(2, 3, 4, 5)
    spread = jnp.dot(spread_ref[...], pair, preferred_element_type=F32)
    out_ref[...] = or_inf(spread[:, :LANES], spread[:, LANES:]).reshape(out_ref.shape)
    payload_body(cell_ref, (low_ref, high_ref), (low_out, high_out))


def neighbourhoods(faces, tiles):
    around = np.full((faces * tiles, 16), -1)
    for f in range(faces):
        for t in range(tiles):
            for n, (dr, dc) in enumerate(NEIGHBOURS):
                if 0 <= t + dr < tiles:
                    around[f * tiles + t, n] = (f + dc) % faces * tiles + t + dr
    return around


def heat_table(ocean, slots, cells, air, capacity, faces, tiles):
    devices = faces * tiles
    around = neighbourhoods(faces, tiles)
    rows, channels, cols = air.shape
    ins = [ocean, slots.reshape(1, -1), cells]
    payload = jax.ShapeDtypeStruct((2 * channels + 16, cols), BF)
    every = slice(None)
    if capacity == LANES:
        spread = (around.reshape(-1, 1) == np.arange(devices)).astype(np.float32)
        return call(
            spread_table_body,
            (jax.ShapeDtypeStruct((devices, 16, LANES), BF), payload, payload),
            ins + [air, air, jnp.asarray(spread, BF)],
            parts={
                0: (slice(0, 16), every),
                3: (slice(0, 2), every, every),
                4: (slice(rows - 2, rows), every, every),
            },
            limit=VMEM_WHOLE,
        )
    table = jax.ShapeDtypeStruct((devices * capacity // LANES, LANES), BF)
    table, low, high = call(
        slot_table_body, (table, payload, payload), ins + [air[:2], air[rows - 2 :]]
    )
    table = table.reshape(devices, capacity)
    table = jnp.where((around >= 0)[:, :, None], table[np.maximum(around, 0)], jnp.inf)
    return table.astype(BF), low, high


def heat_slots(table, both):
    capacity = table.shape[2]
    got = lax.all_to_all(table, both, split_axis=0, concat_axis=0, tiled=True)
    if capacity != LANES:
        got = jnp.transpose(got, (1, 0, 2)).reshape(16, -1, LANES)
        got = jnp.transpose(got, (1, 0, 2))
    return got


def row_and_column(cell, cols):
    return cell >> (cols.bit_length() - 1), cell & (cols - 1)


def for_chunks(count, many, body):
    def step(i, carry):
        for part in range(many):
            body(i * many + part)
        return carry

    lax.fori_loop(0, count // many, step, 0)


def lanes_at(e, width=LANES):
    return pl.ds(pl.multiple_of(e * width, width), width)


def one_hot_heat(value, live, high, size):
    match = lax.broadcasted_iota(jnp.int32, (size, LANES), 0) == jnp.where(live, high, -1)
    both = [jnp.where(match, value, 0.0), jnp.where(match, 1.0, 0.0)]
    return jnp.concatenate(both, axis=0).astype(BF)


def mean_heat(ref, first, count, rows_on, lanes):
    return ref[first : first + count, lanes] / jnp.maximum(
        ref[first + rows_on : first + rows_on + count, lanes], 1.0
    )


def scatter_own_body(
    wait, vals_ref, cell_ref, weight1_ref, weight2_ref,
    out_ref, first_ref, second_ref, before_ref, list_ref, left, right, prod, lives, packed, places,
):
    rows, cols = out_ref.shape
    blocks = cols // LANES
    span = rows * blocks
    chunks = vals_ref.shape[0]

    def chunk(e):
        lanes = lanes_at(e)
        value = vals_ref[e].astype(F32)[0:1]
        live = value < jnp.inf
        row, col = row_and_column(cell_ref[:, lanes], cols)
        high = (col >> 7) * rows + row
        left[:, lanes] = one_hot_heat(jnp.where(live, value, 0.0), live, high, span)
        right[:, lanes] = one_hot(col & 127, LANES)
        lives[pl.ds(e, 1), :] = jnp.where(live, 1.0, 0.0)

    for_chunks(chunks, 4, chunk)

    def triangle(size, above):
        row = lax.broadcasted_iota(jnp.int32, (size, size), 0)
        column = lax.broadcasted_iota(jnp.int32, (size, size), 1)
        return jnp.where(row < column if above else row > column, 1.0, 0.0).astype(BF)

    live = lives[...].astype(BF)
    in_row = jnp.dot(live, triangle(LANES, True), preferred_element_type=F32)
    rows_above = jnp.dot(triangle(chunks, False), live, preferred_element_type=F32)
    rows_above = jnp.sum(rows_above, axis=1, keepdims=True)
    before_ref[...] = (in_row + rows_above).astype(jnp.int32)
    tiles, width = list_ref.shape

    def pack(e):
        lanes = lanes_at(e)
        place = jnp.where(lives[pl.ds(e, 1), :] > 0.5, before_ref[pl.ds(e, 1), :], -1)
        cell = cell_ref[:, lanes]
        match = lax.broadcasted_iota(jnp.int32, (tiles, LANES), 0) == place >> 8
        parts = [jnp.where(match, part.astype(F32), 0.0) for part in (cell >> 7, cell & 127)]
        packed[:, lanes] = jnp.concatenate(parts, axis=0).astype(BF)
        places[:, lanes] = one_hot(place & (width - 1), width)

    for_chunks(chunks, 4, pack)
    cells = nt_dot(packed[...], places[...])
    list_ref[...] = (cells[:tiles] * 128.0 + cells[tiles:]).astype(jnp.int32)
    stack_weight(weight1_ref, first_ref)
    stack_weight(weight2_ref, second_ref)
    prod[...] = nt_dot(left[...], right[...])
    for b in range(blocks):
        out_ref[:, b * LANES : (b + 1) * LANES] = mean_heat(prod, b * rows, rows, span, slice(None))


def scatter_own(vals, cells, first, second, rows, cols):
    span = rows * (cols // LANES)
    channels = first.shape[2]
    slots = cells.size
    chunks, tiles = slots // LANES, slots // 256
    stacked = jax.ShapeDtypeStruct((6 * channels, 4 * channels), BF)
    return call(
        scatter_own_body,
        (
            jax.ShapeDtypeStruct((rows, cols), F32),
            stacked,
            stacked,
            jax.ShapeDtypeStruct((chunks, LANES), jnp.int32),
            jax.ShapeDtypeStruct((tiles, 256), jnp.int32),
        ),
        [vals, cells, first, second],
        scratch=[
            pltpu.VMEM((2 * span, slots), BF),
            pltpu.VMEM((LANES, slots), BF),
            pltpu.VMEM((2 * span, LANES), F32),
            pltpu.VMEM((chunks, LANES), F32),
            pltpu.VMEM((2 * tiles, slots), BF),
            pltpu.VMEM((256, slots), BF),
        ],
    )


def scatter_ends_body(
    wait, own_ref, vals_ref, above_ref, below_ref, out_ref, targets, left, right, prod
):
    rows, cols = own_ref.shape
    out_ref[2 : rows + 2, :] = own_ref[...]
    for n, (ref, dr) in enumerate(((above_ref, -1), (below_ref, 1))):
        code = unfolded(ref[ref.shape[0] - 16 :])
        row, col = row_and_column(decoded(code), cols)
        row = row - (rows - 2) if dr < 0 else row
        near = (row >= 0) & (row < 2)
        targets[2 * n] = jnp.where(near, 2 * (col >> 7) + row, -1)
        targets[2 * n + 1] = col & 127

    def chunk(e):
        lanes = lanes_at(e)
        values = vals_ref[e].astype(F32)
        for n in range(2):
            value = values[n + 1 : n + 2]
            live = value < jnp.inf
            high, low = (targets[2 * n + part, pl.ds(e, 1), :] for part in range(2))
            left[16 * n : 16 * (n + 1), lanes] = one_hot_heat(
                jnp.where(live, value, 0.0), live, high, 8
            )
            right[n * LANES : (n + 1) * LANES, lanes] = one_hot(low, LANES)

    for_chunks(vals_ref.shape[0], 4, chunk)
    prod[...] = nt_dot(left[...], right[...])
    for b in range(cols // LANES):
        to = slice(b * LANES, (b + 1) * LANES)
        out_ref[0:2, to] = mean_heat(prod, 2 * b, 2, 8, slice(0, LANES))
        out_ref[rows + 2 : rows + 4, to] = mean_heat(prod, 16 + 2 * b, 2, 8, slice(LANES, None))


def scatter_ends(own, vals, above, below):
    rows, cols = own.shape
    slots = vals.shape[0] * LANES
    return call(
        scatter_ends_body,
        jax.ShapeDtypeStruct((rows + 8, cols), F32),
        [own, vals, above, below],
        scratch=[
            pltpu.VMEM((4, slots // LANES, LANES), jnp.int32),
            pltpu.VMEM((32, slots), BF),
            pltpu.VMEM((2 * LANES, slots), BF),
            pltpu.VMEM((32, 2 * LANES), F32),
        ],
    )


def scatter_beside(vals_ref, west_ref, east_ref, targets, left, right, rows, cols):
    for ref, places in ((west_ref, (0, 2, 3)), (east_ref, (1, 4, 5))):
        first = ref.shape[0] - 3 * 64
        for part, place in enumerate(places):
            dr, dc = NEIGHBOURS[3 + place]
            cell = decoded(ref[first + 64 * part : first + 64 * (part + 1)])
            row, col = row_and_column(cell, cols)
            row = row + (rows * dr + 2)
            col = col if dc > 0 else col - (cols - 2)
            near = (row >= 0) & (row < rows + 4) & (col >= 0) & (col < 2)
            targets[place] = jnp.where(near, 2 * row + col, -1)

    def chunk(e):
        lanes = lanes_at(e)
        values = vals_ref[e].astype(F32)
        live = values < jnp.inf
        heats = [jnp.where(live, values, 0.0), jnp.where(live, 1.0, 0.0)]
        left[:, lanes] = jnp.concatenate(heats, axis=0).astype(BF)
        place = lax.broadcasted_iota(jnp.int32, (64, LANES), 0)
        halves = [jnp.zeros((64, LANES), F32)] * 2
        for k, (_, dc) in enumerate(NEIGHBOURS[3:]):
            side = 0 if dc < 0 else 1
            halves[side] = jnp.where(place == targets[k, pl.ds(e, 1), :], 1.0, halves[side])
        right[:, lanes] = jnp.concatenate(halves, axis=0).astype(BF)

    for_chunks(vals_ref.shape[0], 4, chunk)
    prod = nt_dot(left[...], right[...])
    lane = lax.broadcasted_iota(jnp.int32, (1, LANES), 1)
    place = lane & 63
    around = jnp.zeros((1, LANES), F32)
    for k, (dr, dc) in enumerate(NEIGHBOURS[3:]):
        first, last = {-1: (0, 4), 0: (4, 2 * rows + 4), 1: (2 * rows + 4, 2 * rows + 8)}[dr]
        here = (place >= first) & (place < last) & ((lane >= 64) == (dc > 0))
        mean = prod[k + 3 : k + 4] / jnp.maximum(prod[k + 19 : k + 20], 1.0)
        around = jnp.where(here, mean, around)
    return around


def end_columns(field):
    high, cols = field.shape
    row = lax.broadcasted_iota(jnp.int32, (high, LANES), 0)
    lane = lax.broadcasted_iota(jnp.int32, (high, LANES), 1)
    here = row < high - 4
    own = jnp.where(here & (lane == 2 * row), field[:, 0:1], 0.0) + jnp.where(
        here & (lane == 2 * row + 65), field[:, cols - 1 : cols], 0.0
    )
    return jnp.sum(own, axis=0, keepdims=True)


def coded(cells):
    return jnp.concatenate([cells >> 7, cells & 127], axis=0).astype(BF)


def decoded(code):
    half = code.shape[0] // 2
    return (code[:half].astype(F32) * 128.0 + code[half:].astype(F32)).astype(jnp.int32)


def side_body(wait, air_ref, above_ref, below_ref, own_ref, west_ref, east_ref):
    rows, channels, cols = air_ref.shape

    def column(i, lanes):
        if i < 2:
            return above_ref[i * channels : (i + 1) * channels, lanes]
        if i < rows + 2:
            return air_ref[i - 2, :, lanes]
        i = i - rows - 2
        return below_ref[i * channels : (i + 1) * channels, lanes]

    lane = lax.broadcasted_iota(jnp.int32, (channels, LANES), 1)
    for ref, lanes, shift, half in (
        (west_ref, slice(0, LANES), 0, 0),
        (east_ref, slice(cols - LANES, cols), 66, 32),
    ):
        total = jnp.zeros((channels, LANES), F32)
        for i in range(rows + 4):
            moved = pltpu.roll(column(i, lanes).astype(F32), (2 * i + shift) % LANES, 1)
            total = jnp.where(lane >> 1 == i + half, moved, total)
        ref[0:channels] = total.astype(BF)
        first = channels
        for payload in (own_ref, above_ref, below_ref):
            ref[first : first + 64] = unfolded(payload[2 * channels :]).astype(BF)
            first += 64


def sides(air, above, below, own, ready):
    out = jax.ShapeDtypeStruct((air.shape[1] + 3 * 64, LANES), BF)
    return call(side_body, (out, out), [air, above, below, own, ready], untouched=(4,))


def shifted(center, from_left, from_right, at_left, at_right, left_lane, right_lane):
    width = center.shape[1]
    left = pltpu.roll(from_left, 1, 1)
    right = pltpu.roll(from_right, width - 1, 1)
    lane = lax.broadcasted_iota(jnp.int32, at_left.shape, 1)
    first = jnp.where(lane == 0, pltpu.roll(at_left, LANES - left_lane, 1), left[:, :LANES])
    last = jnp.where(
        lane == LANES - 1, pltpu.roll(at_right, LANES - 1 - right_lane, 1), right[:, -LANES:]
    )
    left = jnp.concatenate([first, left[:, LANES:]], axis=1)
    right = jnp.concatenate([right[:, :-LANES], last], axis=1)
    return center + (left + right)


def stack_weight(weight_ref, out):
    taps, _, channels, _ = weight_ref.shape
    none = jnp.zeros((channels, channels), F32)
    for u in range(taps):
        rows = [weight_ref[p, u].astype(F32) for p in range(taps)]
        for k, line in enumerate((rows + [none], [none] + rows)):
            first = (k * taps + u) * channels
            out[first : first + channels] = jnp.concatenate(line, axis=1).astype(BF)


def atmosphere_body(
    wait, air_ref, above_ref, below_ref, west_ref, east_ref, own_west_ref, own_east_ref, field,
    vals_ref, before_ref, number_ref, list_ref, heat_weight_ref, first_ref, second_ref,
    next_out, send_ref,
    next_ref, out_done, start, hidden, edge1, edge2, targets, left, right, compact,
):
    rows, channels, cols = next_ref.shape
    taps = 3 * channels
    tile, tiles = lax.axis_index("tile"), lax.axis_size("tile")
    edge_ref = [jnp.where(tile > 0, 1.0, 0.0), jnp.where(tile < tiles - 1, 1.0, 0.0)]
    wait(3, 4, 8)
    around = scatter_beside(vals_ref, west_ref, east_ref, targets, left, right, rows, cols)
    wait(0, 1, 2, 5, 6, 7, 9, 10, 11, 12, 13, 14)
    lane = lax.broadcasted_iota(jnp.int32, (channels, LANES), 1)
    row = lax.broadcasted_iota(jnp.int32, (channels, channels), 0)
    same = row == lax.broadcasted_iota(jnp.int32, (channels, channels), 1)
    weights = jnp.sum(jnp.where(same, heat_weight_ref[...], 0.0), axis=1, keepdims=True)
    heat_weight = jnp.broadcast_to(weights, (channels, cols))

    beside = jnp.where(
        lane < 64, east_ref[0:channels].astype(F32), west_ref[0:channels].astype(F32)
    )
    beside = pltpu.roll(beside, 64, 1)
    own = own_west_ref[0:channels].astype(F32) + own_east_ref[0:channels].astype(F32)
    narrow = heat_weight[:, 0:LANES]
    beside = beside + narrow * around
    own = own + narrow * end_columns(field[...])

    def three_rows(x):
        return jnp.concatenate(
            [x, pltpu.roll(x, LANES - 2, 1), pltpu.roll(x, LANES - 4, 1)], axis=0
        ).astype(BF)

    plain = jnp.dot(
        first_ref[0:taps, 0:taps],
        jnp.concatenate([three_rows(beside), three_rows(own)], axis=1),
        preferred_element_type=F32,
    )

    def tap(u, of_own):
        return plain[u * channels : (u + 1) * channels, of_own * LANES : (of_own + 1) * LANES]

    def back(x):
        return pltpu.roll(x, LANES - 1, 1)

    edge1[0] = tap(0, 0)
    edge1[1] = tap(2, 0)
    at_left = tap(0, 0) + back(tap(1, 0)) + tap(2, 1)
    at_right = back(tap(0, 1)) + tap(1, 0) + back(tap(2, 0))
    place = lane & 63
    inside = jnp.where(
        place == 0, edge_ref[0], jnp.where(place == 2 * (rows + 1), edge_ref[1], 1.0)
    )
    hidden_beside = gelu(jnp.where(lane < 64, at_left, at_right)) * inside
    plain = jnp.dot(
        second_ref[0:taps, 0:taps], three_rows(hidden_beside), preferred_element_type=F32
    )
    edge2[0] = plain[0:channels]
    edge2[1] = plain[2 * channels : taps]

    for i in range(2):
        for ref, r in ((above_ref, i), (below_ref, rows + 2 + i)):
            x = ref[i * channels : (i + 1) * channels, 0:cols].astype(F32)
            start[r] = (x + heat_weight * field[r : r + 1, :]).astype(BF)

    def first_stage(j):
        for k in range(2):
            r = 2 * j + k
            x = air_ref[r].astype(F32) + heat_weight * field[pl.ds(r + 2, 1), :]
            start[r + 2] = x.astype(BF)

    def mixed(weight_ref, source, j):
        window = source[pl.ds(2 * j, 4)].reshape(4 * channels, cols)
        return jnp.dot(weight_ref[...], window, preferred_element_type=F32)

    def parts(product, k):
        return [
            product[(3 * k + u) * channels : (3 * k + u + 1) * channels] for u in (1, 0, 2)
        ]

    def second_stage(j):
        product = mixed(first_ref, start, j)
        for k in range(2):
            h = 2 * j + k
            inside = jnp.where(h == 0, edge_ref[0], jnp.where(h == rows + 1, edge_ref[1], 1.0))
            total = shifted(*parts(product, k), edge1[0], edge1[1], 2 * h + 1, 64 + 2 * h)
            hidden[h] = (gelu(total) * inside).astype(BF)

    def third_stage(j):
        product = mixed(second_ref, hidden, j)
        for k in range(2):
            r = 2 * j + k
            total = shifted(*parts(product, k), edge2[0], edge2[1], 2 * r, 64 + 2 * r)
            next_ref[r] = (start[r + 2].astype(F32) + total).astype(BF)

    def steps(first, last, *stages):
        def step(j):
            for stage, late in stages:
                stage(first + j - late)

        for_chunks(last - first, 1, step)

    half = rows // 2
    one, two, three = (first_stage, 0), (second_stage, 1), (third_stage, 3)
    steps(0, 1, one)
    steps(1, 3, two, one)
    steps(3, half, three, two, one)
    steps(half, half + 2, three, two)
    steps(half + 2, half + 3, three)


    copy = pltpu.make_async_copy(next_ref, next_out, out_done.at[0])
    copy.start()
    gather_live(next_ref, list_ref, number_ref, compact)
    spread_live(compact, before_ref, number_ref, send_ref)
    copy.wait()


def gather_live(next_ref, list_ref, number_ref, compact):
    rows, channels, cols = next_ref.shape
    shift = cols.bit_length() - 1
    tiles, width = list_ref.shape
    group, many = 6, 2
    compact[...] = jnp.zeros(compact.shape, BF)

    def pick(tile):
        cell = list_ref[pl.ds(tile, 1), :]
        low = one_hot(cell & (cols - 1), cols)
        high = (cell >> shift).astype(F32).astype(BF)
        total = jnp.zeros((channels, width), BF)
        for g in range(0, rows, group):
            block = next_ref[g : g + group].reshape(group * channels, cols)
            got = jnp.dot(block, low, preferred_element_type=F32).astype(BF)
            for r in range(group):
                here = high == jnp.asarray(g + r, BF)
                total = jnp.where(here, got[r * channels : (r + 1) * channels], total)
        compact[tile] = total

    def step(i, carry):
        for part in range(many):
            pick(i * many + part)
        return carry

    last = number_ref[number_ref.shape[0] - 1, number_ref.shape[1] - 1] + 1
    tiles_live = (last + (width - 1)) >> 8
    lax.fori_loop(0, tiles_live >> 1, step, 0)

    @pl.when((tiles_live & 1) == 1)
    def _():
        pick(tiles_live - 1)


def spread_live(compact, before_ref, number_ref, send_ref):
    _, channels, width = compact.shape

    def spread(i):
        place = jnp.concatenate(
            [before_ref[pl.ds(2 * i, 1), :], before_ref[pl.ds(2 * i + 1, 1), :]], axis=1
        )
        first = number_ref[2 * i, 0] >> 8
        window = compact[pl.ds(first, 2)].reshape(2 * channels, width)
        got = jnp.dot(window, one_hot(place & (width - 1), width), preferred_element_type=F32)
        total = jnp.where(place >> 8 == first, got[:channels], got[channels:]).astype(BF)
        for part in range(width // LANES):
            send_ref[2 * i + part] = total[:, part * LANES : (part + 1) * LANES]

    for_chunks(send_ref.shape[0] * LANES // width, 4, spread)


def atmosphere(
    air, above, below, west, east, to_west, to_east, field, vals, before, cells, heat_weight,
    first, second,
):
    rows, channels, cols = air.shape
    slots = before.size
    tiles = cells.shape[0]
    return call(
        atmosphere_body,
        (
            jax.ShapeDtypeStruct((rows, channels, cols), BF),
            jax.ShapeDtypeStruct((slots // LANES, channels, LANES), BF),
        ),
        [
            air, above, below, west, east, to_west, to_east, field, vals, before, before, cells,
            heat_weight.reshape(1, -1), first, second,
        ],
        scalars=(10,),
        out_specs=(HBM, VMEM),
        limit=VMEM_MOST,
        scratch=[
            pltpu.VMEM((rows, channels, cols), BF),
            pltpu.SemaphoreType.DMA((1,)),
            pltpu.VMEM((rows + 4, channels, cols), BF),
            pltpu.VMEM((rows + 2, channels, cols), BF),
            pltpu.VMEM((2, channels, LANES), F32),
            pltpu.VMEM((2, channels, LANES), F32),
            pltpu.VMEM((6, slots // LANES, LANES), jnp.int32),
            pltpu.VMEM((32, slots), BF),
            pltpu.VMEM((LANES, slots), BF),
            pltpu.VMEM((tiles + 1, channels, 256), BF),
        ],
    )


def forcing_body(
    wait, arrived_ref, slot_ref, ocean_ref, index_ref, out_ref, head_ref, tail_ref, table
):
    groups, channels, depth = table.shape
    wait(0, 1, 2, 3)
    parts = depth // LANES
    for g in range(groups):
        for p in range(parts):
            table[g, :, p * LANES : (p + 1) * LANES] = arrived_ref[g * parts + p]
    shift = depth.bit_length() - 1
    width = 256

    def block(b):
        lanes = lanes_at(b, width)
        slot = slot_ref[:, lanes]
        low = one_hot(slot & (depth - 1), depth)
        high = slot >> shift
        got = jnp.dot(
            table[...].reshape(groups * channels, depth), low, preferred_element_type=F32
        )
        total = got[0:channels]
        for g in range(1, groups):
            total = jnp.where(high == g, got[g * channels : (g + 1) * channels], total)
        out_ref[:, lanes] = (ocean_ref[:, lanes].astype(F32) + total).astype(BF)

    channels, cells = ocean_ref.shape
    for_chunks(cells // width, 2, block)
    reach = 2 * HALO
    for ref, first, start in ((head_ref, 0, 0), (tail_ref, cells - reach, cells - HALO)):
        ref[0:channels] = out_ref[:, first : first + reach]
        index = index_ref[:, start : start + HALO]
        far = index - start - lax.broadcasted_iota(jnp.int32, index.shape, 1)
        rest = jnp.zeros((ref.shape[0] - channels - index.shape[0], reach), F32)
        code = jnp.concatenate([far & (HALO - 1), far >> 8], axis=1).astype(F32)
        ref[channels:] = jnp.concatenate([code, rest], axis=0).astype(BF)


def add_forcing(arrived, slots, ocean, index, *ready):
    channels = ocean.shape[0]
    depth = 512
    end = jax.ShapeDtypeStruct((channels + 16, 2 * HALO), BF)
    return call(
        forcing_body,
        (jax.ShapeDtypeStruct(ocean.shape, BF), end, end),
        [arrived, slots.reshape(1, -1), ocean, index, *ready],
        untouched=range(4, 4 + len(ready)),
        scratch=[pltpu.VMEM((arrived.shape[0] * LANES // depth, channels, depth), BF)],
    )


def neighbour_block(source, b, local, weight):
    channels, width = source.shape[1:]
    window = source[pl.ds(b, 3)].reshape(3 * channels, width)
    picked = []
    for k in range(local.shape[0]):
        where = local[k : k + 1, :]
        got = jnp.dot(window, one_hot(where & (width - 1), width), preferred_element_type=F32)
        high = where >> 8
        picked.append(
            jnp.where(
                high == 0,
                got[0:channels],
                jnp.where(high == 1, got[channels : 2 * channels], got[2 * channels :]),
            ).astype(BF)
        )
    return jnp.dot(weight, jnp.concatenate(picked, axis=0), preferred_element_type=F32)


def own_positions(index_ref, b):
    return index_ref[:, b * HALO : (b + 1) * HALO] - b * HALO


def hide_block(hidden, at, values, b, local, weight_ref, inside=None):
    mixed = gelu(neighbour_block(values, b, local, weight_ref[...]))
    hidden[at] = (mixed if inside is None else mixed * inside).astype(BF)


def inner_body(
    wait, own_ref, index_ref, first_ref, second_ref, hidden_ref, out_ref, values, local
):
    wait(0, 1, 2, 3)
    taps = index_ref.shape[0]
    blocks = values.shape[0]
    for b in range(blocks):
        values[b] = own_ref[:, b * HALO : (b + 1) * HALO]
    for b in range(blocks - 2):
        local[b, 0:taps] = own_positions(index_ref, b + 1)

    def hide(b):
        hide_block(hidden_ref, b, values, b, local[b, 0:taps], first_ref)

    for_chunks(blocks - 2, 2, hide)

    def finish(b):
        mixed = neighbour_block(hidden_ref, b, local[b + 1, 0:taps], second_ref[...])
        out_ref[:, lanes_at(b, HALO)] = (values[b + 2].astype(F32) + mixed).astype(BF)

    for_chunks(blocks - 4, 2, finish)


def ocean_inner(own, index, first, second):
    channels, cells = own.shape
    blocks = cells // HALO
    return call(
        inner_body,
        (
            jax.ShapeDtypeStruct((blocks - 2, channels, HALO), BF),
            jax.ShapeDtypeStruct((channels, cells - 4 * HALO), BF),
        ),
        [own, index, first, second],
        scratch=[
            pltpu.VMEM((blocks, channels, HALO), BF),
            pltpu.VMEM((blocks - 2, 16, HALO), jnp.int32),
        ],
    )


def outer_body(
    wait, own_ref, inner_ref, done_ref, before_ref, after_ref, index_ref, first_ref, second_ref,
    out_ref, values, hidden, local,
):
    width = HALO
    both = ("face", "tile")
    number, devices = lax.axis_index(both), lax.axis_size(both)
    edge_ref = [jnp.where(number > 0, 1.0, 0.0), jnp.where(number < devices - 1, 1.0, 0.0)]
    wait(*range(8))
    channels, blocks = own_ref.shape[0], own_ref.shape[1] // width
    taps = index_ref.shape[0]
    for b in range(2):
        lanes = slice(b * width, (b + 1) * width)
        values[b] = before_ref[0:channels, lanes]
        values[2 + b] = own_ref[:, lanes]
        values[4 + b] = own_ref[:, (blocks - 2 + b) * width : (blocks - 1 + b) * width]
        values[6 + b] = after_ref[0:channels, lanes]
        hidden[2 + b] = inner_ref[b]
        hidden[4 + b] = inner_ref[blocks - 4 + b]
    out_ref[:, 2 * width : (blocks - 2) * width] = done_ref[...]
    for i, b in enumerate((0, 1, blocks - 2, blocks - 1)):
        local[1 + i, 0:taps] = own_positions(index_ref, b)
    place = lax.broadcasted_iota(jnp.int32, (taps, width), 1)
    for i, ref in ((0, before_ref), (5, after_ref)):
        code = ref[channels:].astype(F32).astype(jnp.int32)[0:taps]
        local[i, 0:taps] = place + code[:, :width] + (code[:, width:] << 8)
    for at, first, i, inside in (
        (0, 0, 0, edge_ref[0]), (1, 1, 1, None), (6, 4, 4, None), (7, 5, 5, edge_ref[1])
    ):
        hide_block(hidden, at, values, first, local[i, 0:taps], first_ref, inside)
    for b, first, i in ((0, 0, 1), (1, 1, 2), (blocks - 2, 4, 3), (blocks - 1, 5, 4)):
        mixed = neighbour_block(hidden, first, local[i, 0:taps], second_ref[...])
        lanes = slice(b * width, (b + 1) * width)
        out_ref[:, lanes] = (own_ref[:, lanes].astype(F32) + mixed).astype(BF)


def flat_weight(weight):
    taps, out, inner = weight.shape
    return jnp.transpose(weight, (1, 0, 2)).reshape(out, taps * inner)


def ocean_outer(own, inner, done, before, after, index, first, second):
    channels = own.shape[0]
    return call(
        outer_body,
        jax.ShapeDtypeStruct(own.shape, BF),
        [own, inner, done, before, after, index, first, second],
        scratch=[
            pltpu.VMEM((8, channels, HALO), BF),
            pltpu.VMEM((8, channels, HALO), BF),
            pltpu.VMEM((6, 16, HALO), jnp.int32),
        ],
    )


def from_neighbours(low, high, axis, closed=False):
    count = lax.axis_size(axis)
    ends = count if closed else count - 1
    before = lax.ppermute(high, axis, [(i, (i + 1) % count) for i in range(ends)])
    after = lax.ppermute(low, axis, [((i + 1) % count, i) for i in range(ends)])
    return before, after


def shards(
    atmos,
    ocean,
    surface_heat_weight,
    air_conv_first_weight,
    air_conv_second_weight,
    marine_conv_first_weight,
    marine_conv_second_weight,
    marine_coupling_slot,
    coupling_air_cells,
    marine_neighbour_index,
):
    both = ("face", "tile")
    devices = lax.axis_size(both)
    faces, tiles = lax.axis_size("face"), lax.axis_size("tile")
    slot_space = coupling_air_cells.shape[1]
    capacity = slot_space // devices
    channels, rows, cols = atmos.shape

    air = jnp.transpose(atmos, (1, 0, 2))

    table, low, high = heat_table(
        ocean, marine_coupling_slot, coupling_air_cells, air, capacity, faces, tiles
    )
    above, below = from_neighbours(low, high, "tile")
    heat = heat_slots(table, both)

    field, first, second, before, live_cells = scatter_own(
        heat, coupling_air_cells, air_conv_first_weight, air_conv_second_weight, rows, cols
    )
    to_west, to_east = sides(air, above, below, low, field)
    west, east = from_neighbours(to_west, to_east, "face", closed=True)

    field = scatter_ends(field, heat, above, below)
    air_next, outgoing = atmosphere(
        air, above, below, west, east, to_west, to_east, field, heat, before, live_cells,
        surface_heat_weight, first, second,
    )
    air_out = jnp.transpose(air_next, (1, 0, 2))

    def by_device(blocks):
        many = LANES // capacity
        split = blocks.reshape(-1, channels, many, capacity)
        return jnp.transpose(split, (0, 2, 1, 3)).reshape(devices, channels, capacity)

    def by_lanes(blocks):
        many = LANES // capacity
        split = blocks.reshape(-1, many, channels, capacity)
        return jnp.transpose(split, (0, 2, 1, 3)).reshape(-1, channels, LANES)

    if capacity != LANES:
        outgoing = by_device(outgoing)
    arrived = lax.all_to_all(outgoing, both, split_axis=0, concat_axis=0, tiled=True)
    if capacity != LANES:
        arrived = by_lanes(arrived)

    first_mix = flat_weight(marine_conv_first_weight)
    second_mix = flat_weight(marine_conv_second_weight)
    ocean_start, head, tail = add_forcing(
        arrived, marine_coupling_slot, ocean, marine_neighbour_index, air_out, first_mix, second_mix
    )
    ocean_before, ocean_after = from_neighbours(head, tail, both)
    inner, done = ocean_inner(ocean_start, marine_neighbour_index, first_mix, second_mix)
    ocean_next = ocean_outer(
        ocean_start,
        inner,
        done,
        ocean_before,
        ocean_after,
        marine_neighbour_index,
        first_mix,
        second_mix,
    )
    return (air_out, ocean_next)


def solution(mesh):
    placed = (
        P(None, "tile", "face"),
        P(None, ("face", "tile")),
        P(),
        P(),
        P(),
        P(),
        P(),
        P(("face", "tile")),
        P(("face", "tile"), None),
        P(None, ("face", "tile")),
    )
    return jax.shard_map(
        shards,
        mesh=mesh,
        in_specs=placed,
        out_specs=(P(None, "tile", "face"), P(None, ("face", "tile"))),
        check_vma=False,
    )
```

```python
import jax
import jax.numpy as jnp
import numpy as np
from jax import lax
from jax.experimental import pallas as pl
from jax.experimental.pallas import tpu as pltpu
from jax.sharding import PartitionSpec as P

HALO = 256
LANES = 128
BF = jnp.bfloat16
F32 = jnp.float32
NEIGHBOURS = ((0, 0), (-1, 0), (1, 0), (0, -1), (0, 1), (-1, -1), (1, -1), (-1, 1), (1, 1))
VMEM_LIMIT = 20 * 1024 * 1024
VMEM_WHOLE = 60 * 1024 * 1024
VMEM_MOST = 62_200_000

VMEM = pl.BlockSpec(memory_space=pltpu.VMEM)
ANY = pl.BlockSpec(memory_space=pl.ANY)
HBM = pl.BlockSpec(memory_space=pltpu.HBM)


def call(body, outs, ins, scratch=(), parts=None, untouched=(), scalars=(), out_specs=None, limit=None):
    if limit is None:
        touched = [i for i in range(len(ins)) if i not in untouched]

        def plain(*refs):
            body(lambda *_: None, *(refs[i] for i in touched), *refs[len(ins) :])

        return pl.pallas_call(
            plain,
            out_shape=outs,
            in_specs=[VMEM if i in touched else ANY for i in range(len(ins))],
            out_specs=jax.tree.map(lambda _: VMEM, outs),
            scratch_shapes=list(scratch),
            compiler_params=pltpu.CompilerParams(vmem_limit_bytes=VMEM_LIMIT),
        )(*ins)
    parts = parts or {}
    held = [i for i in range(len(ins)) if i not in untouched]
    shapes = [
        tuple(len(range(*cut.indices(n))) for cut, n in zip(parts[i], ins[i].shape))
        if i in parts
        else ins[i].shape
        for i in held
    ]
    count = len(jax.tree.leaves(outs))

    def kernel(*refs):
        sources, refs = refs[: len(ins)], refs[len(ins) :]
        results, refs = refs[:count], refs[count:]
        copies, refs, done = refs[: len(held)], refs[len(held) : -1], refs[-1]
        moves = {}
        for k, i in enumerate(held):
            source = sources[i].at[parts[i]] if i in parts else sources[i]
            moves[i] = pltpu.make_async_copy(source, copies[k], done.at[k])
            moves[i].start()
        waiting = set(held)

        def wait(*which):
            for i in which:
                waiting.remove(i)
                moves[i].wait()

        body(wait, *copies, *results, *refs)
        assert not waiting

    return pl.pallas_call(
        kernel,
        out_shape=outs,
        in_specs=[ANY] * len(ins),
        out_specs=out_specs or jax.tree.map(lambda _: VMEM, outs),
        scratch_shapes=[
            (pltpu.SMEM if i in scalars else pltpu.VMEM)(shape, ins[i].dtype)
            for shape, i in zip(shapes, held)
        ]
        + list(scratch)
        + [pltpu.SemaphoreType.DMA((len(held),))],
        compiler_params=pltpu.CompilerParams(vmem_limit_bytes=limit),
    )(*ins)


def one_hot(index_row, size):
    places = lax.broadcasted_iota(jnp.int32, (size, index_row.shape[1]), 0)
    return jnp.where(places == index_row, 1.0, 0.0).astype(BF)


def nt_dot(a, b):
    return lax.dot_general(a, b, (((1,), (1,)), ((), ())), preferred_element_type=F32)


def gelu(x):
    inner = x * (0.7978845608028654 + 0.035677408136300125 * (x * x))
    return (0.5 * x) * (1.0 + jnp.tanh(inner))


def slot_values(heat_ref, slot_ref, rows):
    heat = heat_ref[0:16, :].astype(F32)[0:1]
    slot = slot_ref[...]
    places = lax.broadcasted_iota(jnp.int32, (rows, slot.shape[1]), 0)
    match = places == (slot >> 7)
    left = jnp.concatenate([jnp.where(match, heat, 0.0), jnp.where(match, 1.0, 0.0)], axis=0)
    return nt_dot(left.astype(BF), one_hot(slot & 127, LANES))


def or_inf(value, live):
    return jnp.where(live > 0.5, value, jnp.inf).astype(BF)


def fold(rows):
    return jnp.concatenate([rows[e : e + 8] for e in range(0, rows.shape[0], 8)], axis=1)


def unfold(block):
    cols = block.shape[1]
    return jnp.concatenate([block[:, at : at + LANES] for at in range(0, cols, LANES)], axis=0)


def unfolded(code):
    code = code.astype(F32)
    return jnp.concatenate([unfold(code[:8]), unfold(code[8:])], axis=0)


def payload_body(cell_ref, rows, payloads):
    count = cell_ref.shape[1] // LANES
    cells = jnp.concatenate(
        [cell_ref[:, e * LANES : (e + 1) * LANES] for e in range(count)], axis=0
    )
    code = coded(fold(cells))
    for row_ref, out_ref in zip(rows, payloads):
        size = row_ref.shape[0]
        out_ref[0:size] = row_ref[...]
        out_ref[size:] = code


def slot_table_body(
    wait, heat_ref, slot_ref, cell_ref, low_ref, high_ref, out_ref, low_out, high_out
):
    rows = out_ref.shape[0]
    table = slot_values(heat_ref, slot_ref, rows)
    out_ref[...] = or_inf(table[:rows], table[rows:])
    payload_body(cell_ref, (low_ref, high_ref), (low_out, high_out))


def spread_table_body(
    wait, heat_ref, slot_ref, cell_ref, low_ref, high_ref, spread_ref, out_ref, low_out, high_out
):
    wait(0, 1)
    count, rows = spread_ref.shape
    table = slot_values(heat_ref, slot_ref, rows)
    pair = jnp.concatenate([table[:rows], table[rows:]], axis=1).astype(BF)
    wait(2, 3, 4, 5)
    spread = jnp.dot(spread_ref[...], pair, preferred_element_type=F32)
    out_ref[...] = or_inf(spread[:, :LANES], spread[:, LANES:]).reshape(out_ref.shape)
    payload_body(cell_ref, (low_ref, high_ref), (low_out, high_out))


def neighbourhoods(faces, tiles):
    around = np.full((faces * tiles, 16), -1)
    for f in range(faces):
        for t in range(tiles):
            for n, (dr, dc) in enumerate(NEIGHBOURS):
                if 0 <= t + dr < tiles:
                    around[f * tiles + t, n] = (f + dc) % faces * tiles + t + dr
    return around


def heat_table(ocean, slots, cells, low, high, capacity, faces, tiles):
    devices = faces * tiles
    around = neighbourhoods(faces, tiles)
    ins = [ocean, slots.reshape(1, -1), cells, low, high]
    payload = jax.ShapeDtypeStruct((low.shape[0] + 16, low.shape[1]), BF)
    if capacity == LANES:
        spread = (around.reshape(-1, 1) == np.arange(devices)).astype(np.float32)
        return call(
            spread_table_body,
            (jax.ShapeDtypeStruct((devices, 16, LANES), BF), payload, payload),
            ins + [jnp.asarray(spread, BF)],
            parts={0: (slice(0, 16), slice(None))},
            limit=VMEM_WHOLE,
        )
    rows = devices * capacity // LANES
    table, low, high = call(
        slot_table_body, (jax.ShapeDtypeStruct((rows, LANES), BF), payload, payload), ins
    )
    table = table.reshape(devices, capacity)
    table = jnp.where((around >= 0)[:, :, None], table[np.maximum(around, 0)], jnp.inf)
    return table.astype(BF), low, high


def heat_slots(table, both):
    capacity = table.shape[2]
    got = lax.all_to_all(table, both, split_axis=0, concat_axis=0, tiled=True)
    if capacity != LANES:
        got = jnp.transpose(got, (1, 0, 2)).reshape(16, -1, LANES)
        got = jnp.transpose(got, (1, 0, 2))
    return got


def row_and_column(cell, cols):
    return cell >> (cols.bit_length() - 1), cell & (cols - 1)


def for_chunks(count, many, body):
    def step(i, carry):
        for part in range(many):
            body(i * many + part)
        return carry

    lax.fori_loop(0, count // many, step, 0)


def lanes_at(e, width=LANES):
    return pl.ds(pl.multiple_of(e * width, width), width)


def one_hot_heat(value, live, high, size):
    match = lax.broadcasted_iota(jnp.int32, (size, LANES), 0) == jnp.where(live, high, -1)
    both = [jnp.where(match, value, 0.0), jnp.where(match, 1.0, 0.0)]
    return jnp.concatenate(both, axis=0).astype(BF)


def mean_heat(ref, first, count, rows_on, lanes):
    return ref[first : first + count, lanes] / jnp.maximum(
        ref[first + rows_on : first + rows_on + count, lanes], 1.0
    )


def scatter_own_body(
    wait, vals_ref, cell_ref, weight1_ref, weight2_ref,
    out_ref, first_ref, second_ref, before_ref, list_ref, left, right, prod, lives, packed, places,
):
    rows, cols = out_ref.shape
    blocks = cols // LANES
    span = rows * blocks
    chunks = vals_ref.shape[0]

    def chunk(e):
        lanes = lanes_at(e)
        value = vals_ref[e].astype(F32)[0:1]
        live = value < jnp.inf
        row, col = row_and_column(cell_ref[:, lanes], cols)
        high = (col >> 7) * rows + row
        left[:, lanes] = one_hot_heat(jnp.where(live, value, 0.0), live, high, span)
        right[:, lanes] = one_hot(col & 127, LANES)
        lives[pl.ds(e, 1), :] = jnp.where(live, 1.0, 0.0)

    for_chunks(chunks, 4, chunk)

    def triangle(size, above):
        row = lax.broadcasted_iota(jnp.int32, (size, size), 0)
        column = lax.broadcasted_iota(jnp.int32, (size, size), 1)
        return jnp.where(row < column if above else row > column, 1.0, 0.0).astype(BF)

    live = lives[...].astype(BF)
    in_row = jnp.dot(live, triangle(LANES, True), preferred_element_type=F32)
    rows_above = jnp.dot(triangle(chunks, False), live, preferred_element_type=F32)
    rows_above = jnp.sum(rows_above, axis=1, keepdims=True)
    before_ref[...] = (in_row + rows_above).astype(jnp.int32)
    tiles, width = list_ref.shape

    def pack(e):
        lanes = lanes_at(e)
        place = jnp.where(lives[pl.ds(e, 1), :] > 0.5, before_ref[pl.ds(e, 1), :], -1)
        cell = cell_ref[:, lanes]
        match = lax.broadcasted_iota(jnp.int32, (tiles, LANES), 0) == place >> 8
        parts = [jnp.where(match, part.astype(F32), 0.0) for part in (cell >> 7, cell & 127)]
        packed[:, lanes] = jnp.concatenate(parts, axis=0).astype(BF)
        places[:, lanes] = one_hot(place & (width - 1), width)

    for_chunks(chunks, 4, pack)
    cells = nt_dot(packed[...], places[...])
    list_ref[...] = (cells[:tiles] * 128.0 + cells[tiles:]).astype(jnp.int32)
    stack_weight(weight1_ref, first_ref)
    stack_weight(weight2_ref, second_ref)
    prod[...] = nt_dot(left[...], right[...])
    for b in range(blocks):
        out_ref[:, b * LANES : (b + 1) * LANES] = mean_heat(prod, b * rows, rows, span, slice(None))


def scatter_own(vals, cells, first, second, rows, cols):
    span = rows * (cols // LANES)
    channels = first.shape[2]
    slots = cells.size
    chunks, tiles = slots // LANES, slots // 256
    stacked = jax.ShapeDtypeStruct((6 * channels, 4 * channels), BF)
    return call(
        scatter_own_body,
        (
            jax.ShapeDtypeStruct((rows, cols), F32),
            stacked,
            stacked,
            jax.ShapeDtypeStruct((chunks, LANES), jnp.int32),
            jax.ShapeDtypeStruct((tiles, 256), jnp.int32),
        ),
        [vals, cells, first, second],
        scratch=[
            pltpu.VMEM((2 * span, slots), BF),
            pltpu.VMEM((LANES, slots), BF),
            pltpu.VMEM((2 * span, LANES), F32),
            pltpu.VMEM((chunks, LANES), F32),
            pltpu.VMEM((2 * tiles, slots), BF),
            pltpu.VMEM((256, slots), BF),
        ],
    )


def scatter_ends_body(
    wait, own_ref, vals_ref, above_ref, below_ref, out_ref, targets, left, right, prod
):
    rows, cols = own_ref.shape
    out_ref[2 : rows + 2, :] = own_ref[...]
    for n, (ref, dr) in enumerate(((above_ref, -1), (below_ref, 1))):
        code = unfolded(ref[ref.shape[0] - 16 :])
        row, col = row_and_column(decoded(code), cols)
        row = row - (rows - 2) if dr < 0 else row
        near = (row >= 0) & (row < 2)
        targets[2 * n] = jnp.where(near, 2 * (col >> 7) + row, -1)
        targets[2 * n + 1] = col & 127

    def chunk(e):
        lanes = lanes_at(e)
        values = vals_ref[e].astype(F32)
        for n in range(2):
            value = values[n + 1 : n + 2]
            live = value < jnp.inf
            high, low = (targets[2 * n + part, pl.ds(e, 1), :] for part in range(2))
            left[16 * n : 16 * (n + 1), lanes] = one_hot_heat(
                jnp.where(live, value, 0.0), live, high, 8
            )
            right[n * LANES : (n + 1) * LANES, lanes] = one_hot(low, LANES)

    for_chunks(vals_ref.shape[0], 4, chunk)
    prod[...] = nt_dot(left[...], right[...])
    for b in range(cols // LANES):
        to = slice(b * LANES, (b + 1) * LANES)
        out_ref[0:2, to] = mean_heat(prod, 2 * b, 2, 8, slice(0, LANES))
        out_ref[rows + 2 : rows + 4, to] = mean_heat(prod, 16 + 2 * b, 2, 8, slice(LANES, None))


def scatter_ends(own, vals, above, below):
    rows, cols = own.shape
    slots = vals.shape[0] * LANES
    return call(
        scatter_ends_body,
        jax.ShapeDtypeStruct((rows + 8, cols), F32),
        [own, vals, above, below],
        scratch=[
            pltpu.VMEM((4, slots // LANES, LANES), jnp.int32),
            pltpu.VMEM((32, slots), BF),
            pltpu.VMEM((2 * LANES, slots), BF),
            pltpu.VMEM((32, 2 * LANES), F32),
        ],
    )


def scatter_beside(vals_ref, west_ref, east_ref, targets, left, right, rows, cols):
    for ref, places in ((west_ref, (0, 2, 3)), (east_ref, (1, 4, 5))):
        first = ref.shape[0] - 3 * 64
        for part, place in enumerate(places):
            dr, dc = NEIGHBOURS[3 + place]
            cell = decoded(ref[first + 64 * part : first + 64 * (part + 1)])
            row, col = row_and_column(cell, cols)
            row = row + (rows * dr + 2)
            col = col if dc > 0 else col - (cols - 2)
            near = (row >= 0) & (row < rows + 4) & (col >= 0) & (col < 2)
            targets[place] = jnp.where(near, 2 * row + col, -1)

    def chunk(e):
        lanes = lanes_at(e)
        values = vals_ref[e].astype(F32)
        live = values < jnp.inf
        heats = [jnp.where(live, values, 0.0), jnp.where(live, 1.0, 0.0)]
        left[:, lanes] = jnp.concatenate(heats, axis=0).astype(BF)
        place = lax.broadcasted_iota(jnp.int32, (64, LANES), 0)
        halves = [jnp.zeros((64, LANES), F32)] * 2
        for k, (_, dc) in enumerate(NEIGHBOURS[3:]):
            side = 0 if dc < 0 else 1
            halves[side] = jnp.where(place == targets[k, pl.ds(e, 1), :], 1.0, halves[side])
        right[:, lanes] = jnp.concatenate(halves, axis=0).astype(BF)

    for_chunks(vals_ref.shape[0], 4, chunk)
    prod = nt_dot(left[...], right[...])
    lane = lax.broadcasted_iota(jnp.int32, (1, LANES), 1)
    place = lane & 63
    around = jnp.zeros((1, LANES), F32)
    for k, (dr, dc) in enumerate(NEIGHBOURS[3:]):
        first, last = {-1: (0, 4), 0: (4, 2 * rows + 4), 1: (2 * rows + 4, 2 * rows + 8)}[dr]
        here = (place >= first) & (place < last) & ((lane >= 64) == (dc > 0))
        mean = prod[k + 3 : k + 4] / jnp.maximum(prod[k + 19 : k + 20], 1.0)
        around = jnp.where(here, mean, around)
    return around


def end_columns(field):
    high, cols = field.shape
    row = lax.broadcasted_iota(jnp.int32, (high, LANES), 0)
    lane = lax.broadcasted_iota(jnp.int32, (high, LANES), 1)
    here = row < high - 4
    own = jnp.where(here & (lane == 2 * row), field[:, 0:1], 0.0) + jnp.where(
        here & (lane == 2 * row + 65), field[:, cols - 1 : cols], 0.0
    )
    return jnp.sum(own, axis=0, keepdims=True)


def coded(cells):
    return jnp.concatenate([cells >> 7, cells & 127], axis=0).astype(BF)


def decoded(code):
    half = code.shape[0] // 2
    return (code[:half].astype(F32) * 128.0 + code[half:].astype(F32)).astype(jnp.int32)


def side_body(wait, air_ref, above_ref, below_ref, own_ref, west_ref, east_ref):
    rows, channels, cols = air_ref.shape

    def column(i, lanes):
        if i < 2:
            return above_ref[i * channels : (i + 1) * channels, lanes]
        if i < rows + 2:
            return air_ref[i - 2, :, lanes]
        i = i - rows - 2
        return below_ref[i * channels : (i + 1) * channels, lanes]

    lane = lax.broadcasted_iota(jnp.int32, (channels, LANES), 1)
    for ref, lanes, shift, half in (
        (west_ref, slice(0, LANES), 0, 0),
        (east_ref, slice(cols - LANES, cols), 66, 32),
    ):
        total = jnp.zeros((channels, LANES), F32)
        for i in range(rows + 4):
            moved = pltpu.roll(column(i, lanes).astype(F32), (2 * i + shift) % LANES, 1)
            total = jnp.where(lane >> 1 == i + half, moved, total)
        ref[0:channels] = total.astype(BF)
        first = channels
        for payload in (own_ref, above_ref, below_ref):
            ref[first : first + 64] = unfolded(payload[2 * channels :]).astype(BF)
            first += 64


def sides(air, above, below, own, ready):
    out = jax.ShapeDtypeStruct((air.shape[1] + 3 * 64, LANES), BF)
    return call(side_body, (out, out), [air, above, below, own, ready], untouched=(4,))


def shifted(center, from_left, from_right, at_left, at_right, left_lane, right_lane):
    width = center.shape[1]
    left = pltpu.roll(from_left, 1, 1)
    right = pltpu.roll(from_right, width - 1, 1)
    lane = lax.broadcasted_iota(jnp.int32, at_left.shape, 1)
    first = jnp.where(lane == 0, pltpu.roll(at_left, LANES - left_lane, 1), left[:, :LANES])
    last = jnp.where(
        lane == LANES - 1, pltpu.roll(at_right, LANES - 1 - right_lane, 1), right[:, -LANES:]
    )
    left = jnp.concatenate([first, left[:, LANES:]], axis=1)
    right = jnp.concatenate([right[:, :-LANES], last], axis=1)
    return center + (left + right)


def stack_weight(weight_ref, out):
    taps, _, channels, _ = weight_ref.shape
    none = jnp.zeros((channels, channels), F32)
    for u in range(taps):
        rows = [weight_ref[p, u].astype(F32) for p in range(taps)]
        for k, line in enumerate((rows + [none], [none] + rows)):
            first = (k * taps + u) * channels
            out[first : first + channels] = jnp.concatenate(line, axis=1).astype(BF)


def atmosphere_body(
    wait, air_ref, above_ref, below_ref, west_ref, east_ref, own_west_ref, own_east_ref, field,
    vals_ref, before_ref, number_ref, list_ref, heat_weight_ref, first_ref, second_ref,
    next_out, send_ref,
    next_ref, out_done, start, hidden, edge1, edge2, targets, left, right, compact,
):
    rows, channels, cols = next_ref.shape
    taps = 3 * channels
    tile, tiles = lax.axis_index("tile"), lax.axis_size("tile")
    edge_ref = [jnp.where(tile > 0, 1.0, 0.0), jnp.where(tile < tiles - 1, 1.0, 0.0)]
    wait(3, 4, 8)
    around = scatter_beside(vals_ref, west_ref, east_ref, targets, left, right, rows, cols)
    wait(0, 1, 2, 5, 6, 7, 9, 10, 11, 12, 13, 14)
    lane = lax.broadcasted_iota(jnp.int32, (channels, LANES), 1)
    row = lax.broadcasted_iota(jnp.int32, (channels, channels), 0)
    same = row == lax.broadcasted_iota(jnp.int32, (channels, channels), 1)
    weights = jnp.sum(jnp.where(same, heat_weight_ref[...], 0.0), axis=1, keepdims=True)
    heat_weight = jnp.broadcast_to(weights, (channels, cols))

    beside = jnp.where(
        lane < 64, east_ref[0:channels].astype(F32), west_ref[0:channels].astype(F32)
    )
    beside = pltpu.roll(beside, 64, 1)
    own = own_west_ref[0:channels].astype(F32) + own_east_ref[0:channels].astype(F32)
    narrow = heat_weight[:, 0:LANES]
    beside = beside + narrow * around
    own = own + narrow * end_columns(field[...])

    def three_rows(x):
        return jnp.concatenate(
            [x, pltpu.roll(x, LANES - 2, 1), pltpu.roll(x, LANES - 4, 1)], axis=0
        ).astype(BF)

    plain = jnp.dot(
        first_ref[0:taps, 0:taps],
        jnp.concatenate([three_rows(beside), three_rows(own)], axis=1),
        preferred_element_type=F32,
    )

    def tap(u, of_own):
        return plain[u * channels : (u + 1) * channels, of_own * LANES : (of_own + 1) * LANES]

    def back(x):
        return pltpu.roll(x, LANES - 1, 1)

    edge1[0] = tap(0, 0)
    edge1[1] = tap(2, 0)
    at_left = tap(0, 0) + back(tap(1, 0)) + tap(2, 1)
    at_right = back(tap(0, 1)) + tap(1, 0) + back(tap(2, 0))
    place = lane & 63
    inside = jnp.where(
        place == 0, edge_ref[0], jnp.where(place == 2 * (rows + 1), edge_ref[1], 1.0)
    )
    hidden_beside = gelu(jnp.where(lane < 64, at_left, at_right)) * inside
    plain = jnp.dot(
        second_ref[0:taps, 0:taps], three_rows(hidden_beside), preferred_element_type=F32
    )
    edge2[0] = plain[0:channels]
    edge2[1] = plain[2 * channels : taps]

    for i in range(2):
        for ref, r in ((above_ref, i), (below_ref, rows + 2 + i)):
            x = ref[i * channels : (i + 1) * channels, 0:cols].astype(F32)
            start[r] = (x + heat_weight * field[r : r + 1, :]).astype(BF)

    def first_stage(j):
        for k in range(2):
            r = 2 * j + k
            x = air_ref[r].astype(F32) + heat_weight * field[pl.ds(r + 2, 1), :]
            start[r + 2] = x.astype(BF)

    def mixed(weight_ref, source, j):
        window = source[pl.ds(2 * j, 4)].reshape(4 * channels, cols)
        return jnp.dot(weight_ref[...], window, preferred_element_type=F32)

    def parts(product, k):
        return [
            product[(3 * k + u) * channels : (3 * k + u + 1) * channels] for u in (1, 0, 2)
        ]

    def second_stage(j):
        product = mixed(first_ref, start, j)
        for k in range(2):
            h = 2 * j + k
            inside = jnp.where(h == 0, edge_ref[0], jnp.where(h == rows + 1, edge_ref[1], 1.0))
            total = shifted(*parts(product, k), edge1[0], edge1[1], 2 * h + 1, 64 + 2 * h)
            hidden[h] = (gelu(total) * inside).astype(BF)

    def third_stage(j):
        product = mixed(second_ref, hidden, j)
        for k in range(2):
            r = 2 * j + k
            total = shifted(*parts(product, k), edge2[0], edge2[1], 2 * r, 64 + 2 * r)
            next_ref[r] = (start[r + 2].astype(F32) + total).astype(BF)

    def steps(first, last, *stages):
        def step(j):
            for stage, late in stages:
                stage(first + j - late)

        for_chunks(last - first, 1, step)

    half = rows // 2
    one, two, three = (first_stage, 0), (second_stage, 1), (third_stage, 3)
    steps(0, 1, one)
    steps(1, 3, two, one)
    steps(3, half, three, two, one)
    steps(half, half + 2, three, two)
    steps(half + 2, half + 3, three)


    copy = pltpu.make_async_copy(next_ref, next_out, out_done.at[0])
    copy.start()
    gather_live(next_ref, list_ref, number_ref, compact)
    spread_live(compact, before_ref, number_ref, send_ref)
    copy.wait()


def gather_live(next_ref, list_ref, number_ref, compact):
    rows, channels, cols = next_ref.shape
    shift = cols.bit_length() - 1
    tiles, width = list_ref.shape
    group, many = 6, 2
    compact[...] = jnp.zeros(compact.shape, BF)

    def pick(tile):
        cell = list_ref[pl.ds(tile, 1), :]
        low = one_hot(cell & (cols - 1), cols)
        high = (cell >> shift).astype(F32).astype(BF)
        total = jnp.zeros((channels, width), BF)
        for g in range(0, rows, group):
            block = next_ref[g : g + group].reshape(group * channels, cols)
            got = jnp.dot(block, low, preferred_element_type=F32).astype(BF)
            for r in range(group):
                here = high == jnp.asarray(g + r, BF)
                total = jnp.where(here, got[r * channels : (r + 1) * channels], total)
        compact[tile] = total

    def step(i, carry):
        for part in range(many):
            pick(i * many + part)
        return carry

    last = number_ref[number_ref.shape[0] - 1, number_ref.shape[1] - 1] + 1
    tiles_live = (last + (width - 1)) >> 8
    lax.fori_loop(0, tiles_live >> 1, step, 0)

    @pl.when((tiles_live & 1) == 1)
    def _():
        pick(tiles_live - 1)


def spread_live(compact, before_ref, number_ref, send_ref):
    _, channels, width = compact.shape

    def spread(i):
        place = jnp.concatenate(
            [before_ref[pl.ds(2 * i, 1), :], before_ref[pl.ds(2 * i + 1, 1), :]], axis=1
        )
        first = number_ref[2 * i, 0] >> 8
        window = compact[pl.ds(first, 2)].reshape(2 * channels, width)
        got = jnp.dot(window, one_hot(place & (width - 1), width), preferred_element_type=F32)
        total = jnp.where(place >> 8 == first, got[:channels], got[channels:]).astype(BF)
        for part in range(width // LANES):
            send_ref[2 * i + part] = total[:, part * LANES : (part + 1) * LANES]

    for_chunks(send_ref.shape[0] * LANES // width, 4, spread)


def atmosphere(
    air, above, below, west, east, to_west, to_east, field, vals, before, cells, heat_weight,
    first, second,
):
    rows, channels, cols = air.shape
    slots = before.size
    tiles = cells.shape[0]
    return call(
        atmosphere_body,
        (
            jax.ShapeDtypeStruct((rows, channels, cols), BF),
            jax.ShapeDtypeStruct((slots // LANES, channels, LANES), BF),
        ),
        [
            air, above, below, west, east, to_west, to_east, field, vals, before, before, cells,
            heat_weight.reshape(1, -1), first, second,
        ],
        scalars=(10,),
        out_specs=(HBM, VMEM),
        limit=VMEM_MOST,
        scratch=[
            pltpu.VMEM((rows, channels, cols), BF),
            pltpu.SemaphoreType.DMA((1,)),
            pltpu.VMEM((rows + 4, channels, cols), BF),
            pltpu.VMEM((rows + 2, channels, cols), BF),
            pltpu.VMEM((2, channels, LANES), F32),
            pltpu.VMEM((2, channels, LANES), F32),
            pltpu.VMEM((6, slots // LANES, LANES), jnp.int32),
            pltpu.VMEM((32, slots), BF),
            pltpu.VMEM((LANES, slots), BF),
            pltpu.VMEM((tiles + 1, channels, 256), BF),
        ],
    )


def forcing_body(
    wait, arrived_ref, slot_ref, ocean_ref, index_ref, out_ref, head_ref, tail_ref, table
):
    groups, channels, depth = table.shape
    wait(0, 1, 2, 3)
    parts = depth // LANES
    for g in range(groups):
        for p in range(parts):
            table[g, :, p * LANES : (p + 1) * LANES] = arrived_ref[g * parts + p]
    shift = depth.bit_length() - 1
    width = 256

    def block(b):
        lanes = lanes_at(b, width)
        slot = slot_ref[:, lanes]
        low = one_hot(slot & (depth - 1), depth)
        high = slot >> shift
        got = jnp.dot(
            table[...].reshape(groups * channels, depth), low, preferred_element_type=F32
        )
        total = got[0:channels]
        for g in range(1, groups):
            total = jnp.where(high == g, got[g * channels : (g + 1) * channels], total)
        out_ref[:, lanes] = (ocean_ref[:, lanes].astype(F32) + total).astype(BF)

    channels, cells = ocean_ref.shape
    for_chunks(cells // width, 2, block)
    reach = 2 * HALO
    for ref, first, start in ((head_ref, 0, 0), (tail_ref, cells - reach, cells - HALO)):
        ref[0:channels] = out_ref[:, first : first + reach]
        index = index_ref[:, start : start + HALO]
        far = index - start - lax.broadcasted_iota(jnp.int32, index.shape, 1)
        rest = jnp.zeros((ref.shape[0] - channels - index.shape[0], reach), F32)
        code = jnp.concatenate([far & (HALO - 1), far >> 8], axis=1).astype(F32)
        ref[channels:] = jnp.concatenate([code, rest], axis=0).astype(BF)


def add_forcing(arrived, slots, ocean, index, *ready):
    channels = ocean.shape[0]
    depth = 512
    end = jax.ShapeDtypeStruct((channels + 16, 2 * HALO), BF)
    return call(
        forcing_body,
        (jax.ShapeDtypeStruct(ocean.shape, BF), end, end),
        [arrived, slots.reshape(1, -1), ocean, index, *ready],
        untouched=range(4, 4 + len(ready)),
        scratch=[pltpu.VMEM((arrived.shape[0] * LANES // depth, channels, depth), BF)],
    )


def neighbour_block(source, b, local, weight):
    channels, width = source.shape[1:]
    window = source[pl.ds(b, 3)].reshape(3 * channels, width)
    picked = []
    for k in range(local.shape[0]):
        where = local[k : k + 1, :]
        got = jnp.dot(window, one_hot(where & (width - 1), width), preferred_element_type=F32)
        high = where >> 8
        picked.append(
            jnp.where(
                high == 0,
                got[0:channels],
                jnp.where(high == 1, got[channels : 2 * channels], got[2 * channels :]),
            ).astype(BF)
        )
    return jnp.dot(weight, jnp.concatenate(picked, axis=0), preferred_element_type=F32)


def own_positions(index_ref, b):
    return index_ref[:, b * HALO : (b + 1) * HALO] - b * HALO


def hide_block(hidden, at, values, b, local, weight_ref, inside=None):
    mixed = gelu(neighbour_block(values, b, local, weight_ref[...]))
    hidden[at] = (mixed if inside is None else mixed * inside).astype(BF)


def inner_body(
    wait, own_ref, index_ref, first_ref, second_ref, hidden_ref, out_ref, values, local
):
    wait(0, 1, 2, 3)
    taps = index_ref.shape[0]
    blocks = values.shape[0]
    for b in range(blocks):
        values[b] = own_ref[:, b * HALO : (b + 1) * HALO]
    for b in range(blocks - 2):
        local[b, 0:taps] = own_positions(index_ref, b + 1)

    def hide(b):
        hide_block(hidden_ref, b, values, b, local[b, 0:taps], first_ref)

    for_chunks(blocks - 2, 2, hide)

    def finish(b):
        mixed = neighbour_block(hidden_ref, b, local[b + 1, 0:taps], second_ref[...])
        out_ref[:, lanes_at(b, HALO)] = (values[b + 2].astype(F32) + mixed).astype(BF)

    for_chunks(blocks - 4, 2, finish)


def ocean_inner(own, index, first, second):
    channels, cells = own.shape
    blocks = cells // HALO
    return call(
        inner_body,
        (
            jax.ShapeDtypeStruct((blocks - 2, channels, HALO), BF),
            jax.ShapeDtypeStruct((channels, cells - 4 * HALO), BF),
        ),
        [own, index, first, second],
        scratch=[
            pltpu.VMEM((blocks, channels, HALO), BF),
            pltpu.VMEM((blocks - 2, 16, HALO), jnp.int32),
        ],
    )


def outer_body(
    wait, own_ref, inner_ref, done_ref, before_ref, after_ref, index_ref, first_ref, second_ref,
    out_ref, values, hidden, local,
):
    width = HALO
    both = ("face", "tile")
    number, devices = lax.axis_index(both), lax.axis_size(both)
    edge_ref = [jnp.where(number > 0, 1.0, 0.0), jnp.where(number < devices - 1, 1.0, 0.0)]
    wait(*range(8))
    channels, blocks = own_ref.shape[0], own_ref.shape[1] // width
    taps = index_ref.shape[0]
    for b in range(2):
        lanes = slice(b * width, (b + 1) * width)
        values[b] = before_ref[0:channels, lanes]
        values[2 + b] = own_ref[:, lanes]
        values[4 + b] = own_ref[:, (blocks - 2 + b) * width : (blocks - 1 + b) * width]
        values[6 + b] = after_ref[0:channels, lanes]
        hidden[2 + b] = inner_ref[b]
        hidden[4 + b] = inner_ref[blocks - 4 + b]
    out_ref[:, 2 * width : (blocks - 2) * width] = done_ref[...]
    for i, b in enumerate((0, 1, blocks - 2, blocks - 1)):
        local[1 + i, 0:taps] = own_positions(index_ref, b)
    place = lax.broadcasted_iota(jnp.int32, (taps, width), 1)
    for i, ref in ((0, before_ref), (5, after_ref)):
        code = ref[channels:].astype(F32).astype(jnp.int32)[0:taps]
        local[i, 0:taps] = place + code[:, :width] + (code[:, width:] << 8)
    for at, first, i, inside in (
        (0, 0, 0, edge_ref[0]), (1, 1, 1, None), (6, 4, 4, None), (7, 5, 5, edge_ref[1])
    ):
        hide_block(hidden, at, values, first, local[i, 0:taps], first_ref, inside)
    for b, first, i in ((0, 0, 1), (1, 1, 2), (blocks - 2, 4, 3), (blocks - 1, 5, 4)):
        mixed = neighbour_block(hidden, first, local[i, 0:taps], second_ref[...])
        lanes = slice(b * width, (b + 1) * width)
        out_ref[:, lanes] = (own_ref[:, lanes].astype(F32) + mixed).astype(BF)


def flat_weight(weight):
    taps, out, inner = weight.shape
    return jnp.transpose(weight, (1, 0, 2)).reshape(out, taps * inner)


def ocean_outer(own, inner, done, before, after, index, first, second):
    channels = own.shape[0]
    return call(
        outer_body,
        jax.ShapeDtypeStruct(own.shape, BF),
        [own, inner, done, before, after, index, first, second],
        scratch=[
            pltpu.VMEM((8, channels, HALO), BF),
            pltpu.VMEM((8, channels, HALO), BF),
            pltpu.VMEM((6, 16, HALO), jnp.int32),
        ],
    )


def from_neighbours(low, high, axis, closed=False):
    count = lax.axis_size(axis)
    ends = count if closed else count - 1
    before = lax.ppermute(high, axis, [(i, (i + 1) % count) for i in range(ends)])
    after = lax.ppermute(low, axis, [((i + 1) % count, i) for i in range(ends)])
    return before, after


def shards(
    atmos,
    ocean,
    surface_heat_weight,
    air_conv_first_weight,
    air_conv_second_weight,
    marine_conv_first_weight,
    marine_conv_second_weight,
    marine_coupling_slot,
    coupling_air_cells,
    marine_neighbour_index,
):
    both = ("face", "tile")
    devices = lax.axis_size(both)
    faces, tiles = lax.axis_size("face"), lax.axis_size("tile")
    slot_space = coupling_air_cells.shape[1]
    capacity = slot_space // devices
    channels, rows, cols = atmos.shape

    def two_rows(first):
        return jnp.transpose(atmos[:, first : first + 2], (1, 0, 2)).reshape(2 * channels, cols)

    table, low, high = heat_table(
        ocean, marine_coupling_slot, coupling_air_cells, two_rows(0), two_rows(rows - 2),
        capacity, faces, tiles,
    )
    above, below = from_neighbours(low, high, "tile")
    heat = heat_slots(table, both)

    air = jnp.transpose(atmos, (1, 0, 2))
    field, first, second, before, live_cells = scatter_own(
        heat, coupling_air_cells, air_conv_first_weight, air_conv_second_weight, rows, cols
    )
    to_west, to_east = sides(air, above, below, low, field)
    west, east = from_neighbours(to_west, to_east, "face", closed=True)

    field = scatter_ends(field, heat, above, below)
    air_next, outgoing = atmosphere(
        air, above, below, west, east, to_west, to_east, field, heat, before, live_cells,
        surface_heat_weight, first, second,
    )
    air_out = jnp.transpose(air_next, (1, 0, 2))

    def by_device(blocks):
        many = LANES // capacity
        split = blocks.reshape(-1, channels, many, capacity)
        return jnp.transpose(split, (0, 2, 1, 3)).reshape(devices, channels, capacity)

    def by_lanes(blocks):
        many = LANES // capacity
        split = blocks.reshape(-1, many, channels, capacity)
        return jnp.transpose(split, (0, 2, 1, 3)).reshape(-1, channels, LANES)

    if capacity != LANES:
        outgoing = by_device(outgoing)
    arrived = lax.all_to_all(outgoing, both, split_axis=0, concat_axis=0, tiled=True)
    if capacity != LANES:
        arrived = by_lanes(arrived)

    first_mix = flat_weight(marine_conv_first_weight)
    second_mix = flat_weight(marine_conv_second_weight)
    ocean_start, head, tail = add_forcing(
        arrived, marine_coupling_slot, ocean, marine_neighbour_index, air_out, first_mix, second_mix
    )
    ocean_before, ocean_after = from_neighbours(head, tail, both)
    inner, done = ocean_inner(ocean_start, marine_neighbour_index, first_mix, second_mix)
    ocean_next = ocean_outer(
        ocean_start,
        inner,
        done,
        ocean_before,
        ocean_after,
        marine_neighbour_index,
        first_mix,
        second_mix,
    )
    return (air_out, ocean_next)


def solution(mesh):
    placed = (
        P(None, "tile", "face"),
        P(None, ("face", "tile")),
        P(),
        P(),
        P(),
        P(),
        P(),
        P(("face", "tile")),
        P(("face", "tile"), None),
        P(None, ("face", "tile")),
    )
    return jax.shard_map(
        shards,
        mesh=mesh,
        in_specs=placed,
        out_specs=(P(None, "tile", "face"), P(None, ("face", "tile"))),
        check_vma=False,
    )
```

```python
import jax
import jax.numpy as jnp
import numpy as np
from jax import lax
from jax.experimental import pallas as pl
from jax.experimental.pallas import tpu as pltpu
from jax.sharding import PartitionSpec as P

HALO = 256
LANES = 128
BF = jnp.bfloat16
F32 = jnp.float32
NEIGHBOURS = ((0, 0), (-1, 0), (1, 0), (0, -1), (0, 1), (-1, -1), (1, -1), (-1, 1), (1, 1))
VMEM_LIMIT = 20 * 1024 * 1024
VMEM_WHOLE = 60 * 1024 * 1024
VMEM_MOST = 62_200_000

VMEM = pl.BlockSpec(memory_space=pltpu.VMEM)
ANY = pl.BlockSpec(memory_space=pl.ANY)
HBM = pl.BlockSpec(memory_space=pltpu.HBM)


def call(body, outs, ins, scratch=(), parts=None, untouched=(), scalars=(), out_specs=None, limit=None):
    if limit is None:
        touched = [i for i in range(len(ins)) if i not in untouched]

        def plain(*refs):
            body(lambda *_: None, *(refs[i] for i in touched), *refs[len(ins) :])

        return pl.pallas_call(
            plain,
            out_shape=outs,
            in_specs=[VMEM if i in touched else ANY for i in range(len(ins))],
            out_specs=jax.tree.map(lambda _: VMEM, outs),
            scratch_shapes=list(scratch),
            compiler_params=pltpu.CompilerParams(vmem_limit_bytes=VMEM_LIMIT),
        )(*ins)
    parts = parts or {}
    held = [i for i in range(len(ins)) if i not in untouched]
    shapes = [
        tuple(len(range(*cut.indices(n))) for cut, n in zip(parts[i], ins[i].shape))
        if i in parts
        else ins[i].shape
        for i in held
    ]
    count = len(jax.tree.leaves(outs))

    def kernel(*refs):
        sources, refs = refs[: len(ins)], refs[len(ins) :]
        results, refs = refs[:count], refs[count:]
        copies, refs, done = refs[: len(held)], refs[len(held) : -1], refs[-1]
        moves = {}
        for k, i in enumerate(held):
            source = sources[i].at[parts[i]] if i in parts else sources[i]
            moves[i] = pltpu.make_async_copy(source, copies[k], done.at[k])
            moves[i].start()
        waiting = set(held)

        def wait(*which):
            for i in which:
                waiting.remove(i)
                moves[i].wait()

        body(wait, *copies, *results, *refs)
        assert not waiting

    return pl.pallas_call(
        kernel,
        out_shape=outs,
        in_specs=[ANY] * len(ins),
        out_specs=out_specs or jax.tree.map(lambda _: VMEM, outs),
        scratch_shapes=[
            (pltpu.SMEM if i in scalars else pltpu.VMEM)(shape, ins[i].dtype)
            for shape, i in zip(shapes, held)
        ]
        + list(scratch)
        + [pltpu.SemaphoreType.DMA((len(held),))],
        compiler_params=pltpu.CompilerParams(vmem_limit_bytes=limit),
    )(*ins)


def one_hot(index_row, size):
    places = lax.broadcasted_iota(jnp.int32, (size, index_row.shape[1]), 0)
    return jnp.where(places == index_row, 1.0, 0.0).astype(BF)


def nt_dot(a, b):
    return lax.dot_general(a, b, (((1,), (1,)), ((), ())), preferred_element_type=F32)


def gelu(x):
    inner = x * (0.7978845608028654 + 0.035677408136300125 * (x * x))
    return (0.5 * x) * (1.0 + jnp.tanh(inner))


def slot_values(heat_ref, slot_ref, rows):
    heat = heat_ref[0:16, :].astype(F32)[0:1]
    slot = slot_ref[...]
    places = lax.broadcasted_iota(jnp.int32, (rows, slot.shape[1]), 0)
    match = places == (slot >> 7)
    left = jnp.concatenate([jnp.where(match, heat, 0.0), jnp.where(match, 1.0, 0.0)], axis=0)
    return nt_dot(left.astype(BF), one_hot(slot & 127, LANES))


def or_inf(value, live):
    return jnp.where(live > 0.5, value, jnp.inf).astype(BF)


def fold(rows):
    return jnp.concatenate([rows[e : e + 8] for e in range(0, rows.shape[0], 8)], axis=1)


def unfold(block):
    cols = block.shape[1]
    return jnp.concatenate([block[:, at : at + LANES] for at in range(0, cols, LANES)], axis=0)


def unfolded(code):
    code = code.astype(F32)
    return jnp.concatenate([unfold(code[:8]), unfold(code[8:])], axis=0)


def payload_body(cell_ref, rows, payloads):
    count = cell_ref.shape[1] // LANES
    cells = jnp.concatenate(
        [cell_ref[:, e * LANES : (e + 1) * LANES] for e in range(count)], axis=0
    )
    code = coded(fold(cells))
    for row_ref, out_ref in zip(rows, payloads):
        size = row_ref.shape[0]
        out_ref[0:size] = row_ref[...]
        out_ref[size:] = code


def slot_table_body(
    wait, heat_ref, slot_ref, cell_ref, low_ref, high_ref, out_ref, low_out, high_out
):
    rows = out_ref.shape[0]
    table = slot_values(heat_ref, slot_ref, rows)
    out_ref[...] = or_inf(table[:rows], table[rows:])
    payload_body(cell_ref, (low_ref, high_ref), (low_out, high_out))


def spread_table_body(
    wait, heat_ref, slot_ref, cell_ref, low_ref, high_ref, spread_ref, out_ref, low_out, high_out
):
    wait(0, 1)
    count, rows = spread_ref.shape
    table = slot_values(heat_ref, slot_ref, rows)
    pair = jnp.concatenate([table[:rows], table[rows:]], axis=1).astype(BF)
    wait(2, 3, 4, 5)
    spread = jnp.dot(spread_ref[...], pair, preferred_element_type=F32)
    out_ref[...] = or_inf(spread[:, :LANES], spread[:, LANES:]).reshape(out_ref.shape)
    payload_body(cell_ref, (low_ref, high_ref), (low_out, high_out))


def neighbourhoods(faces, tiles):
    around = np.full((faces * tiles, 16), -1)
    for f in range(faces):
        for t in range(tiles):
            for n, (dr, dc) in enumerate(NEIGHBOURS):
                if 0 <= t + dr < tiles:
                    around[f * tiles + t, n] = (f + dc) % faces * tiles + t + dr
    return around


def heat_table(ocean, slots, cells, low, high, capacity, faces, tiles):
    devices = faces * tiles
    around = neighbourhoods(faces, tiles)
    ins = [ocean, slots.reshape(1, -1), cells, low, high]
    payload = jax.ShapeDtypeStruct((low.shape[0] + 16, low.shape[1]), BF)
    if capacity == LANES:
        spread = (around.reshape(-1, 1) == np.arange(devices)).astype(np.float32)
        return call(
            spread_table_body,
            (jax.ShapeDtypeStruct((devices, 16, LANES), BF), payload, payload),
            ins + [jnp.asarray(spread, BF)],
            parts={0: (slice(0, 16), slice(None))},
            limit=VMEM_WHOLE,
        )
    rows = devices * capacity // LANES
    table, low, high = call(
        slot_table_body, (jax.ShapeDtypeStruct((rows, LANES), BF), payload, payload), ins
    )
    table = table.reshape(devices, capacity)
    table = jnp.where((around >= 0)[:, :, None], table[np.maximum(around, 0)], jnp.inf)
    return table.astype(BF), low, high


def heat_slots(table, both):
    capacity = table.shape[2]
    got = lax.all_to_all(table, both, split_axis=0, concat_axis=0, tiled=True)
    if capacity != LANES:
        got = jnp.transpose(got, (1, 0, 2)).reshape(16, -1, LANES)
        got = jnp.transpose(got, (1, 0, 2))
    return got


def row_and_column(cell, cols):
    return cell >> (cols.bit_length() - 1), cell & (cols - 1)


def for_chunks(count, many, body):
    def step(i, carry):
        for part in range(many):
            body(i * many + part)
        return carry

    lax.fori_loop(0, count // many, step, 0)


def lanes_at(e, width=LANES):
    return pl.ds(pl.multiple_of(e * width, width), width)


def one_hot_heat(value, live, high, size):
    match = lax.broadcasted_iota(jnp.int32, (size, LANES), 0) == jnp.where(live, high, -1)
    both = [jnp.where(match, value, 0.0), jnp.where(match, 1.0, 0.0)]
    return jnp.concatenate(both, axis=0).astype(BF)


def mean_heat(ref, first, count, rows_on, lanes):
    return ref[first : first + count, lanes] / jnp.maximum(
        ref[first + rows_on : first + rows_on + count, lanes], 1.0
    )


def scatter_own_body(
    wait, vals_ref, cell_ref, weight1_ref, weight2_ref,
    out_ref, first_ref, second_ref, before_ref, list_ref, left, right, prod, lives, packed, places,
):
    rows, cols = out_ref.shape
    blocks = cols // LANES
    span = rows * blocks
    chunks = vals_ref.shape[0]

    def chunk(e):
        lanes = lanes_at(e)
        value = vals_ref[e].astype(F32)[0:1]
        live = value < jnp.inf
        row, col = row_and_column(cell_ref[:, lanes], cols)
        high = (col >> 7) * rows + row
        left[:, lanes] = one_hot_heat(jnp.where(live, value, 0.0), live, high, span)
        right[:, lanes] = one_hot(col & 127, LANES)
        lives[pl.ds(e, 1), :] = jnp.where(live, 1.0, 0.0)

    for_chunks(chunks, 4, chunk)

    def triangle(size, above):
        row = lax.broadcasted_iota(jnp.int32, (size, size), 0)
        column = lax.broadcasted_iota(jnp.int32, (size, size), 1)
        return jnp.where(row < column if above else row > column, 1.0, 0.0).astype(BF)

    live = lives[...].astype(BF)
    in_row = jnp.dot(live, triangle(LANES, True), preferred_element_type=F32)
    rows_above = jnp.dot(triangle(chunks, False), live, preferred_element_type=F32)
    rows_above = jnp.sum(rows_above, axis=1, keepdims=True)
    before_ref[...] = (in_row + rows_above).astype(jnp.int32)
    tiles, width = list_ref.shape

    def pack(e):
        lanes = lanes_at(e)
        place = jnp.where(lives[pl.ds(e, 1), :] > 0.5, before_ref[pl.ds(e, 1), :], -1)
        cell = cell_ref[:, lanes]
        match = lax.broadcasted_iota(jnp.int32, (tiles, LANES), 0) == place >> 8
        parts = [jnp.where(match, part.astype(F32), 0.0) for part in (cell >> 7, cell & 127)]
        packed[:, lanes] = jnp.concatenate(parts, axis=0).astype(BF)
        places[:, lanes] = one_hot(place & (width - 1), width)

    for_chunks(chunks, 4, pack)
    cells = nt_dot(packed[...], places[...])
    list_ref[...] = (cells[:tiles] * 128.0 + cells[tiles:]).astype(jnp.int32)
    stack_weight(weight1_ref, first_ref)
    stack_weight(weight2_ref, second_ref)
    prod[...] = nt_dot(left[...], right[...])
    for b in range(blocks):
        out_ref[:, b * LANES : (b + 1) * LANES] = mean_heat(prod, b * rows, rows, span, slice(None))


def scatter_own(vals, cells, first, second, rows, cols):
    span = rows * (cols // LANES)
    channels = first.shape[2]
    slots = cells.size
    chunks, tiles = slots // LANES, slots // 256
    stacked = jax.ShapeDtypeStruct((6 * channels, 4 * channels), BF)
    return call(
        scatter_own_body,
        (
            jax.ShapeDtypeStruct((rows, cols), F32),
            stacked,
            stacked,
            jax.ShapeDtypeStruct((chunks, LANES), jnp.int32),
            jax.ShapeDtypeStruct((tiles, 256), jnp.int32),
        ),
        [vals, cells, first, second],
        scratch=[
            pltpu.VMEM((2 * span, slots), BF),
            pltpu.VMEM((LANES, slots), BF),
            pltpu.VMEM((2 * span, LANES), F32),
            pltpu.VMEM((chunks, LANES), F32),
            pltpu.VMEM((2 * tiles, slots), BF),
            pltpu.VMEM((256, slots), BF),
        ],
    )


def scatter_ends_body(
    wait, own_ref, vals_ref, above_ref, below_ref, out_ref, targets, left, right, prod
):
    rows, cols = own_ref.shape
    out_ref[2 : rows + 2, :] = own_ref[...]
    for n, (ref, dr) in enumerate(((above_ref, -1), (below_ref, 1))):
        code = unfolded(ref[ref.shape[0] - 16 :])
        row, col = row_and_column(decoded(code), cols)
        row = row - (rows - 2) if dr < 0 else row
        near = (row >= 0) & (row < 2)
        targets[2 * n] = jnp.where(near, 2 * (col >> 7) + row, -1)
        targets[2 * n + 1] = col & 127

    def chunk(e):
        lanes = lanes_at(e)
        values = vals_ref[e].astype(F32)
        for n in range(2):
            value = values[n + 1 : n + 2]
            live = value < jnp.inf
            high, low = (targets[2 * n + part, pl.ds(e, 1), :] for part in range(2))
            left[16 * n : 16 * (n + 1), lanes] = one_hot_heat(
                jnp.where(live, value, 0.0), live, high, 8
            )
            right[n * LANES : (n + 1) * LANES, lanes] = one_hot(low, LANES)

    for_chunks(vals_ref.shape[0], 4, chunk)
    prod[...] = nt_dot(left[...], right[...])
    for b in range(cols // LANES):
        to = slice(b * LANES, (b + 1) * LANES)
        out_ref[0:2, to] = mean_heat(prod, 2 * b, 2, 8, slice(0, LANES))
        out_ref[rows + 2 : rows + 4, to] = mean_heat(prod, 16 + 2 * b, 2, 8, slice(LANES, None))


def scatter_ends(own, vals, above, below):
    rows, cols = own.shape
    slots = vals.shape[0] * LANES
    return call(
        scatter_ends_body,
        jax.ShapeDtypeStruct((rows + 8, cols), F32),
        [own, vals, above, below],
        scratch=[
            pltpu.VMEM((4, slots // LANES, LANES), jnp.int32),
            pltpu.VMEM((32, slots), BF),
            pltpu.VMEM((2 * LANES, slots), BF),
            pltpu.VMEM((32, 2 * LANES), F32),
        ],
    )


def scatter_beside(vals_ref, west_ref, east_ref, targets, left, right, rows, cols):
    for ref, places in ((west_ref, (0, 2, 3)), (east_ref, (1, 4, 5))):
        first = ref.shape[0] - 3 * 64
        for part, place in enumerate(places):
            dr, dc = NEIGHBOURS[3 + place]
            cell = decoded(ref[first + 64 * part : first + 64 * (part + 1)])
            row, col = row_and_column(cell, cols)
            row = row + (rows * dr + 2)
            col = col if dc > 0 else col - (cols - 2)
            near = (row >= 0) & (row < rows + 4) & (col >= 0) & (col < 2)
            targets[place] = jnp.where(near, 2 * row + col, -1)

    def chunk(e):
        lanes = lanes_at(e)
        values = vals_ref[e].astype(F32)
        live = values < jnp.inf
        heats = [jnp.where(live, values, 0.0), jnp.where(live, 1.0, 0.0)]
        left[:, lanes] = jnp.concatenate(heats, axis=0).astype(BF)
        place = lax.broadcasted_iota(jnp.int32, (64, LANES), 0)
        halves = [jnp.zeros((64, LANES), F32)] * 2
        for k, (_, dc) in enumerate(NEIGHBOURS[3:]):
            side = 0 if dc < 0 else 1
            halves[side] = jnp.where(place == targets[k, pl.ds(e, 1), :], 1.0, halves[side])
        right[:, lanes] = jnp.concatenate(halves, axis=0).astype(BF)

    for_chunks(vals_ref.shape[0], 4, chunk)
    prod = nt_dot(left[...], right[...])
    lane = lax.broadcasted_iota(jnp.int32, (1, LANES), 1)
    place = lane & 63
    around = jnp.zeros((1, LANES), F32)
    for k, (dr, dc) in enumerate(NEIGHBOURS[3:]):
        first, last = {-1: (0, 4), 0: (4, 2 * rows + 4), 1: (2 * rows + 4, 2 * rows + 8)}[dr]
        here = (place >= first) & (place < last) & ((lane >= 64) == (dc > 0))
        mean = prod[k + 3 : k + 4] / jnp.maximum(prod[k + 19 : k + 20], 1.0)
        around = jnp.where(here, mean, around)
    return around


def end_columns(field):
    high, cols = field.shape
    row = lax.broadcasted_iota(jnp.int32, (high, LANES), 0)
    lane = lax.broadcasted_iota(jnp.int32, (high, LANES), 1)
    here = row < high - 4
    own = jnp.where(here & (lane == 2 * row), field[:, 0:1], 0.0) + jnp.where(
        here & (lane == 2 * row + 65), field[:, cols - 1 : cols], 0.0
    )
    return jnp.sum(own, axis=0, keepdims=True)


def coded(cells):
    return jnp.concatenate([cells >> 7, cells & 127], axis=0).astype(BF)


def decoded(code):
    half = code.shape[0] // 2
    return (code[:half].astype(F32) * 128.0 + code[half:].astype(F32)).astype(jnp.int32)


def side_body(wait, air_ref, above_ref, below_ref, own_ref, west_ref, east_ref):
    rows, channels, cols = air_ref.shape

    def column(i, lanes):
        if i < 2:
            return above_ref[i * channels : (i + 1) * channels, lanes]
        if i < rows + 2:
            return air_ref[i - 2, :, lanes]
        i = i - rows - 2
        return below_ref[i * channels : (i + 1) * channels, lanes]

    lane = lax.broadcasted_iota(jnp.int32, (channels, LANES), 1)
    for ref, lanes, shift, half in (
        (west_ref, slice(0, LANES), 0, 0),
        (east_ref, slice(cols - LANES, cols), 66, 32),
    ):
        total = jnp.zeros((channels, LANES), F32)
        for i in range(rows + 4):
            moved = pltpu.roll(column(i, lanes).astype(F32), (2 * i + shift) % LANES, 1)
            total = jnp.where(lane >> 1 == i + half, moved, total)
        ref[0:channels] = total.astype(BF)
        first = channels
        for payload in (own_ref, above_ref, below_ref):
            ref[first : first + 64] = unfolded(payload[2 * channels :]).astype(BF)
            first += 64


def sides(air, above, below, own, ready):
    out = jax.ShapeDtypeStruct((air.shape[1] + 3 * 64, LANES), BF)
    return call(side_body, (out, out), [air, above, below, own, ready], untouched=(4,))


def shifted(center, from_left, from_right, at_left, at_right, left_lane, right_lane):
    width = center.shape[1]
    left = pltpu.roll(from_left, 1, 1)
    right = pltpu.roll(from_right, width - 1, 1)
    lane = lax.broadcasted_iota(jnp.int32, at_left.shape, 1)
    first = jnp.where(lane == 0, pltpu.roll(at_left, LANES - left_lane, 1), left[:, :LANES])
    last = jnp.where(
        lane == LANES - 1, pltpu.roll(at_right, LANES - 1 - right_lane, 1), right[:, -LANES:]
    )
    left = jnp.concatenate([first, left[:, LANES:]], axis=1)
    right = jnp.concatenate([right[:, :-LANES], last], axis=1)
    return center + (left + right)


def stack_weight(weight_ref, out):
    taps, _, channels, _ = weight_ref.shape
    none = jnp.zeros((channels, channels), F32)
    for u in range(taps):
        rows = [weight_ref[p, u].astype(F32) for p in range(taps)]
        for k, line in enumerate((rows + [none], [none] + rows)):
            first = (k * taps + u) * channels
            out[first : first + channels] = jnp.concatenate(line, axis=1).astype(BF)


def atmosphere_body(
    wait, air_ref, above_ref, below_ref, west_ref, east_ref, own_west_ref, own_east_ref, field,
    vals_ref, before_ref, number_ref, list_ref, heat_weight_ref, first_ref, second_ref,
    next_out, send_ref,
    next_ref, out_done, start, hidden, edge1, edge2, targets, left, right, compact,
):
    rows, channels, cols = next_ref.shape
    taps = 3 * channels
    tile, tiles = lax.axis_index("tile"), lax.axis_size("tile")
    edge_ref = [jnp.where(tile > 0, 1.0, 0.0), jnp.where(tile < tiles - 1, 1.0, 0.0)]
    wait(3, 4, 8)
    around = scatter_beside(vals_ref, west_ref, east_ref, targets, left, right, rows, cols)
    wait(0, 1, 2, 5, 6, 7, 9, 10, 11, 12, 13, 14)
    lane = lax.broadcasted_iota(jnp.int32, (channels, LANES), 1)
    row = lax.broadcasted_iota(jnp.int32, (channels, channels), 0)
    same = row == lax.broadcasted_iota(jnp.int32, (channels, channels), 1)
    weights = jnp.sum(jnp.where(same, heat_weight_ref[...], 0.0), axis=1, keepdims=True)
    heat_weight = jnp.broadcast_to(weights, (channels, cols))

    beside = jnp.where(
        lane < 64, east_ref[0:channels].astype(F32), west_ref[0:channels].astype(F32)
    )
    beside = pltpu.roll(beside, 64, 1)
    own = own_west_ref[0:channels].astype(F32) + own_east_ref[0:channels].astype(F32)
    narrow = heat_weight[:, 0:LANES]
    beside = beside + narrow * around
    own = own + narrow * end_columns(field[...])

    def three_rows(x):
        return jnp.concatenate(
            [x, pltpu.roll(x, LANES - 2, 1), pltpu.roll(x, LANES - 4, 1)], axis=0
        ).astype(BF)

    plain = jnp.dot(
        first_ref[0:taps, 0:taps],
        jnp.concatenate([three_rows(beside), three_rows(own)], axis=1),
        preferred_element_type=F32,
    )

    def tap(u, of_own):
        return plain[u * channels : (u + 1) * channels, of_own * LANES : (of_own + 1) * LANES]

    def back(x):
        return pltpu.roll(x, LANES - 1, 1)

    edge1[0] = tap(0, 0)
    edge1[1] = tap(2, 0)
    at_left = tap(0, 0) + back(tap(1, 0)) + tap(2, 1)
    at_right = back(tap(0, 1)) + tap(1, 0) + back(tap(2, 0))
    place = lane & 63
    inside = jnp.where(
        place == 0, edge_ref[0], jnp.where(place == 2 * (rows + 1), edge_ref[1], 1.0)
    )
    hidden_beside = gelu(jnp.where(lane < 64, at_left, at_right)) * inside
    plain = jnp.dot(
        second_ref[0:taps, 0:taps], three_rows(hidden_beside), preferred_element_type=F32
    )
    edge2[0] = plain[0:channels]
    edge2[1] = plain[2 * channels : taps]

    for i in range(2):
        for ref, r in ((above_ref, i), (below_ref, rows + 2 + i)):
            x = ref[i * channels : (i + 1) * channels, 0:cols].astype(F32)
            start[r] = (x + heat_weight * field[r : r + 1, :]).astype(BF)

    def first_stage(j):
        for k in range(2):
            r = 2 * j + k
            x = air_ref[r].astype(F32) + heat_weight * field[pl.ds(r + 2, 1), :]
            start[r + 2] = x.astype(BF)

    def mixed(weight_ref, source, j):
        window = source[pl.ds(2 * j, 4)].reshape(4 * channels, cols)
        return jnp.dot(weight_ref[...], window, preferred_element_type=F32)

    def parts(product, k):
        return [
            product[(3 * k + u) * channels : (3 * k + u + 1) * channels] for u in (1, 0, 2)
        ]

    def second_stage(j):
        product = mixed(first_ref, start, j)
        for k in range(2):
            h = 2 * j + k
            inside = jnp.where(h == 0, edge_ref[0], jnp.where(h == rows + 1, edge_ref[1], 1.0))
            total = shifted(*parts(product, k), edge1[0], edge1[1], 2 * h + 1, 64 + 2 * h)
            hidden[h] = (gelu(total) * inside).astype(BF)

    def third_stage(j):
        product = mixed(second_ref, hidden, j)
        for k in range(2):
            r = 2 * j + k
            total = shifted(*parts(product, k), edge2[0], edge2[1], 2 * r, 64 + 2 * r)
            next_ref[r] = (start[r + 2].astype(F32) + total).astype(BF)

    def steps(first, last, *stages):
        def step(j):
            for stage, late in stages:
                stage(first + j - late)

        for_chunks(last - first, 1, step)

    half = rows // 2
    one, two, three = (first_stage, 0), (second_stage, 1), (third_stage, 3)
    steps(0, 1, one)
    steps(1, 3, two, one)
    steps(3, half, three, two, one)
    steps(half, half + 2, three, two)
    steps(half + 2, half + 3, three)


    copy = pltpu.make_async_copy(next_ref, next_out, out_done.at[0])
    copy.start()
    gather_live(next_ref, list_ref, number_ref, compact)
    spread_live(compact, before_ref, number_ref, send_ref)
    copy.wait()


def gather_live(next_ref, list_ref, number_ref, compact):
    rows, channels, cols = next_ref.shape
    shift = cols.bit_length() - 1
    tiles, width = list_ref.shape
    group, many = 6, 4
    compact[...] = jnp.zeros(compact.shape, BF)

    def pick(tile):
        cell = list_ref[pl.ds(tile, 1), :]
        low = one_hot(cell & (cols - 1), cols)
        high = (cell >> shift).astype(F32).astype(BF)
        total = jnp.zeros((channels, width), BF)
        for g in range(0, rows, group):
            block = next_ref[g : g + group].reshape(group * channels, cols)
            got = jnp.dot(block, low, preferred_element_type=F32).astype(BF)
            for r in range(group):
                here = high == jnp.asarray(g + r, BF)
                total = jnp.where(here, got[r * channels : (r + 1) * channels], total)
        compact[tile] = total

    def step(i, carry):
        for part in range(many):
            pick(i * many + part)
        return carry

    last = number_ref[number_ref.shape[0] - 1, number_ref.shape[1] - 1] + 1
    tiles_live = (last + (width - 1)) >> 8
    steps = tiles_live >> 2
    lax.fori_loop(0, steps, step, 0)

    def single(tile, carry):
        pick(tile)
        return carry

    lax.fori_loop(steps * many, tiles_live, single, 0)


def spread_live(compact, before_ref, number_ref, send_ref):
    _, channels, width = compact.shape

    def spread(i):
        place = jnp.concatenate(
            [before_ref[pl.ds(2 * i, 1), :], before_ref[pl.ds(2 * i + 1, 1), :]], axis=1
        )
        first = number_ref[2 * i, 0] >> 8
        window = compact[pl.ds(first, 2)].reshape(2 * channels, width)
        got = jnp.dot(window, one_hot(place & (width - 1), width), preferred_element_type=F32)
        total = jnp.where(place >> 8 == first, got[:channels], got[channels:]).astype(BF)
        for part in range(width // LANES):
            send_ref[2 * i + part] = total[:, part * LANES : (part + 1) * LANES]

    for_chunks(send_ref.shape[0] * LANES // width, 8, spread)


def atmosphere(
    air, above, below, west, east, to_west, to_east, field, vals, before, cells, heat_weight,
    first, second,
):
    rows, channels, cols = air.shape
    slots = before.size
    tiles = cells.shape[0]
    return call(
        atmosphere_body,
        (
            jax.ShapeDtypeStruct((rows, channels, cols), BF),
            jax.ShapeDtypeStruct((slots // LANES, channels, LANES), BF),
        ),
        [
            air, above, below, west, east, to_west, to_east, field, vals, before, before, cells,
            heat_weight.reshape(1, -1), first, second,
        ],
        scalars=(10,),
        out_specs=(HBM, VMEM),
        limit=VMEM_MOST,
        scratch=[
            pltpu.VMEM((rows, channels, cols), BF),
            pltpu.SemaphoreType.DMA((1,)),
            pltpu.VMEM((rows + 4, channels, cols), BF),
            pltpu.VMEM((rows + 2, channels, cols), BF),
            pltpu.VMEM((2, channels, LANES), F32),
            pltpu.VMEM((2, channels, LANES), F32),
            pltpu.VMEM((6, slots // LANES, LANES), jnp.int32),
            pltpu.VMEM((32, slots), BF),
            pltpu.VMEM((LANES, slots), BF),
            pltpu.VMEM((tiles + 1, channels, 256), BF),
        ],
    )


def forcing_body(
    wait, arrived_ref, slot_ref, ocean_ref, index_ref, out_ref, head_ref, tail_ref, table
):
    groups, channels, depth = table.shape
    wait(0, 1, 2, 3)
    parts = depth // LANES
    for g in range(groups):
        for p in range(parts):
            table[g, :, p * LANES : (p + 1) * LANES] = arrived_ref[g * parts + p]
    shift = depth.bit_length() - 1
    width = 256

    def block(b):
        lanes = lanes_at(b, width)
        slot = slot_ref[:, lanes]
        low = one_hot(slot & (depth - 1), depth)
        high = slot >> shift
        got = jnp.dot(
            table[...].reshape(groups * channels, depth), low, preferred_element_type=F32
        )
        total = got[0:channels]
        for g in range(1, groups):
            total = jnp.where(high == g, got[g * channels : (g + 1) * channels], total)
        out_ref[:, lanes] = (ocean_ref[:, lanes].astype(F32) + total).astype(BF)

    channels, cells = ocean_ref.shape
    for_chunks(cells // width, 4, block)
    reach = 2 * HALO
    for ref, first, start in ((head_ref, 0, 0), (tail_ref, cells - reach, cells - HALO)):
        ref[0:channels] = out_ref[:, first : first + reach]
        index = index_ref[:, start : start + HALO]
        far = index - start - lax.broadcasted_iota(jnp.int32, index.shape, 1)
        rest = jnp.zeros((ref.shape[0] - channels - index.shape[0], reach), F32)
        code = jnp.concatenate([far & (HALO - 1), far >> 8], axis=1).astype(F32)
        ref[channels:] = jnp.concatenate([code, rest], axis=0).astype(BF)


def add_forcing(arrived, slots, ocean, index, *ready):
    channels = ocean.shape[0]
    depth = 512
    end = jax.ShapeDtypeStruct((channels + 16, 2 * HALO), BF)
    return call(
        forcing_body,
        (jax.ShapeDtypeStruct(ocean.shape, BF), end, end),
        [arrived, slots.reshape(1, -1), ocean, index, *ready],
        untouched=range(4, 4 + len(ready)),
        scratch=[pltpu.VMEM((arrived.shape[0] * LANES // depth, channels, depth), BF)],
    )


def neighbour_block(source, b, local, weight):
    channels, width = source.shape[1:]
    window = source[pl.ds(b, 3)].reshape(3 * channels, width)
    picked = []
    for k in range(local.shape[0]):
        where = local[k : k + 1, :]
        got = jnp.dot(window, one_hot(where & (width - 1), width), preferred_element_type=F32)
        high = where >> 8
        picked.append(
            jnp.where(
                high == 0,
                got[0:channels],
                jnp.where(high == 1, got[channels : 2 * channels], got[2 * channels :]),
            ).astype(BF)
        )
    return jnp.dot(weight, jnp.concatenate(picked, axis=0), preferred_element_type=F32)


def own_positions(index_ref, b):
    return index_ref[:, b * HALO : (b + 1) * HALO] - b * HALO


def hide_block(hidden, at, values, b, local, weight_ref, inside=None):
    mixed = gelu(neighbour_block(values, b, local, weight_ref[...]))
    hidden[at] = (mixed if inside is None else mixed * inside).astype(BF)


def inner_body(
    wait, own_ref, index_ref, first_ref, second_ref, hidden_ref, out_ref, values, local
):
    wait(0, 1, 2, 3)
    taps = index_ref.shape[0]
    blocks = values.shape[0]
    for b in range(blocks):
        values[b] = own_ref[:, b * HALO : (b + 1) * HALO]
    for b in range(blocks - 2):
        local[b, 0:taps] = own_positions(index_ref, b + 1)

    def hide(b):
        hide_block(hidden_ref, b, values, b, local[b, 0:taps], first_ref)

    for_chunks(blocks - 2, 3, hide)

    def finish(b):
        mixed = neighbour_block(hidden_ref, b, local[b + 1, 0:taps], second_ref[...])
        out_ref[:, lanes_at(b, HALO)] = (values[b + 2].astype(F32) + mixed).astype(BF)

    for_chunks(blocks - 4, 4, finish)


def ocean_inner(own, index, first, second):
    channels, cells = own.shape
    blocks = cells // HALO
    return call(
        inner_body,
        (
            jax.ShapeDtypeStruct((blocks - 2, channels, HALO), BF),
            jax.ShapeDtypeStruct((channels, cells - 4 * HALO), BF),
        ),
        [own, index, first, second],
        scratch=[
            pltpu.VMEM((blocks, channels, HALO), BF),
            pltpu.VMEM((blocks - 2, 16, HALO), jnp.int32),
        ],
    )


def outer_body(
    wait, own_ref, inner_ref, done_ref, before_ref, after_ref, index_ref, first_ref, second_ref,
    out_ref, values, hidden, local,
):
    width = HALO
    both = ("face", "tile")
    number, devices = lax.axis_index(both), lax.axis_size(both)
    edge_ref = [jnp.where(number > 0, 1.0, 0.0), jnp.where(number < devices - 1, 1.0, 0.0)]
    wait(*range(8))
    channels, blocks = own_ref.shape[0], own_ref.shape[1] // width
    taps = index_ref.shape[0]
    for b in range(2):
        lanes = slice(b * width, (b + 1) * width)
        values[b] = before_ref[0:channels, lanes]
        values[2 + b] = own_ref[:, lanes]
        values[4 + b] = own_ref[:, (blocks - 2 + b) * width : (blocks - 1 + b) * width]
        values[6 + b] = after_ref[0:channels, lanes]
        hidden[2 + b] = inner_ref[b]
        hidden[4 + b] = inner_ref[blocks - 4 + b]
    out_ref[:, 2 * width : (blocks - 2) * width] = done_ref[...]
    for i, b in enumerate((0, 1, blocks - 2, blocks - 1)):
        local[1 + i, 0:taps] = own_positions(index_ref, b)
    place = lax.broadcasted_iota(jnp.int32, (taps, width), 1)
    for i, ref in ((0, before_ref), (5, after_ref)):
        code = ref[channels:].astype(F32).astype(jnp.int32)[0:taps]
        local[i, 0:taps] = place + code[:, :width] + (code[:, width:] << 8)
    for at, first, i, inside in (
        (0, 0, 0, edge_ref[0]), (1, 1, 1, None), (6, 4, 4, None), (7, 5, 5, edge_ref[1])
    ):
        hide_block(hidden, at, values, first, local[i, 0:taps], first_ref, inside)
    for b, first, i in ((0, 0, 1), (1, 1, 2), (blocks - 2, 4, 3), (blocks - 1, 5, 4)):
        mixed = neighbour_block(hidden, first, local[i, 0:taps], second_ref[...])
        lanes = slice(b * width, (b + 1) * width)
        out_ref[:, lanes] = (own_ref[:, lanes].astype(F32) + mixed).astype(BF)


def flat_weight(weight):
    taps, out, inner = weight.shape
    return jnp.transpose(weight, (1, 0, 2)).reshape(out, taps * inner)


def ocean_outer(own, inner, done, before, after, index, first, second):
    channels = own.shape[0]
    return call(
        outer_body,
        jax.ShapeDtypeStruct(own.shape, BF),
        [own, inner, done, before, after, index, first, second],
        scratch=[
            pltpu.VMEM((8, channels, HALO), BF),
            pltpu.VMEM((8, channels, HALO), BF),
            pltpu.VMEM((6, 16, HALO), jnp.int32),
        ],
    )


def from_neighbours(low, high, axis, closed=False):
    count = lax.axis_size(axis)
    ends = count if closed else count - 1
    before = lax.ppermute(high, axis, [(i, (i + 1) % count) for i in range(ends)])
    after = lax.ppermute(low, axis, [((i + 1) % count, i) for i in range(ends)])
    return before, after


def shards(
    atmos,
    ocean,
    surface_heat_weight,
    air_conv_first_weight,
    air_conv_second_weight,
    marine_conv_first_weight,
    marine_conv_second_weight,
    marine_coupling_slot,
    coupling_air_cells,
    marine_neighbour_index,
):
    both = ("face", "tile")
    devices = lax.axis_size(both)
    faces, tiles = lax.axis_size("face"), lax.axis_size("tile")
    slot_space = coupling_air_cells.shape[1]
    capacity = slot_space // devices
    channels, rows, cols = atmos.shape

    def two_rows(first):
        return jnp.transpose(atmos[:, first : first + 2], (1, 0, 2)).reshape(2 * channels, cols)

    table, low, high = heat_table(
        ocean, marine_coupling_slot, coupling_air_cells, two_rows(0), two_rows(rows - 2),
        capacity, faces, tiles,
    )
    above, below = from_neighbours(low, high, "tile")
    heat = heat_slots(table, both)

    air = jnp.transpose(atmos, (1, 0, 2))
    field, first, second, before, live_cells = scatter_own(
        heat, coupling_air_cells, air_conv_first_weight, air_conv_second_weight, rows, cols
    )
    to_west, to_east = sides(air, above, below, low, field)
    west, east = from_neighbours(to_west, to_east, "face", closed=True)

    field = scatter_ends(field, heat, above, below)
    air_next, outgoing = atmosphere(
        air, above, below, west, east, to_west, to_east, field, heat, before, live_cells,
        surface_heat_weight, first, second,
    )
    air_out = jnp.transpose(air_next, (1, 0, 2))

    def by_device(blocks):
        many = LANES // capacity
        split = blocks.reshape(-1, channels, many, capacity)
        return jnp.transpose(split, (0, 2, 1, 3)).reshape(devices, channels, capacity)

    def by_lanes(blocks):
        many = LANES // capacity
        split = blocks.reshape(-1, many, channels, capacity)
        return jnp.transpose(split, (0, 2, 1, 3)).reshape(-1, channels, LANES)

    if capacity != LANES:
        outgoing = by_device(outgoing)
    arrived = lax.all_to_all(outgoing, both, split_axis=0, concat_axis=0, tiled=True)
    if capacity != LANES:
        arrived = by_lanes(arrived)

    first_mix = flat_weight(marine_conv_first_weight)
    second_mix = flat_weight(marine_conv_second_weight)
    ocean_start, head, tail = add_forcing(
        arrived, marine_coupling_slot, ocean, marine_neighbour_index, air_out, first_mix, second_mix
    )
    ocean_before, ocean_after = from_neighbours(head, tail, both)
    inner, done = ocean_inner(ocean_start, marine_neighbour_index, first_mix, second_mix)
    ocean_next = ocean_outer(
        ocean_start,
        inner,
        done,
        ocean_before,
        ocean_after,
        marine_neighbour_index,
        first_mix,
        second_mix,
    )
    return (air_out, ocean_next)


def solution(mesh):
    placed = (
        P(None, "tile", "face"),
        P(None, ("face", "tile")),
        P(),
        P(),
        P(),
        P(),
        P(),
        P(("face", "tile")),
        P(("face", "tile"), None),
        P(None, ("face", "tile")),
    )
    return jax.shard_map(
        shards,
        mesh=mesh,
        in_specs=placed,
        out_specs=(P(None, "tile", "face"), P(None, ("face", "tile"))),
        check_vma=False,
    )
```
